32 devices in a mesh: dp: 16 (over z, y, x), tensor: 2 (over core).
Axes of the slice: x: 2, y: 2, z: 4, core: 2. Of those that a mesh axis runs over, the one named last changes fastest.
Arguments:
- inputs: bfloat16 [64, 1024, 512], P('dp', 'tensor'), may hold values from -6 to 6
- initial_state: float32 [64, 1024], P('dp', 'tensor'), may hold values from -6 to 6
- first_gain: float32 [512], replicated, may hold values from 0.1 to 1.9
- causal_filter: float32 [4, 512], replicated, may hold values from -3 to 3
- mixer_weight: bfloat16 [512, 2, 1024], P(None, None, 'tensor'), may hold values from -0.25 to 0.25
- gate_bias: float32 [1024], P('tensor'), may hold values from -6 to 2
- readout_weight: bfloat16 [1024, 512], P('tensor'), may hold values from -0.1875 to 0.1875
- second_gain: float32 [512], replicated, may hold values from 0.1 to 1.9
- up_weight: bfloat16 [512, 2048], P(None, 'tensor'), may hold values from -0.25 to 0.25
- up_bias: float32 [2048], P('tensor'), may hold values from -3 to 3
- down_weight: bfloat16 [2048, 512], P('tensor'), may hold values from -0.1875 to 0.1875
- cotangent: bfloat16 [64, 1024, 512], P('dp', 'tensor'), may hold values from -6 to 6
Outputs:
- block_output: bfloat16 [64, 1024, 512], P('dp', 'tensor')
- input_gradient: bfloat16 [64, 1024, 512], P('dp', 'tensor')
- state_gradient: float32 [64, 1024], P('dp', 'tensor')
- first_gain_gradient: float32 [512], replicated
- filter_gradient: float32 [4, 512], replicated
- mixer_gradient: float32 [512, 2, 1024], P(None, None, 'tensor')
- gate_bias_gradient: float32 [1024], P('tensor')
- readout_gradient: float32 [1024, 512], P('tensor')
- second_gain_gradient: float32 [512], replicated
- up_weight_gradient: float32 [512, 2048], P(None, 'tensor')
- up_bias_gradient: float32 [2048], P('tensor')
- down_weight_gradient: float32 [2048, 512], P('tensor')
The draws below stay inside these ranges and needn't reach their ends.
All inputs are finite; a program needn't handle non-finite values.
Results may differ from the reference program's by a relative error of at most 0.0075.
Values may be sent and summed in bfloat16 or wider, within the bound.
No kernel may reach another device: no remote copies, remote signals or barrier semaphores. Data moves between devices by JAX's collectives and lax.ppermute only.
A program may use at most 256 MiB of HBM per device.

```python
import math
import jax
import jax.numpy as jnp
from jax import lax

D = 512
H = 1024
F = 2048
TAPS = 4
LENGTH = 1024
WINDOWS = 64


def shard_levels(own_key, extent, split, least, top_value):
    def one(axis_at, parts):
        draws = jax.random.uniform(jax.random.fold_in(jax.random.fold_in(own_key, 6), axis_at), (parts,), jnp.float32, least / len(split), top_value / len(split))
        return jnp.repeat(jnp.exp(draws), extent[axis_at] // parts).reshape((-1,) + (1,) * (len(extent) - axis_at - 1))

    factor_of = one(*split[0])
    for cut in split[1:]:
        factor_of = factor_of * one(*cut)
    return factor_of


def noise(key, dims, scale, most, pieces=(), dtype=jnp.bfloat16):
    entries = scale * jax.random.normal(key, dims, jnp.float32)
    if pieces:
        entries = entries * shard_levels(key, dims, pieces, -0.22, 0.18)
    return jnp.clip(entries, -most, most).astype(dtype)


def setup_inputs(seed: int = 0) -> dict:
    streams_of = jax.random.split(jax.random.key(seed), 13)
    inputs = noise(streams_of[0], (WINDOWS, LENGTH, D), 1.0, 6.0, ((0, 16), (1, 2)))
    initial_state = noise(streams_of[1], (WINDOWS, H), 1.0, 6.0, ((0, 16), (1, 2)), jnp.float32)
    first_gain = jnp.clip(1.0 + 0.18 * jax.random.normal(streams_of[2], (D,), jnp.float32), 0.1, 1.9)
    causal_filter = noise(streams_of[3], (TAPS, D), 0.5, 3.0, (), jnp.float32)
    mixer_weight = noise(streams_of[4], (D, 2, H), D ** -0.5, 0.25, ((2, 2),))
    gate_bias = jnp.clip(-6.0 + 8.0 * jax.random.uniform(streams_of[5], (H,), jnp.float32) ** shard_levels(streams_of[5], (H,), ((0, 2),), -0.2, 0.2), -6.0, 2.0)
    readout_weight = noise(streams_of[6], (H, D), H ** -0.5, 0.1875, ((0, 2),))
    second_gain = jnp.clip(1.0 + 0.18 * jax.random.normal(streams_of[7], (D,), jnp.float32), 0.1, 1.9)
    up_weight = noise(streams_of[8], (D, F), D ** -0.5, 0.25, ((1, 2),))
    up_bias = noise(streams_of[9], (F,), 0.5, 3.0, ((0, 2),), jnp.float32)
    down_weight = noise(streams_of[10], (F, D), (F // 2) ** -0.5, 0.1875, ((0, 2),))
    cotangent = noise(streams_of[11], (WINDOWS, LENGTH, D), 1.0, 6.0, ((0, 16), (1, 2)))
    return dict(inputs=inputs, initial_state=initial_state, first_gain=first_gain, causal_filter=causal_filter, mixer_weight=mixer_weight, gate_bias=gate_bias, readout_weight=readout_weight, second_gain=second_gain, up_weight=up_weight, up_bias=up_bias, down_weight=down_weight, cotangent=cotangent)


@jax.custom_vjp
def low(v):
    return lax.optimization_barrier(v.astype(jnp.bfloat16)).astype(jnp.float32)

@jax.custom_vjp
def low_back(v):
    return v

def low_keep(v):
    return (low(v), None)

def low_pass(kept, grad):
    return (grad,)

def back_keep(v):
    return (v, None)

def back_low(kept, grad):
    return (low(grad),)
low.defvjp(low_keep, low_pass)
low_back.defvjp(back_keep, back_low)
epsilon = 1e-06
highest = lax.Precision.HIGHEST

def normalize(values, gain):
    return values * lax.rsqrt(lax.optimization_barrier(jnp.mean(values * values, axis=-1, keepdims=True)) + epsilon) * gain

def gating(gate_input, candidate_input):
    return (jax.nn.sigmoid(-gate_input), jax.nn.sigmoid(gate_input) * jax.nn.softplus(candidate_input))

def forward(inputs, initial_state, first_gain, causal_filter, mixer_weight, gate_bias, readout_weight, second_gain, up_weight, up_bias, down_weight):
    length = inputs.shape[1]
    normed = normalize(inputs, first_gain)
    padded = jnp.pad(normed, ((0, 0), (TAPS - 1, 0), (0, 0)))
    filtered = low(sum((causal_filter[tap_index] * padded[:, tap_index:tap_index + length, :] for tap_index in range(TAPS))))
    projected = jnp.einsum('bld,dgh->blgh', filtered, mixer_weight, precision=highest)
    gate_input = low_back(projected[:, :, 0, :] + gate_bias)
    candidate_input = low_back(projected[:, :, 1, :])
    decays, inject = gating(gate_input, candidate_input)

    def advance(state, pair):
        state = pair[0] * state + pair[1]
        return (state, state)
    _, states = lax.scan(advance, initial_state, (jnp.swapaxes(decays, 0, 1), jnp.swapaxes(inject, 0, 1)))
    states_low = low(jnp.swapaxes(states, 0, 1))
    mixed_out = low_back(jnp.einsum('blh,hd->bld', states_low, readout_weight, precision=highest))
    middle = inputs + mixed_out
    normed_two = low(normalize(middle, second_gain))
    hidden = low_back(jnp.einsum('bld,df->blf', normed_two, up_weight, precision=highest) + up_bias)
    activation = low(jax.nn.gelu(hidden))
    down_out = low_back(jnp.einsum('blf,fd->bld', activation, down_weight, precision=highest))
    return middle + down_out

def reference(inputs, initial_state, first_gain, causal_filter, mixer_weight, gate_bias, readout_weight, second_gain, up_weight, up_bias, down_weight, cotangent):
    params = tuple((param.astype(jnp.float32) for param in (first_gain, causal_filter, mixer_weight, gate_bias, readout_weight, second_gain, up_weight, up_bias, down_weight)))
    batch = math.gcd(WINDOWS, 4)
    groups = WINDOWS // batch
    windows_in = inputs.astype(jnp.float32).reshape(groups, batch, LENGTH, D)
    states_in = initial_state.astype(jnp.float32).reshape(groups, batch, H)
    tangents = cotangent.astype(jnp.float32).reshape(groups, batch, LENGTH, D)
    totals = tuple((jnp.zeros_like(param) for param in params))

    def accumulate(carry, item):
        block_out, pull = jax.vjp(forward, item[0], item[1], *params)
        pulled = pull(item[2])
        carry = tuple((left + right for left, right in zip(carry, pulled[2:])))
        return (carry, (block_out, pulled[0], pulled[1]))
    totals, (outputs, input_grads, state_grads) = lax.scan(accumulate, totals, (windows_in, states_in, tangents))
    return (outputs.reshape(WINDOWS, LENGTH, D).astype(jnp.bfloat16), input_grads.reshape(WINDOWS, LENGTH, D).astype(jnp.bfloat16), state_grads.reshape(WINDOWS, H), totals[0], totals[1], totals[2], totals[3], totals[4], totals[5], totals[6], totals[7], totals[8])
```

```python
import functools
import math

import jax
import jax.numpy as jnp
from jax import lax
from jax.experimental import pallas as pl
from jax.experimental.pallas import tpu as pltpu
from jax.sharding import PartitionSpec as P

epsilon = 1e-06
low = jnp.bfloat16
wide = jnp.float32
root = math.sqrt(2.0 / math.pi)
cubic = 0.044715
MIB = 1 << 20


def mm(left, right):
    return lax.dot_general(left, right, (((1,), (0,)), ((), ())), preferred_element_type=wide)


def mm_nt(left, right):
    return lax.dot_general(left, right, (((1,), (1,)), ((), ())), preferred_element_type=wide)


def mm_tn(left, right):
    return lax.dot_general(left, right, (((0,), (0,)), ((), ())), preferred_element_type=wide)


def params(mib, grid):
    return pltpu.CompilerParams(
        vmem_limit_bytes=mib * MIB, dimension_semantics=("arbitrary",) * grid
    )


def cost(macs, moved, curves=0):
    return pl.CostEstimate(flops=2 * macs, bytes_accessed=moved, transcendentals=curves)


def whole(array):
    rank = array.ndim
    return pl.BlockSpec(array.shape, lambda *_: (0,) * rank)


def rows_of(tile, width, lanes=8):
    return lax.broadcasted_iota(jnp.int32, (lanes, width), 0)


def forward_kernel(
    core, own, got, gain, taps, mixer_own, mixer_other, bias, start, read_own, read_other,
    gain_two, filtered_out, decay_out, gate_out, cand_out, state_out, middle_out, normed_out,
    rim, gates, cands, carry,
):
    half_chunks = pl.num_programs(1) // 2
    step = pl.program_id(1)
    rows = own.shape[1]
    width = own.shape[2]
    tap_count = taps.shape[0]
    mine = step // half_chunks == core[0]
    x = jnp.where(mine, own[0], got[0]).astype(wide)
    scale = lax.rsqrt(jnp.mean(x * x, axis=-1, keepdims=True) + epsilon)
    normed = x * scale * gain[...]

    @pl.when(step == 0)
    def _():
        rim[0:8, :] = jnp.zeros((8, width), wide)
        carry[...] = jnp.broadcast_to(start[0], carry.shape)

    rim[8 : 8 + rows, :] = normed
    total = taps[0:1, :] * rim[9 - tap_count : 9 - tap_count + rows, :]
    for tap in range(1, tap_count):
        begin = 9 - tap_count + tap
        total = total + taps[tap : tap + 1, :] * rim[begin : begin + rows, :]
    rim[0:8, :] = normed[rows - 8 :, :]
    filtered = total.astype(low)
    filtered_out[...] = filtered
    channels = read_own.shape[0]
    for at, weight in ((0, mixer_own), (1, mixer_other)):
        lanes = slice(at * channels, (at + 1) * channels)
        gates[:, lanes] = mm(filtered, weight[:, :channels]) + bias[:, lanes]
        cands[:, lanes] = mm(filtered, weight[:, channels:])

    group = min(channels, 256)
    place = rows_of(8, group)

    def sweep(index, _):
        base = pl.multiple_of(index * 16, 16)
        for lane in range(0, 2 * channels, group):
            lanes = slice(lane, lane + group)
            state = carry[:, lanes]
            kept = []
            for sub in (0, 8):
                g = gates[pl.ds(base + sub, 8), lanes]
                c = cands[pl.ds(base + sub, 8), lanes]
                t = 0.5 * jnp.tanh(0.5 * g)
                decay = 0.5 - t
                opened = 0.5 + t
                soft = jnp.maximum(c, 0.0) + jnp.log1p(jnp.exp(-jnp.abs(c)))
                a = decay
                b = opened * soft
                for hop in (1, 2, 4):
                    inside = place >= hop
                    a_back = jnp.where(inside, pltpu.roll(a, hop, 0), 1.0)
                    b_back = jnp.where(inside, pltpu.roll(b, hop, 0), 0.0)
                    b = a * b_back + b
                    a = a * a_back
                h = a * state + b
                before = jnp.where(place >= 1, pltpu.roll(h, 1, 0), state)
                state = jnp.broadcast_to(h[7:8, :], h.shape)
                decay_out[pl.ds(base + sub, 8), lanes] = decay
                kept.append(
                    (
                        decay * opened * (soft - before),
                        opened * (0.5 + 0.5 * jnp.tanh(0.5 * c)),
                        h,
                    )
                )
            carry[:, lanes] = state
            for ref, parts in zip((gate_out, cand_out, state_out), zip(*kept)):
                ref[pl.ds(base, 16), lanes] = jnp.concatenate(parts, axis=0).astype(low)
        return 0

    lax.fori_loop(0, rows // 16, sweep, 0)
    mixed = mm(state_out[:, :channels], read_own[...]) + mm(
        state_out[:, channels:], read_other[...]
    )
    middle = x + mixed
    middle_out[...] = middle
    scale_two = lax.rsqrt(jnp.mean(middle * middle, axis=-1, keepdims=True) + epsilon)
    normed_out[...] = (middle * scale_two * gain_two[...]).astype(low)


def halves_specs(chunk, width, windows, halves):
    return (
        pl.BlockSpec(
            (1, chunk, width), lambda w, t, core: (windows * core[0] + w, t % halves, 0)
        ),
        pl.BlockSpec((1, chunk, width), lambda w, t, core: (w, t % halves, 0)),
    )


def fixed(array):
    rank = array.ndim
    return pl.BlockSpec(array.shape, lambda w, t, core: (0,) * rank)


def forward(core, inputs, got, gain, taps, mixers, bias, start, reads, gain_two):
    windows, half, width = got.shape
    channels = reads[0].shape[0]
    chunk = math.gcd(half, 256)
    halves = half // chunk
    steps = 2 * halves
    rows = 2 * half * windows
    row = lambda lanes: pl.BlockSpec((chunk, lanes), lambda w, t, core: (w * steps + t, 0))
    out = lambda lanes, dtype: jax.ShapeDtypeStruct((rows, lanes), dtype)
    return pl.pallas_call(
        forward_kernel,
        grid_spec=pltpu.PrefetchScalarGridSpec(
            num_scalar_prefetch=1,
            grid=(windows, steps),
            in_specs=[
                *halves_specs(chunk, width, windows, halves),
                fixed(gain),
                fixed(taps),
                fixed(mixers[0]),
                fixed(mixers[1]),
                fixed(bias),
                pl.BlockSpec((1, 1, 2 * channels), lambda w, t, core: (w, 0, 0)),
                fixed(reads[0]),
                fixed(reads[1]),
                fixed(gain_two),
            ],
            out_specs=[
                row(width),
                row(2 * channels),
                row(2 * channels),
                row(2 * channels),
                row(2 * channels),
                row(width),
                row(width),
            ],
            scratch_shapes=[
                pltpu.VMEM((chunk + 8, width), wide),
                pltpu.VMEM((chunk, 2 * channels), wide),
                pltpu.VMEM((chunk, 2 * channels), wide),
                pltpu.VMEM((8, 2 * channels), wide),
            ],
        ),
        out_shape=[
            out(width, low),
            out(2 * channels, wide),
            out(2 * channels, low),
            out(2 * channels, low),
            out(2 * channels, low),
            out(width, wide),
            out(width, low),
        ],
        compiler_params=params(48, 2),
        cost_estimate=cost(rows * width * channels * 6, rows * channels * 24, rows * channels * 8),
        name="forward_mixer",
    )(core, inputs, got, gain, taps, *mixers, bias, start, *reads, gain_two)


def feed_kernel(
    core, own, got, normed, up_own, up_other, bias, down_own, down_other,
    tangent_out, active_out, back_out, bias_out,
):
    half_chunks = pl.num_programs(1) // 2
    step = pl.program_id(1)
    tangent = jnp.where(step // half_chunks == core[0], own[0], got[0])
    tangent_out[...] = tangent
    low_rows = normed[...]
    units = up_own.shape[1]
    block = min(units, 512)

    @pl.when((step == 0) & (pl.program_id(0) == 0))
    def _():
        bias_out[...] = jnp.zeros_like(bias_out)

    for at, (up, down) in enumerate(((up_own, down_own), (up_other, down_other))):
        for first in range(0, units, block):
            own_lanes = slice(first, first + block)
            lanes = slice(at * units + first, at * units + first + block)
            v = mm(low_rows, up[:, own_lanes]) + bias[:, lanes]
            back = mm_nt(tangent, down[own_lanes, :])
            square = v * v
            t = jnp.tanh(v * (root + (root * cubic) * square))
            half = 0.5 * v
            active_out[:, lanes] = (half + half * t).astype(low)
            slope = (0.5 + 0.5 * t) + (half * (1.0 - t * t)) * (
                root + (3.0 * root * cubic) * square
            )
            hidden_back = (back * slope).astype(low)
            back_out[:, lanes] = hidden_back
            bias_out[:, lanes] += jnp.sum(hidden_back.astype(wide), axis=0, keepdims=True)


def feed(core, cotangent, got, normed, ups, bias, downs):
    windows, half, width = got.shape
    units = ups[0].shape[1]
    chunk = math.gcd(half, 256)
    halves = half // chunk
    steps = 2 * halves
    rows = 2 * half * windows
    row = lambda lanes: pl.BlockSpec((chunk, lanes), lambda w, t, core: (w * steps + t, 0))
    out = lambda lanes: jax.ShapeDtypeStruct((rows, lanes), low)
    return pl.pallas_call(
        feed_kernel,
        grid_spec=pltpu.PrefetchScalarGridSpec(
            num_scalar_prefetch=1,
            grid=(windows, steps),
            in_specs=[
                *halves_specs(chunk, width, windows, halves),
                row(width),
                fixed(ups[0]),
                fixed(ups[1]),
                fixed(bias),
                fixed(downs[0]),
                fixed(downs[1]),
            ],
            out_specs=[
                row(width),
                row(2 * units),
                row(2 * units),
                pl.BlockSpec((1, 2 * units), lambda w, t, core: (0, 0)),
            ],
        ),
        out_shape=[
            out(width),
            out(2 * units),
            out(2 * units),
            jax.ShapeDtypeStruct((1, 2 * units), wide),
        ],
        compiler_params=params(48, 2),
        cost_estimate=cost(rows * width * units * 4, rows * units * 8, rows * units * 2),
        name="feed_forward",
    )(core, cotangent, got, normed, *ups, bias, *downs)


def outer_kernel(left, right, own_out, other_out):
    step = pl.program_id(0)
    count = pl.num_programs(0) // 2
    product = mm_tn(left[...], right[...])

    @pl.when(step < count)
    def _():
        other_out[...] = product.astype(low)

    @pl.when(step >= count)
    def _():
        own_out[...] = product


def outer(left, right, name):
    rows, width = left.shape
    lanes = right.shape[1] // 2
    block = min(lanes, 512)
    count = lanes // block
    return pl.pallas_call(
        outer_kernel,
        grid=(2 * count,),
        in_specs=[
            whole(left),
            pl.BlockSpec((rows, block), lambda j: (0, (j + count) % (2 * count))),
        ],
        out_specs=[
            pl.BlockSpec((width, block), lambda j: (0, jnp.maximum(j - count, 0))),
            pl.BlockSpec((width, block), lambda j: (0, jnp.minimum(j, count - 1))),
        ],
        out_shape=[
            jax.ShapeDtypeStruct((width, lanes), wide),
            jax.ShapeDtypeStruct((width, lanes), low),
        ],
        compiler_params=params(40, 1),
        cost_estimate=cost(rows * width * lanes * 2, rows * (lanes * 4 + width * 2)),
        name=name,
    )(left, right)


def backward_kernel(
    tangent, back_hidden, middle_in, decay_in, gate_in, cand_in, up_own, up_other, read_own,
    read_other, gain_two, middle_out, mixed_out, project_out, state_out, gain_out, bias_out,
    states, carry,
):
    step = pl.program_id(1)
    rows, width = tangent.shape
    units = up_own.shape[1]
    channels = read_own.shape[0]

    @pl.when((step == 0) & (pl.program_id(0) == 0))
    def _():
        gain_out[...] = jnp.zeros_like(gain_out)
        bias_out[...] = jnp.zeros_like(bias_out)

    @pl.when(step == 0)
    def _():
        carry[...] = jnp.zeros_like(carry)

    back = mm_nt(back_hidden[:, :units], up_own[...]) + mm_nt(
        back_hidden[:, units:], up_other[...]
    )
    middle = middle_in[...]
    scale = lax.rsqrt(jnp.mean(middle * middle, axis=-1, keepdims=True) + epsilon)
    gain_out[...] += jnp.sum(back * (middle * scale), axis=0, keepdims=True)
    weighted = gain_two[...] * back
    inner = jnp.mean(weighted * middle, axis=-1, keepdims=True)
    back_middle = (
        tangent[...].astype(wide) + scale * weighted - middle * (scale * scale * scale * inner)
    )
    middle_out[...] = back_middle
    mixed = back_middle.astype(low)
    mixed_out[...] = mixed
    states[:, :channels] = mm_nt(mixed, read_own[...])
    states[:, channels:] = mm_nt(mixed, read_other[...])

    group = min(channels, 256)
    place = rows_of(8, group)
    count = rows // 16

    def sweep(index, _):
        base = pl.multiple_of((count - 1 - index) * 16, 16)
        for at in (0, 1):
            for lane in range(0, channels, group):
                lanes = slice(at * channels + lane, at * channels + lane + group)
                later = carry[:, lanes]
                kept = []
                for sub in (8, 0):
                    d = decay_in[pl.ds(base + sub, 8), lanes]
                    s = states[pl.ds(base + sub, 8), lanes]
                    a = d
                    b = d * s
                    for hop in (1, 2, 4):
                        inside = place < 8 - hop
                        a_next = jnp.where(inside, pltpu.roll(a, 8 - hop, 0), 1.0)
                        b_next = jnp.where(inside, pltpu.roll(b, 8 - hop, 0), 0.0)
                        b = a * b_next + b
                        a = a * a_next
                    u = a * later + b
                    carried = s + jnp.where(place < 7, pltpu.roll(u, 7, 0), later)
                    later = jnp.broadcast_to(u[0:1, :], u.shape)
                    kept.insert(0, carried)
                carry[:, lanes] = later
                both = jnp.concatenate(kept, axis=0)
                gate = (both * gate_in[pl.ds(base, 16), lanes].astype(wide)).astype(low)
                cand = (both * cand_in[pl.ds(base, 16), lanes].astype(wide)).astype(low)
                first = 2 * at * channels + lane
                project_out[pl.ds(base, 16), first : first + group] = gate
                project_out[pl.ds(base, 16), first + channels : first + channels + group] = cand
                rounded = gate.astype(wide)
                bias_out[:, lanes] += rounded[:8] + rounded[8:]
        return 0

    lax.fori_loop(0, count, sweep, 0)

    @pl.when(step == pl.num_programs(1) - 1)
    def _():
        state_out[0] = carry[0:1, :]


def backward(windows, tangent, back_hidden, middle, decay, gate, cand, ups, reads, gain_two):
    rows, width = tangent.shape
    units = ups[0].shape[1]
    channels = reads[0].shape[0]
    length = rows // windows
    chunk = math.gcd(length, 256)
    steps = length // chunk
    row = lambda lanes: pl.BlockSpec((chunk, lanes), lambda w, t: (w * steps + steps - 1 - t, 0))
    out = lambda lanes, dtype: jax.ShapeDtypeStruct((rows, lanes), dtype)
    return pl.pallas_call(
        backward_kernel,
        grid=(windows, steps),
        in_specs=[
            row(width),
            row(2 * units),
            row(width),
            row(2 * channels),
            row(2 * channels),
            row(2 * channels),
            whole(ups[0]),
            whole(ups[1]),
            whole(reads[0]),
            whole(reads[1]),
            whole(gain_two),
        ],
        out_specs=[
            row(width),
            row(width),
            row(4 * channels),
            pl.BlockSpec((1, 1, 2 * channels), lambda w, t: (w, 0, 0)),
            pl.BlockSpec((1, width), lambda w, t: (0, 0)),
            pl.BlockSpec((8, 2 * channels), lambda w, t: (0, 0)),
        ],
        out_shape=[
            out(width, wide),
            out(width, low),
            out(4 * channels, low),
            jax.ShapeDtypeStruct((windows, 1, 2 * channels), wide),
            jax.ShapeDtypeStruct((1, width), wide),
            jax.ShapeDtypeStruct((8, 2 * channels), wide),
        ],
        scratch_shapes=[
            pltpu.VMEM((chunk, 2 * channels), wide),
            pltpu.VMEM((8, 2 * channels), wide),
        ],
        compiler_params=params(48, 2),
        cost_estimate=cost(
            rows * width * (2 * units + 2 * channels), rows * (units * 4 + channels * 24)
        ),
        name="backward_mixer",
    )(tangent, back_hidden, middle, decay, gate, cand, *ups, *reads, gain_two)


def entry_kernel(
    core, own, got, project, middle_in, mixer_own, mixer_other, gain, taps,
    grad_out, gain_out, taps_out, rim,
):
    step = pl.program_id(1)
    steps = pl.num_programs(1)
    half_chunks = steps // 2
    position = steps - 1 - step
    rows, width = own.shape[1:]
    tap_count = taps.shape[0]
    lanes = mixer_own.shape[1]

    @pl.when((step == 0) & (pl.program_id(0) == 0))
    def _():
        gain_out[...] = jnp.zeros_like(gain_out)
        taps_out[...] = jnp.zeros_like(taps_out)

    @pl.when(step == 0)
    def _():
        rim[rows : rows + 8, :] = jnp.zeros((8, width), wide)

    rim[0:rows, :] = mm_nt(project[:, :lanes], mixer_own[...]) + mm_nt(
        project[:, lanes:], mixer_other[...]
    )
    x = jnp.where(position // half_chunks == core[0], own[0], got[0]).astype(wide)
    scale = lax.rsqrt(jnp.mean(x * x, axis=-1, keepdims=True) + epsilon)
    unit = x * scale
    normed = unit * gain[...]
    back = jnp.zeros((rows, width), wide)
    for tap in range(tap_count):
        ahead = rim[tap_count - 1 - tap : tap_count - 1 - tap + rows, :]
        back = back + taps[tap : tap + 1, :] * ahead
        taps_out[tap : tap + 1, :] += jnp.sum(ahead * normed, axis=0, keepdims=True)
    rim[rows : rows + 8, :] = rim[0:8, :]
    gain_out[...] += jnp.sum(back * unit, axis=0, keepdims=True)
    weighted = gain[...] * back
    inner = jnp.mean(weighted * x, axis=-1, keepdims=True)
    grad_out[...] = (
        middle_in[...] + scale * weighted - x * (scale * scale * scale * inner)
    ).astype(low)


def entry(core, inputs, got, project, back_middle, mixers, gain, taps):
    windows, half, width = got.shape
    chunk = math.gcd(half, 256)
    halves = half // chunk
    steps = 2 * halves
    rows = 2 * half * windows
    row = lambda lanes: pl.BlockSpec(
        (chunk, lanes), lambda w, t, core: (w * steps + steps - 1 - t, 0)
    )
    return pl.pallas_call(
        entry_kernel,
        grid_spec=pltpu.PrefetchScalarGridSpec(
            num_scalar_prefetch=1,
            grid=(windows, steps),
            in_specs=[
                pl.BlockSpec(
                    (1, chunk, width),
                    lambda w, t, core: (windows * core[0] + w, (steps - 1 - t) % halves, 0),
                ),
                pl.BlockSpec((1, chunk, width), lambda w, t, core: (w, (steps - 1 - t) % halves, 0)),
                row(project.shape[1]),
                row(width),
                fixed(mixers[0]),
                fixed(mixers[1]),
                fixed(gain),
                fixed(taps),
            ],
            out_specs=[
                row(width),
                pl.BlockSpec((1, width), lambda w, t, core: (0, 0)),
                pl.BlockSpec(taps.shape, lambda w, t, core: (0, 0)),
            ],
            scratch_shapes=[pltpu.VMEM((chunk + 8, width), wide)],
        ),
        out_shape=[
            jax.ShapeDtypeStruct((rows, width), low),
            jax.ShapeDtypeStruct((1, width), wide),
            jax.ShapeDtypeStruct(taps.shape, wide),
        ],
        compiler_params=params(48, 2),
        cost_estimate=cost(rows * width * project.shape[1], rows * project.shape[1] * 4),
        name="input_gradient",
    )(core, inputs, got, project, back_middle, *mixers, gain, taps)


def exit_kernel(active, middle, down_own, down_other, out):
    units = down_own.shape[0]
    out[...] = (
        middle[...] + mm(active[:, :units], down_own[...]) + mm(active[:, units:], down_other[...])
    ).astype(low)


def leave(active, middle, downs):
    rows, width = middle.shape
    chunk = math.gcd(rows, 512)
    row = lambda lanes: pl.BlockSpec((chunk, lanes), lambda t: (t, 0))
    return pl.pallas_call(
        exit_kernel,
        grid=(rows // chunk,),
        in_specs=[row(active.shape[1]), row(width), whole(downs[0]), whole(downs[1])],
        out_specs=row(width),
        out_shape=jax.ShapeDtypeStruct((rows, width), low),
        compiler_params=params(48, 1),
        cost_estimate=cost(rows * width * active.shape[1], rows * active.shape[1] * 3),
        name="block_output",
    )(active, middle, *downs)


def partner(array):
    return lax.ppermute(array, "tensor", [(0, 1), (1, 0)])


def across(array, bits):
    sizes = (lax.axis_size("dp"), lax.axis_size("tensor"))
    route = [
        (d * sizes[1] + c, (d ^ (1 << bits[c])) * sizes[1] + c)
        for d in range(sizes[0])
        for c in range(sizes[1])
    ]
    return lax.ppermute(array, ("dp", "tensor"), route)


def bit_orders():
    count = lax.axis_size("dp").bit_length() - 1
    first = list(range(count))
    second = first[:]
    if count >= 3:
        second[:3] = [2, 0, 1]
    return list(zip(first, second))


def sum_over_dp(total):
    index, core = lax.axis_index("dp"), lax.axis_index("tensor")
    stages = []
    for bits in bit_orders():
        bit = jnp.where(core == 0, (index >> bits[0]) & 1, (index >> bits[1]) & 1)
        half = total.shape[0] // 2
        keep = lax.dynamic_slice_in_dim(total, bit * half, half)
        send = lax.dynamic_slice_in_dim(total, (1 - bit) * half, half).astype(low)
        total = keep + across(send, bits).astype(wide)
        stages.append((bits, bit))
    piece = total.astype(low)
    for bits, bit in reversed(stages):
        other = across(piece, bits)
        piece = jnp.where(
            bit == 0, jnp.concatenate([piece, other]), jnp.concatenate([other, piece])
        )
    return piece


def sum_small(values):
    for bit in range(lax.axis_size("dp").bit_length() - 1):
        values = values + across(values, (bit, bit))
    return values


def local(
    inputs,
    initial_state,
    first_gain,
    causal_filter,
    mixer_weight,
    gate_bias,
    readout_weight,
    second_gain,
    up_weight,
    up_bias,
    down_weight,
    cotangent,
):
    sides = lax.axis_size("tensor")
    windows = inputs.shape[0] // sides
    half, width = inputs.shape[1:]
    channels = gate_bias.shape[0]
    units = up_bias.shape[0]
    core = lax.axis_index("tensor")
    core_at = core.reshape(1).astype(jnp.int32)

    def own_windows(array):
        return lax.dynamic_slice_in_dim(array, core * windows, windows)

    def other_windows(array):
        return lax.dynamic_slice_in_dim(array, (1 - core) * windows, windows)

    mixer = mixer_weight.reshape(width, 2 * channels)
    got_inputs = partner(other_windows(inputs))
    short = jnp.concatenate([gate_bias[None], up_bias.reshape(-1, channels), other_windows(initial_state)])
    got_short = partner(short)
    bias_rows = 1 + units // channels
    mixers = (mixer, partner(mixer))
    reads = (readout_weight, partner(readout_weight))
    got_cotangent = partner(other_windows(cotangent))
    ups = (up_weight, partner(up_weight))
    downs = (down_weight, partner(down_weight))
    gate_bias_all = jnp.concatenate([gate_bias, got_short[0]])[None]
    up_bias_all = jnp.concatenate([up_bias, got_short[1:bias_rows].reshape(-1)])[None]
    start = jnp.concatenate([own_windows(initial_state), got_short[bias_rows:]], axis=1)[:, None]
    gain, gain_two = first_gain[None], second_gain[None]

    filtered, decay, gate, cand, states, middle, normed = forward(
        core_at, inputs, got_inputs, gain, causal_filter, mixers, gate_bias_all, start, reads, gain_two
    )
    tangent, active, back_hidden, up_bias_grad = feed(
        core_at, cotangent, got_cotangent, normed, ups, up_bias_all, downs
    )
    down_own, down_other = outer(tangent, active, "down_gradient")
    up_own, up_other = outer(normed, back_hidden, "up_gradient")
    feed_total = jnp.concatenate([down_own, up_own]) + partner(
        jnp.concatenate([down_other, up_other])
    ).astype(wide)
    feed_sum = sum_over_dp(feed_total)
    back_middle, back_mixed, project, state_grad, gain_two_grad, gate_bias_grad = backward(
        windows, tangent, back_hidden, middle, decay, gate, cand, ups, reads, gain_two
    )
    read_own, read_other = outer(back_mixed, states, "readout_gradient")
    mixer_own, mixer_other = outer(filtered, project, "mixer_gradient")
    mixer_total = jnp.concatenate([mixer_own, read_own], axis=1) + partner(
        jnp.concatenate([mixer_other, read_other], axis=1)
    ).astype(wide)
    mixer_sum = sum_over_dp(mixer_total)
    input_grad, gain_grad, taps_grad = entry(
        core_at, inputs, got_inputs, project, back_middle, mixers, gain, causal_filter
    )
    output = leave(active, middle, downs)

    gate_bias_grad = jnp.sum(gate_bias_grad, axis=0)
    up_bias_grad = up_bias_grad[0]
    common = jnp.concatenate([gain_grad[0], taps_grad.reshape(-1), gain_two_grad[0]])
    sent = partner(jnp.concatenate([common, gate_bias_grad[channels:], up_bias_grad[units:]]))
    short_sum = sum_small(
        jnp.concatenate([common, gate_bias_grad[:channels], up_bias_grad[:units]]) + sent
    )
    cuts = [width, width + causal_filter.size, 2 * width + causal_filter.size]
    cuts += [cuts[-1] + channels]
    gain_sum, taps_sum, gain_two_sum, gate_bias_sum, up_bias_sum = jnp.split(short_sum, cuts)

    def place(mine, got):
        return jnp.where(core == 0, jnp.concatenate([mine, got]), jnp.concatenate([got, mine]))

    def give_back(rows):
        parts = rows.reshape(windows, sides, half, width)
        mine = lax.dynamic_index_in_dim(parts, core, 1, keepdims=False)
        other = lax.dynamic_index_in_dim(parts, 1 - core, 1, keepdims=False)
        return place(mine, partner(other))

    state_rows = state_grad[:, 0]
    state_gradient = place(state_rows[:, :channels], partner(state_rows[:, channels:]))
    return (
        give_back(output),
        give_back(input_grad),
        state_gradient,
        gain_sum,
        taps_sum.reshape(causal_filter.shape),
        mixer_sum[:, : 2 * channels].astype(wide).reshape(width, 2, channels),
        gate_bias_sum,
        mixer_sum[:, 2 * channels :].astype(wide).T,
        gain_two_sum,
        feed_sum[width:].astype(wide),
        up_bias_sum,
        feed_sum[:width].astype(wide).T,
    )


def solution(mesh):
    return jax.shard_map(
        local,
        mesh=mesh,
        in_specs=(
            P("dp", "tensor", None),
            P("dp", "tensor"),
            P(),
            P(),
            P(None, None, "tensor"),
            P("tensor"),
            P("tensor", None),
            P(),
            P(None, "tensor"),
            P("tensor"),
            P("tensor", None),
            P("dp", "tensor", None),
        ),
        out_specs=(
            P("dp", "tensor", None),
            P("dp", "tensor", None),
            P("dp", "tensor"),
            P(),
            P(),
            P(None, None, "tensor"),
            P("tensor"),
            P("tensor", None),
            P(),
            P(None, "tensor"),
            P("tensor"),
            P("tensor", None),
        ),
        check_vma=False,
    )
```

```python
import functools
import math

import jax
import jax.numpy as jnp
from jax import lax
from jax.experimental import pallas as pl
from jax.experimental.pallas import tpu as pltpu
from jax.sharding import PartitionSpec as P

epsilon = 1e-06
low = jnp.bfloat16
wide = jnp.float32
root = math.sqrt(2.0 / math.pi)
cubic = 0.044715
MIB = 1 << 20


def mm(left, right):
    return lax.dot_general(left, right, (((1,), (0,)), ((), ())), preferred_element_type=wide)


def mm_nt(left, right):
    return lax.dot_general(left, right, (((1,), (1,)), ((), ())), preferred_element_type=wide)


def mm_tn(left, right):
    return lax.dot_general(left, right, (((0,), (0,)), ((), ())), preferred_element_type=wide)


def params(mib, grid):
    return pltpu.CompilerParams(
        vmem_limit_bytes=mib * MIB, dimension_semantics=("arbitrary",) * grid
    )


def cost(macs, moved, curves=0):
    return pl.CostEstimate(flops=2 * macs, bytes_accessed=moved, transcendentals=curves)


def whole(array):
    rank = array.ndim
    return pl.BlockSpec(array.shape, lambda *_: (0,) * rank, pipeline_mode=pl.Buffered(1))


def stream_order(rows, inverse):
    at = lax.broadcasted_iota(jnp.int32, (rows, rows), 1 if inverse else 0)
    source = lax.broadcasted_iota(jnp.int32, (rows, rows), 0 if inverse else 1)
    return (source == at % 8 * (rows // 8) + at // 8).astype(low)


def forward_kernel(
    core, own, got, order, gain, taps, mixer_own, mixer_other, bias_own, bias_other, start_own, start_other,
    read_own, read_other,
    gain_two, filtered_out, decay_out, differ_out, cand_out, state_out, middle_out, normed_out,
    streams, rim, tail, gates, cands, carry,
):
    half_chunks = pl.num_programs(1) // 2
    step = pl.program_id(1)
    rows = own.shape[1]
    width = own.shape[2]
    count = rows // 8
    tap_count = taps.shape[0]
    edge = 8 * (tap_count - 1)
    channels = read_own.shape[0]
    mine = step // half_chunks == core[0]
    x = mm(order[...], jnp.where(mine, own[0], got[0]))
    streams[...] = x
    scale = lax.rsqrt(jnp.mean(x * x, axis=-1, keepdims=True) + epsilon)
    normed = x * scale * gain[...]

    @pl.when(step == 0)
    def _():
        tail[...] = jnp.zeros_like(tail)
        for at, start in enumerate((start_own, start_other)):
            carry[:, at * channels : (at + 1) * channels] = jnp.broadcast_to(start[0], (8, channels))

    rim[edge:, :] = normed
    first = lax.broadcasted_iota(jnp.int32, (8, width), 0) == 0
    for at in range(0, edge, 8):
        ends = normed[rows - edge + at : rows - edge + at + 8, :]
        rim[at : at + 8, :] = jnp.where(
            first, pltpu.roll(tail[at : at + 8, :], 1, 0), pltpu.roll(ends, 1, 0)
        )
        tail[at : at + 8, :] = ends
    total = taps[0:1, :] * rim[0:rows, :]
    for tap in range(1, tap_count):
        total = total + taps[tap : tap + 1, :] * rim[8 * tap : 8 * tap + rows, :]
    filtered = total.astype(low)
    filtered_out[...] = filtered
    for at, (weight, bias) in enumerate(((mixer_own, bias_own), (mixer_other, bias_other))):
        lanes = slice(at * channels, (at + 1) * channels)
        gates[:, lanes] = mm(filtered, weight[:, :channels]) + bias[...]
        cands[:, lanes] = mm(filtered, weight[:, channels:])

    group = min(2 * channels, 1024)
    place = lax.broadcasted_iota(jnp.int32, (8, group), 0)
    for lane in range(0, 2 * channels, group):
        lanes = slice(lane, lane + group)

        def open_gates(index, state):
            factor, offset = state
            base = pl.multiple_of(index * 16, 16)
            kept = []
            for sub in (0, 8):
                c = cands[pl.ds(base + sub, 8), lanes]
                decay = jax.nn.sigmoid(-gates[pl.ds(base + sub, 8), lanes])
                soft = jnp.maximum(c, jnp.log(1.0 + jnp.exp(jnp.minimum(c, 60.0))))
                decay_out[pl.ds(base + sub, 8), lanes] = decay
                gates[pl.ds(base + sub, 8), lanes] = soft
                factor = factor * decay
                offset = soft + decay * (offset - soft)
                kept.append(c)
            cand_out[pl.ds(base, 16), lanes] = jnp.concatenate(kept, axis=0).astype(low)
            return factor, offset

        factor, offset = lax.fori_loop(
            0,
            count // 2,
            open_gates,
            (jnp.ones((8, group), wide), jnp.zeros((8, group), wide)),
            unroll=True,
        )
        for hop in (1, 2, 4):
            inside = place >= hop
            offset = factor * jnp.where(inside, pltpu.roll(offset, hop, 0), 0.0) + offset
            factor = factor * jnp.where(inside, pltpu.roll(factor, hop, 0), 1.0)
        entered = carry[:, lanes]
        leaving = factor * entered + offset
        carry[:, lanes] = jnp.broadcast_to(leaving[7:8, :], leaving.shape)
        entered = jnp.where(place >= 1, pltpu.roll(leaving, 1, 0), entered)

        def run_states(index, state):
            base = pl.multiple_of(index * 16, 16)
            held, differ = [], []
            for sub in (0, 8):
                soft = gates[pl.ds(base + sub, 8), lanes]
                differ.append(soft - state)
                state = soft - decay_out[pl.ds(base + sub, 8), lanes] * differ[-1]
                held.append(state)
            differ_out[pl.ds(base, 16), lanes] = jnp.concatenate(differ, axis=0).astype(low)
            state_out[pl.ds(base, 16), lanes] = jnp.concatenate(held, axis=0).astype(low)
            return state

        lax.fori_loop(0, count // 2, run_states, entered, unroll=True)

    mixed = mm(state_out[:, :channels], read_own[...]) + mm(
        state_out[:, channels:], read_other[...]
    )
    middle = streams[...] + mixed
    middle_out[...] = middle
    scale_two = lax.rsqrt(jnp.mean(middle * middle, axis=-1, keepdims=True) + epsilon)
    normed_out[...] = (middle * scale_two * gain_two[...]).astype(low)


def halves_specs(chunk, width, windows, halves):
    return (
        pl.BlockSpec(
            (1, chunk, width), lambda w, t, core: (windows * core[0] + w, t % halves, 0)
        ),
        pl.BlockSpec((1, chunk, width), lambda w, t, core: (w, t % halves, 0)),
    )


def forward(core, inputs, got, order, gain, taps, mixers, biases, starts, reads, gain_two):
    windows, half, width = got.shape
    channels = reads[0].shape[0]
    chunk = math.gcd(half, 512)
    halves = half // chunk
    steps = 2 * halves
    rows = 2 * half * windows
    row = lambda lanes: pl.BlockSpec((chunk, lanes), lambda w, t, core: (w * steps + t, 0))
    out = lambda lanes, dtype: jax.ShapeDtypeStruct((rows, lanes), dtype)
    return pl.pallas_call(
        forward_kernel,
        grid_spec=pltpu.PrefetchScalarGridSpec(
            num_scalar_prefetch=1,
            grid=(windows, steps),
            in_specs=[
                *halves_specs(chunk, width, windows, halves),
                whole(order),
                whole(gain),
                whole(taps),
                whole(mixers[0]),
                whole(mixers[1]),
                whole(biases[0]),
                whole(biases[1]),
                *[
                    pl.BlockSpec((1, 1, channels), lambda w, t, core: (windows * core[0] + w, 0, 0))
                    for _ in starts
                ],
                whole(reads[0]),
                whole(reads[1]),
                whole(gain_two),
            ],
            out_specs=[
                row(width),
                row(2 * channels),
                row(2 * channels),
                row(2 * channels),
                row(2 * channels),
                row(width),
                row(width),
            ],
            scratch_shapes=[
                pltpu.VMEM((chunk, width), wide),
                pltpu.VMEM((chunk + 8 * (taps.shape[0] - 1), width), wide),
                pltpu.VMEM((8 * (taps.shape[0] - 1), width), wide),
                pltpu.VMEM((chunk, 2 * channels), wide),
                pltpu.VMEM((chunk, 2 * channels), wide),
                pltpu.VMEM((8, 2 * channels), wide),
            ],
        ),
        out_shape=[
            out(width, low),
            out(2 * channels, wide),
            out(2 * channels, low),
            out(2 * channels, low),
            out(2 * channels, low),
            out(width, wide),
            out(width, low),
        ],
        compiler_params=params(60, 2),
        cost_estimate=cost(rows * width * channels * 6, rows * channels * 24, rows * channels * 8),
        name="forward_mixer",
    )(core, inputs, got, order, gain, taps, *mixers, *biases, *starts, *reads, gain_two)


def feed(core, cotangent, got, order, tangent, normed, up, bias, down, dtype):
    windows, half, width = got.shape
    units = up.shape[1]
    rows = normed.shape[0]
    chunk = order.shape[0]
    block = min(units, 512)
    fresh = tangent is None

    def kernel(core, *refs):
        if fresh:
            own, came, order_in, *refs, tangent_in = refs
        else:
            tangent_in, *refs = refs
        normed_in, up_in, bias_in, down_in, active_out, back_out, bias_out, grad_out = refs

        if fresh:

            @pl.when(pl.program_id(0) == 0)
            def _():
                for window in range(windows):
                    for side in range(2):
                        mine = core[0] == side
                        for at in range(0, half, chunk):
                            rows_at = slice(at, at + chunk)
                            to = (2 * window + side) * half + at
                            tangent_in[to : to + chunk, :] = mm(
                                order_in[...],
                                jnp.where(mine, own[window, rows_at, :], came[window, rows_at, :]),
                            ).astype(low)

        sums = [jnp.zeros((8, block), wide), 0.0, 0.0]
        for at in range(0, rows, chunk):
            rows_at = slice(at, at + chunk)
            v = mm(normed_in[rows_at, :], up_in[...]) + bias_in[...]
            back = mm_nt(tangent_in[rows_at, :], down_in[...])
            square = v * v
            s = jax.nn.sigmoid(v * (2.0 * root + (2.0 * root * cubic) * square))
            active = v * s
            slope = s + (active * (1.0 - s)) * (2.0 * root + (6.0 * root * cubic) * square)
            back = back * slope
            for row in range(0, chunk, 8):
                sums[0] = sums[0] + back[row : row + 8, :]
            active_low, back_low = active.astype(low), back.astype(low)
            active_out[rows_at, :] = active_low
            back_out[rows_at, :] = back_low
            sums[1] = sums[1] + mm_tn(tangent_in[rows_at, :], active_low)
            sums[2] = sums[2] + mm_tn(normed_in[rows_at, :], back_low)
        bias_out[...] = sums[0]
        grad_out[0:width, :] = sums[1].astype(dtype)
        grad_out[width:, :] = sums[2].astype(dtype)

    lanes = lambda count: pl.BlockSpec((count, block), lambda j, core: (0, j))
    in_specs = [whole(normed), lanes(width), lanes(1), pl.BlockSpec((block, width), lambda j, core: (j, 0))]
    arrays = [normed, up, bias, down]
    out_specs = [lanes(rows), lanes(rows), lanes(8), lanes(2 * width)]
    out_shape = [
        jax.ShapeDtypeStruct((rows, units), low),
        jax.ShapeDtypeStruct((rows, units), low),
        jax.ShapeDtypeStruct((8, units), wide),
        jax.ShapeDtypeStruct((2 * width, units), dtype),
    ]
    if fresh:
        in_specs = [
            pl.BlockSpec((windows, half, width), lambda j, core: (core[0], 0, 0)),
            whole(got),
            whole(order),
        ] + in_specs
        arrays = [cotangent, got, order] + arrays
        out_specs.append(pl.BlockSpec((rows, width), lambda j, core: (0, 0)))
        out_shape.append(jax.ShapeDtypeStruct((rows, width), low))
    else:
        in_specs.insert(0, whole(tangent))
        arrays.insert(0, tangent)
    return pl.pallas_call(
        kernel,
        grid_spec=pltpu.PrefetchScalarGridSpec(
            num_scalar_prefetch=1, grid=(units // block,), in_specs=in_specs, out_specs=out_specs
        ),
        out_shape=out_shape,
        compiler_params=params(60, 1),
        cost_estimate=cost(rows * width * units * 4, rows * units * 4, rows * units),
        name="feed_forward",
    )(core, *arrays)


def norm_kernel(
    tangent, back_own, back_other, middle_in, up_own, up_other, gain_two, middle_out, mixed_out, gain_out
):
    @pl.when(pl.program_id(0) == 0)
    def _():
        gain_out[...] = jnp.zeros_like(gain_out)

    rows = tangent.shape[0]
    part = math.gcd(rows, 256)
    for begin in range(0, rows, part):
        at = slice(begin, begin + part)
        back = mm_nt(back_own[at, :], up_own[...]) + mm_nt(back_other[at, :], up_other[...])
        middle = middle_in[at, :]
        scale = lax.rsqrt(jnp.mean(middle * middle, axis=-1, keepdims=True) + epsilon)
        gain_out[...] += jnp.sum(back * (middle * scale), axis=0, keepdims=True)
        weighted = gain_two[...] * back
        inner = jnp.mean(weighted * middle, axis=-1, keepdims=True)
        back_middle = (
            tangent[at, :].astype(wide) + scale * weighted - middle * (scale * scale * scale * inner)
        )
        middle_out[at, :] = back_middle
        mixed_out[at, :] = back_middle.astype(low)


def norm_back(tangent, backs, middle, ups, gain_two):
    rows, width = tangent.shape
    units = ups[0].shape[1]
    chunk = math.gcd(rows, 512)
    row = lambda lanes: pl.BlockSpec((chunk, lanes), lambda t: (t, 0))
    return pl.pallas_call(
        norm_kernel,
        grid=(rows // chunk,),
        in_specs=[
            row(width),
            row(units),
            row(units),
            row(width),
            whole(ups[0]),
            whole(ups[1]),
            whole(gain_two),
        ],
        out_specs=[row(width), row(width), pl.BlockSpec((1, width), lambda t: (0, 0))],
        out_shape=[
            jax.ShapeDtypeStruct((rows, width), wide),
            jax.ShapeDtypeStruct((rows, width), low),
            jax.ShapeDtypeStruct((1, width), wide),
        ],
        compiler_params=params(60, 1),
        cost_estimate=cost(rows * width * 2 * units, rows * (units * 4 + width * 16)),
        name="norm_back",
    )(tangent, *backs, middle, *ups, gain_two)


def scan_kernel(
    windows, chunk, mixed, filtered, read, decay_in, differ_in, cand_in, state_in,
    gate_out, cand_out, state_out, bias_out, grad_out, states,
):
    rows, width = mixed.shape
    group = read.shape[0]
    count = chunk // 16
    chunks = rows // chunk
    each = chunks // windows
    place = lax.broadcasted_iota(jnp.int32, (8, group), 0)
    states[...] = mm_nt(mixed[...], read[...])
    factors = [jnp.ones((8, group), wide)] * chunks
    offsets = [jnp.zeros((8, group), wide)] * chunks
    for index in range(2 * count - 1, -1, -1):
        for at in range(chunks):
            here = slice(at * chunk + 8 * index, at * chunk + 8 * index + 8)
            decay = decay_in[here, :]
            factors[at] = factors[at] * decay
            offsets[at] = decay * (offsets[at] + states[here, :])
    later = [None] * chunks
    for window in range(windows):
        entered = jnp.zeros((8, group), wide)
        for at in range(window * each + each - 1, window * each - 1, -1):
            factor, offset = factors[at], offsets[at]
            for hop in (1, 2, 4):
                inside = place < 8 - hop
                offset = factor * jnp.where(inside, pltpu.roll(offset, 8 - hop, 0), 0.0) + offset
                factor = factor * jnp.where(inside, pltpu.roll(factor, 8 - hop, 0), 1.0)
            leaving = factor * entered + offset
            later[at] = jnp.where(place < 7, pltpu.roll(leaving, 7, 0), entered)
            entered = jnp.broadcast_to(leaving[0:1, :], leaving.shape)
        state_out[window] = entered[0:1, :]
    bias = [jnp.zeros((8, group), wide)] * chunks
    for index in range(count - 1, -1, -1):
        for at in range(chunks):
            base = at * chunk + 16 * index
            both = slice(base, base + 16)
            differ = differ_in[both, :].astype(wide)
            chosen = jax.nn.sigmoid(cand_in[both, :].astype(wide))
            gate, cand = [None] * 2, [None] * 2
            for half in (1, 0):
                near = slice(8 * half, 8 * half + 8)
                here = slice(base + 8 * half, base + 8 * half + 8)
                decay = decay_in[here, :]
                carried = states[here, :] + later[at]
                later[at] = decay * carried
                opened = carried - later[at]
                gate[half] = decay * opened * differ[near]
                cand[half] = opened * chosen[near]
                bias[at] = bias[at] + gate[half]
            gate_out[both, :] = jnp.concatenate(gate, axis=0).astype(low)
            cand_out[both, :] = jnp.concatenate(cand, axis=0).astype(low)
    bias_out[...] = sum(bias[1:], bias[0])
    grad_out[2 * width :, :] = mm_tn(mixed[...], state_in[...]).astype(grad_out.dtype)
    grad_out[0:width, :] = mm_tn(filtered[...], gate_out[...]).astype(grad_out.dtype)
    grad_out[width : 2 * width, :] = mm_tn(filtered[...], cand_out[...]).astype(grad_out.dtype)


def scan_back(windows, chunk, side, mixed, filtered, read, decay, differ, cand, states, dtype):
    rows, width = mixed.shape
    channels = read.shape[0]
    block = min(channels, 256)
    count = channels // block
    lanes = lambda size: pl.BlockSpec((size, block), lambda j: (0, j))
    half = pl.BlockSpec((rows, block), lambda j: (0, side * count + j))
    out = jax.ShapeDtypeStruct((rows, channels), low)
    return pl.pallas_call(
        functools.partial(scan_kernel, windows, chunk),
        grid=(count,),
        in_specs=[
            whole(mixed),
            whole(filtered),
            pl.BlockSpec((block, width), lambda j: (j, 0)),
            half,
            half,
            half,
            half,
        ],
        out_specs=[
            lanes(rows),
            lanes(rows),
            pl.BlockSpec((windows, 1, block), lambda j: (0, 0, j)),
            lanes(8),
            lanes(3 * width),
        ],
        out_shape=[
            out,
            out,
            jax.ShapeDtypeStruct((windows, 1, channels), wide),
            jax.ShapeDtypeStruct((8, channels), wide),
            jax.ShapeDtypeStruct((3 * width, channels), dtype),
        ],
        scratch_shapes=[pltpu.VMEM((rows, block), wide)],
        compiler_params=params(60, 1),
        cost_estimate=cost(rows * width * 4 * channels, rows * channels * 14, rows * channels),
        name="scan_back",
    )(mixed, filtered, read, decay, differ, cand, states)


def entry_kernel(
    core, own, got, order, back_order, gate_own, cand_own, gate_other, cand_other, middle_in, mixer_own,
    mixer_other, gain, taps, mine_out, sent_out, gain_out, taps_out, rim, head,
):
    step = pl.program_id(0)
    steps = pl.num_programs(0)
    half_chunks = steps // 2
    position = steps - 1 - step
    rows, width = own.shape[1:]
    tap_count = taps.shape[0]
    edge = 8 * (tap_count - 1)
    channels = gate_own.shape[1]

    @pl.when(step == 0)
    def _():
        gain_out[...] = jnp.zeros_like(gain_out)
        taps_out[...] = jnp.zeros_like(taps_out)
        head[...] = jnp.zeros_like(head)

    rim[0:rows, :] = (
        mm_nt(gate_own[...], mixer_own[:, :channels])
        + mm_nt(cand_own[...], mixer_own[:, channels:])
        + mm_nt(gate_other[...], mixer_other[:, :channels])
        + mm_nt(cand_other[...], mixer_other[:, channels:])
    )
    last = lax.broadcasted_iota(jnp.int32, (8, width), 0) == 7
    for at in range(0, edge, 8):
        begins = rim[at : at + 8, :]
        rim[rows + at : rows + at + 8, :] = jnp.where(
            last, pltpu.roll(head[at : at + 8, :], 7, 0), pltpu.roll(begins, 7, 0)
        )
        head[at : at + 8, :] = begins
    x = mm(order[...], jnp.where(position // half_chunks == core[0], own[0], got[0]))
    scale = lax.rsqrt(jnp.mean(x * x, axis=-1, keepdims=True) + epsilon)
    unit = x * scale
    normed = unit * gain[...]
    back = jnp.zeros((rows, width), wide)
    for tap in range(tap_count):
        begin = 8 * (tap_count - 1 - tap)
        ahead = rim[begin : begin + rows, :]
        back = back + taps[tap : tap + 1, :] * ahead
        taps_out[tap : tap + 1, :] += jnp.sum(ahead * normed, axis=0, keepdims=True)
    gain_out[...] += jnp.sum(back * unit, axis=0, keepdims=True)
    weighted = gain[...] * back
    inner = jnp.mean(weighted * x, axis=-1, keepdims=True)
    gradient = middle_in[...] + scale * weighted - x * (scale * scale * scale * inner)
    gradient = mm(back_order[...], gradient.astype(low)).astype(low)
    give(gradient, position, half_chunks, core, mine_out, sent_out)


def give(values, position, half_chunks, core, mine_out, sent_out):
    rows = values.shape[0]
    at = pl.ds(pl.multiple_of(position % half_chunks * rows, rows), rows)
    mine = position // half_chunks == core[0]

    @pl.when(mine)
    def _():
        mine_out[at, :] = values

    @pl.when(jnp.logical_not(mine))
    def _():
        sent_out[at, :] = values


def entry(window, core, inputs, got, orders, projects, back_middle, mixers, gain, taps):
    windows, half, width = got.shape
    chunk = math.gcd(half, 512)
    halves = half // chunk
    steps = 2 * halves
    rows = 2 * half
    row_in = lambda lanes: pl.BlockSpec(
        (chunk, lanes), lambda t, core: (window * steps + steps - 1 - t, 0)
    )
    side = pl.BlockSpec((half, width), lambda t, core: (0, 0))
    return pl.pallas_call(
        entry_kernel,
        grid_spec=pltpu.PrefetchScalarGridSpec(
            num_scalar_prefetch=1,
            grid=(steps,),
            in_specs=[
                pl.BlockSpec(
                    (1, chunk, width),
                    lambda t, core: (windows * core[0] + window, (steps - 1 - t) % halves, 0),
                ),
                pl.BlockSpec(
                    (1, chunk, width), lambda t, core: (window, (steps - 1 - t) % halves, 0)
                ),
                whole(orders[0]),
                whole(orders[1]),
                *[row_in(array.shape[1]) for array in projects],
                row_in(width),
                whole(mixers[0]),
                whole(mixers[1]),
                whole(gain),
                whole(taps),
            ],
            out_specs=[
                side,
                side,
                pl.BlockSpec((1, width), lambda t, core: (0, 0)),
                pl.BlockSpec(taps.shape, lambda t, core: (0, 0)),
            ],
            scratch_shapes=[
                pltpu.VMEM((chunk + 8 * (taps.shape[0] - 1), width), wide),
                pltpu.VMEM((8 * (taps.shape[0] - 1), width), wide),
            ],
        ),
        out_shape=[
            jax.ShapeDtypeStruct((half, width), low),
            jax.ShapeDtypeStruct((half, width), low),
            jax.ShapeDtypeStruct((1, width), wide),
            jax.ShapeDtypeStruct(taps.shape, wide),
        ],
        compiler_params=params(60, 1),
        cost_estimate=cost(
            rows * width * 2 * mixers[0].shape[1], rows * mixers[0].shape[1] * 6
        ),
        name="input_gradient",
    )(core, inputs, got, *orders, *projects, back_middle, *mixers, gain, taps)


def leave_kernel(
    core, back_order, active_own, active_other, middle, down_own, down_other, mine_out, sent_out
):
    total = middle[...] + mm(active_own[...], down_own[...]) + mm(active_other[...], down_other[...])
    total = mm(back_order[...], total.astype(low)).astype(low)
    give(total, pl.program_id(0), pl.num_programs(0) // 2, core, mine_out, sent_out)


def leave(window, windows, core, back_order, actives, middle, downs):
    width = middle.shape[1]
    rows = middle.shape[0] // windows
    chunk = back_order.shape[0]
    steps = rows // chunk
    row = lambda lanes: pl.BlockSpec((chunk, lanes), lambda t, core: (window * steps + t, 0))
    side = pl.BlockSpec((rows // 2, width), lambda t, core: (0, 0))
    out = jax.ShapeDtypeStruct((rows // 2, width), low)
    return pl.pallas_call(
        leave_kernel,
        grid_spec=pltpu.PrefetchScalarGridSpec(
            num_scalar_prefetch=1,
            grid=(steps,),
            in_specs=[
                whole(back_order),
                row(actives[0].shape[1]),
                row(actives[1].shape[1]),
                row(width),
                whole(downs[0]),
                whole(downs[1]),
            ],
            out_specs=[side, side],
        ),
        out_shape=[out, out],
        compiler_params=params(60, 1),
        cost_estimate=cost(rows * width * 2 * downs[0].shape[0], rows * downs[0].shape[0] * 6),
        name="block_output",
    )(core, back_order, *actives, middle, *downs)


def pack_kernel(width, windows, *refs):
    *entries, gain_two, gate_own, gate_other, up_own, up_other, mine_out, sent_out = refs
    gains, taps = entries[0][...], entries[windows][...]
    for window in range(1, windows):
        gains = gains + entries[window][...]
        taps = taps + entries[windows + window][...]
    for out, gate, up in ((mine_out, gate_own, up_own), (sent_out, gate_other, up_other)):
        out[...] = jnp.zeros_like(out)
        row = 0
        for part in (
            gains,
            taps,
            gain_two[...],
            jnp.sum(gate[...], axis=0, keepdims=True),
            jnp.sum(up[...], axis=0, keepdims=True),
        ):
            for lane in range(0, part.shape[1], width):
                out[row : row + part.shape[0], 0 : min(width, part.shape[1])] = part[:, lane : lane + width]
                row += part.shape[0]


def pack(width, gains, taps, *rest):
    arrays = [*gains, *taps, *rest]
    count = taps[0].shape[0] + 3 + -(-rest[-1].shape[1] // width)
    out = jax.ShapeDtypeStruct((-(-count // 8) * 8, width), wide)
    return pl.pallas_call(
        functools.partial(pack_kernel, width, len(gains)),
        out_shape=[out, out],
        compiler_params=params(60, 0),
        name="pack_short",
    )(*arrays)


def partner(array):
    return lax.ppermute(array, "tensor", [(0, 1), (1, 0)])


def hold(*values):
    return lax.optimization_barrier(values)


class DpSum:
    def __init__(self, *terms):
        self.terms = terms
        self.piece = None
        count = lax.axis_size("dp").bit_length() - 1
        first = list(range(count))
        if count >= 2:
            groups = [((0,), (1,)), ((1,), (0,))] + [
                (tuple(first[at : at + 2]),) * 2 for at in range(2, count, 2)
            ]
        else:
            groups = [((bit,), (bit,)) for bit in first]
        self.todo = [(False, group) for group in groups] + [(True, group) for group in groups[::-1]]

    def place(self, group):
        index, core = lax.axis_index("dp"), lax.axis_index("tensor")
        return [
            jnp.where(core == 0, (index >> low_bit) & 1, (index >> high_bit) & 1)
            for low_bit, high_bit in zip(*group)
        ]

    def exchange(self, array, group, mask):
        sizes = (lax.axis_size("dp"), lax.axis_size("tensor"))
        flips = [
            sum(1 << bit for at, bit in enumerate(bits) if mask >> at & 1) for bits in group
        ]
        route = [
            (d * sizes[1] + c, (d ^ flips[c]) * sizes[1] + c)
            for d in range(sizes[0])
            for c in range(sizes[1])
        ]
        return lax.ppermute(array, ("dp", "tensor"), route)

    def prepare(self):
        join, group = self.todo[0]
        if join:
            if self.piece is None:
                self.piece = sum(term.astype(wide) for term in self.terms).astype(low)
            self.sends = [self.piece]
            return
        bits = self.place(group)
        self.spot = sum(bit << at for at, bit in enumerate(bits))
        count = 1 << len(bits)
        self.sends = [self.share(self.spot ^ mask, count).astype(low) for mask in range(1, count)]

    def share(self, spot, count):
        size = self.terms[0].shape[0] // count
        cuts = [lax.dynamic_slice_in_dim(term, spot * size, size) for term in self.terms]
        return sum(cut.astype(wide) for cut in cuts)

    def start(self):
        join, group = self.todo[0]
        count = 1 << len(group[0])
        sends = self.sends * (count - 1) if join else self.sends
        self.got = [
            self.exchange(array, group, mask) for array, mask in zip(sends, range(1, count))
        ]

    def finish(self):
        join, group = self.todo.pop(0)
        if not join:
            self.terms = [self.share(self.spot, 1 << len(group[0])), *self.got]
            return
        parts = [self.piece] + self.got
        for bit in self.place(group):
            parts = [
                jnp.where(
                    bit == 0,
                    jnp.concatenate([parts[at], parts[at + 1]]),
                    jnp.concatenate([parts[at + 1], parts[at]]),
                )
                for at in range(0, len(parts), 2)
            ]
        self.piece = parts[0]


class DpSmall(DpSum):
    def __init__(self, total):
        super().__init__(total)
        self.todo = [(join, (group[0], group[0])) for join, group in self.todo if not join]

    def prepare(self):
        self.sends = [self.terms[0]] * ((1 << len(self.todo[0][1][0])) - 1)

    def finish(self):
        _, group = self.todo.pop(0)
        parts = [self.terms[0], *self.got]
        while len(parts) > 1:
            parts = [parts[at] + parts[at + 1] for at in range(0, len(parts), 2)]
        self.terms = parts


def beside(chains, work, *leads):
    chains = [chain for chain in chains if chain.todo]
    for chain in chains:
        chain.prepare()
    held = hold(*leads, *(send for chain in chains for send in chain.sends))
    leads, sends = held[: len(leads)], list(held[len(leads) :])
    for chain in chains:
        chain.sends, sends = sends[: len(chain.sends)], sends[len(chain.sends) :]
        chain.start()
    results = work(*leads)
    held = hold(*results, *(got for chain in chains for got in chain.got))
    results, gots = held[: len(results)], list(held[len(results) :])
    for chain in chains:
        chain.got, gots = gots[: len(chain.got)], gots[len(chain.got) :]
        chain.finish()
    return results


def local(
    inputs,
    initial_state,
    first_gain,
    causal_filter,
    mixer_weight,
    gate_bias,
    readout_weight,
    second_gain,
    up_weight,
    up_bias,
    down_weight,
    cotangent,
):
    sides = lax.axis_size("tensor")
    windows = inputs.shape[0] // sides
    half, width = inputs.shape[1:]
    channels = gate_bias.shape[0]
    units = up_bias.shape[0]
    core = lax.axis_index("tensor")
    core_at = core.reshape(1).astype(jnp.int32)

    def other_windows(array):
        return lax.dynamic_slice_in_dim(array, (1 - core) * windows, windows)

    mixer = mixer_weight.reshape(width, 2 * channels)
    mixers = (mixer, partner(mixer))
    got_inputs = partner(other_windows(inputs))
    reads = (readout_weight, partner(readout_weight))
    biases = (gate_bias[None], partner(gate_bias)[None])
    starts = (initial_state[:, None], partner(initial_state)[:, None])
    got_cotangent = partner(other_windows(cotangent))
    ups = (up_weight, partner(up_weight))
    up_biases = (up_bias[None], partner(up_bias)[None])
    downs = (down_weight, partner(down_weight))
    gain, gain_two = first_gain[None], second_gain[None]
    orders = [stream_order(math.gcd(half, 512), inverse) for inverse in (False, True)]

    filtered, decay, differ, cand, states, middle, normed = forward(
        core_at, inputs, got_inputs, orders[0], gain, causal_filter, mixers, biases, starts, reads, gain_two
    )
    chunk = orders[0].shape[0]
    active_other, back_other, bias_other, feed_other, tangent = feed(
        core_at, cotangent, got_cotangent, orders[0], None, normed, ups[1], up_biases[1], downs[1], low
    )
    tangent, feed_other = hold(tangent, feed_other)
    feed_got = partner(feed_other)
    active_own, back_own, bias_own, feed_own = feed(
        core_at, cotangent, got_cotangent, orders[0], tangent, normed, ups[0], up_biases[0], downs[0], wide
    )
    actives = [active_own, active_other]
    feed_own, feed_got = hold(feed_own, feed_got)
    feed_sum = DpSum(feed_own, feed_got)
    up_bias_own, up_bias_other = bias_own, bias_other

    def scan(side, lead, dtype):
        return scan_back(
            windows, chunk, side, lead, filtered, reads[side], decay, differ, cand, states, dtype
        )

    back_middle, mixed, gain_two_grad = beside(
        [feed_sum],
        lambda lead: norm_back(tangent, [lead, back_other], middle, ups, gain_two),
        back_own,
    )
    gate_other, cand_other, state_other, bias_other, mixer_other = beside(
        [feed_sum], lambda lead: scan(1, lead, low), mixed
    )
    mixed, mixer_other = hold(mixed, mixer_other)
    mixer_got = partner(mixer_other)
    gate_own, cand_own, state_own, bias_own, mixer_own = beside(
        [feed_sum], lambda lead: scan(0, lead, wide), mixed
    )
    mixer_own, mixer_got = hold(mixer_own, mixer_got)
    mixer_sum = DpSum(mixer_own, mixer_got)
    gate_bias_own, gate_bias_other = bias_own, bias_other
    entries, outputs = [], []
    for window in range(windows):
        entries.append(
            beside(
                [feed_sum, mixer_sum],
                lambda lead, window=window: entry(
                    window, core_at, inputs, got_inputs, orders, [lead, cand_own, gate_other, cand_other],
                    back_middle, mixers, gain, causal_filter,
                ),
                gate_own,
            )
        )
    short, sent = pack(
        width,
        [item[2] for item in entries],
        [item[3] for item in entries],
        gain_two_grad,
        gate_bias_own,
        gate_bias_other,
        up_bias_own,
        up_bias_other,
    )

    def place(mine, got):
        return jnp.where(core == 0, jnp.concatenate([mine, got]), jnp.concatenate([got, mine]))

    grad_mine = jnp.stack([item[0] for item in entries])
    grad_sent = jnp.stack([item[1] for item in entries])
    for window in range(windows):

        def work(*leads, window=window):
            output = leave(window, windows, core_at, orders[1], [leads[0], active_other], middle, downs)
            return *output, *(partner(array) for array in leads[1:])

        if window == 0:
            *output, short_got, state_got, grad_got = beside(
                [feed_sum, mixer_sum], work, active_own, sent, state_other[:, 0], grad_sent
            )
            short_sum = DpSmall(short + short_got)
        else:
            output = beside([feed_sum, mixer_sum, short_sum], work, active_own)
        outputs.append(output)
    state_gradient = place(state_own[:, 0], state_got)
    output_mine = jnp.stack([item[0] for item in outputs])
    output_sent = jnp.stack([item[1] for item in outputs])
    (input_gradient, output_got) = beside(
        [mixer_sum, short_sum, feed_sum],
        lambda mine, got, sent: (place(mine, got), partner(sent)),
        grad_mine, grad_got, output_sent,
    )
    output_mine, output_got = hold(output_mine, output_got)

    def feed_results(mine, got, total):
        return place(mine, got), total[width:].astype(wide), total[:width].astype(wide).T

    if feed_sum.todo:
        while feed_sum.todo:
            beside([mixer_sum, short_sum, feed_sum], lambda: ())
    block_output, up_sum, down_sum = beside(
        [mixer_sum, short_sum], feed_results, output_mine, output_got, feed_sum.piece
    )
    while mixer_sum.todo or short_sum.todo:
        beside([mixer_sum, short_sum], lambda: ())
    mixer_sum = mixer_sum.piece
    short_sum = short_sum.terms[0]
    taps = causal_filter.shape[0]
    end = taps + 3 + units // width
    return (
        block_output,
        input_gradient,
        state_gradient,
        short_sum[0],
        short_sum[1 : 1 + taps],
        jnp.stack([mixer_sum[:width], mixer_sum[width : 2 * width]], axis=1).astype(wide),
        short_sum[taps + 2, :channels],
        mixer_sum[2 * width :].astype(wide).T,
        short_sum[taps + 1],
        up_sum,
        short_sum[taps + 3 : end].reshape(units),
        down_sum,
    )


def solution(mesh):
    return jax.shard_map(
        local,
        mesh=mesh,
        in_specs=(
            P("dp", "tensor", None),
            P("dp", "tensor"),
            P(),
            P(),
            P(None, None, "tensor"),
            P("tensor"),
            P("tensor", None),
            P(),
            P(None, "tensor"),
            P("tensor"),
            P("tensor", None),
            P("dp", "tensor", None),
        ),
        out_specs=(
            P("dp", "tensor", None),
            P("dp", "tensor", None),
            P("dp", "tensor"),
            P(),
            P(),
            P(None, None, "tensor"),
            P("tensor"),
            P("tensor", None),
            P(),
            P(None, "tensor"),
            P("tensor"),
            P("tensor", None),
        ),
        check_vma=False,
    )
```

```python
import functools
import math

import jax
import jax.numpy as jnp
from jax import lax
from jax.experimental import pallas as pl
from jax.experimental.pallas import tpu as pltpu
from jax.sharding import PartitionSpec as P

epsilon = 1e-06
low = jnp.bfloat16
wide = jnp.float32
root = math.sqrt(2.0 / math.pi)
cubic = 0.044715
MIB = 1 << 20


def mm(left, right):
    return lax.dot_general(left, right, (((1,), (0,)), ((), ())), preferred_element_type=wide)


def mm_nt(left, right):
    return lax.dot_general(left, right, (((1,), (1,)), ((), ())), preferred_element_type=wide)


def mm_tn(left, right):
    return lax.dot_general(left, right, (((0,), (0,)), ((), ())), preferred_element_type=wide)


def params(mib, grid):
    return pltpu.CompilerParams(
        vmem_limit_bytes=mib * MIB, dimension_semantics=("arbitrary",) * grid
    )


def cost(macs, moved, curves=0):
    return pl.CostEstimate(flops=2 * macs, bytes_accessed=moved, transcendentals=curves)


def whole(array):
    rank = array.ndim
    return pl.BlockSpec(array.shape, lambda *_: (0,) * rank, pipeline_mode=pl.Buffered(1))


def stream_order(rows, inverse):
    at = lax.broadcasted_iota(jnp.int32, (rows, rows), 1 if inverse else 0)
    source = lax.broadcasted_iota(jnp.int32, (rows, rows), 0 if inverse else 1)
    moved = jnp.bitwise_and(at, 7) * (rows // 8) + lax.shift_right_logical(at, 3)
    return jnp.where(source == moved, 1.0, 0.0).astype(low)


def forward_kernel(
    core, own, got, gain, taps, mixer_own, mixer_other, bias_own, bias_other, start_own, start_other,
    read_own, read_other,
    gain_two, filtered_out, decay_out, differ_out, cand_out, state_out, middle_out, normed_out,
    order, back_order, streams, rim, tail, gates, cands, carry,
):
    half_chunks = pl.num_programs(1) // 2
    step = pl.program_id(1)
    rows = own.shape[1]
    width = own.shape[2]
    count = rows // 8
    tap_count = taps.shape[0]
    edge = 8 * (tap_count - 1)
    channels = read_own.shape[0]
    mine = step // half_chunks == core[0]

    @pl.when((step == 0) & (pl.program_id(0) == 0))
    def _():
        order[...] = stream_order(rows, False)
        back_order[...] = stream_order(rows, True)

    x = mm(order[...], jnp.where(mine, own[0], got[0]))
    streams[...] = x
    scale = lax.rsqrt(jnp.mean(x * x, axis=-1, keepdims=True) + epsilon)
    normed = x * scale * gain[...]

    @pl.when(step == 0)
    def _():
        tail[...] = jnp.zeros_like(tail)
        for at, start in enumerate((start_own, start_other)):
            carry[:, at * channels : (at + 1) * channels] = jnp.broadcast_to(start[0], (8, channels))

    rim[edge:, :] = normed
    first = lax.broadcasted_iota(jnp.int32, (8, width), 0) == 0
    for at in range(0, edge, 8):
        ends = normed[rows - edge + at : rows - edge + at + 8, :]
        rim[at : at + 8, :] = jnp.where(
            first, pltpu.roll(tail[at : at + 8, :], 1, 0), pltpu.roll(ends, 1, 0)
        )
        tail[at : at + 8, :] = ends
    total = taps[0:1, :] * rim[0:rows, :]
    for tap in range(1, tap_count):
        total = total + taps[tap : tap + 1, :] * rim[8 * tap : 8 * tap + rows, :]
    filtered = total.astype(low)
    filtered_out[...] = filtered
    for at, (weight, bias) in enumerate(((mixer_own, bias_own), (mixer_other, bias_other))):
        lanes = slice(at * channels, (at + 1) * channels)
        gates[:, lanes] = mm(filtered, weight[:, :channels]) + bias[...]
        cands[:, lanes] = mm(filtered, weight[:, channels:])

    group = min(2 * channels, 1024)
    place = lax.broadcasted_iota(jnp.int32, (8, group), 0)
    for lane in range(0, 2 * channels, group):
        lanes = slice(lane, lane + group)

        def open_gates(index, state):
            factor, offset = state
            base = pl.multiple_of(index * 16, 16)
            kept = []
            for sub in (0, 8):
                c = cands[pl.ds(base + sub, 8), lanes]
                decay = jax.nn.sigmoid(-gates[pl.ds(base + sub, 8), lanes])
                soft = jnp.maximum(c, jnp.log(1.0 + jnp.exp(jnp.minimum(c, 60.0))))
                decay_out[pl.ds(base + sub, 8), lanes] = decay
                gates[pl.ds(base + sub, 8), lanes] = soft
                factor = factor * decay
                offset = soft + decay * (offset - soft)
                kept.append(c)
            cand_out[pl.ds(base, 16), lanes] = jnp.concatenate(kept, axis=0).astype(low)
            return factor, offset

        factor, offset = lax.fori_loop(
            0,
            count // 2,
            open_gates,
            (jnp.ones((8, group), wide), jnp.zeros((8, group), wide)),
            unroll=True,
        )
        for hop in (1, 2, 4):
            inside = place >= hop
            offset = factor * jnp.where(inside, pltpu.roll(offset, hop, 0), 0.0) + offset
            factor = factor * jnp.where(inside, pltpu.roll(factor, hop, 0), 1.0)
        entered = carry[:, lanes]
        leaving = factor * entered + offset
        carry[:, lanes] = jnp.broadcast_to(leaving[7:8, :], leaving.shape)
        entered = jnp.where(place >= 1, pltpu.roll(leaving, 1, 0), entered)

        def run_states(index, state):
            base = pl.multiple_of(index * 16, 16)
            held, differ = [], []
            for sub in (0, 8):
                soft = gates[pl.ds(base + sub, 8), lanes]
                differ.append(soft - state)
                state = soft - decay_out[pl.ds(base + sub, 8), lanes] * differ[-1]
                held.append(state)
            differ_out[pl.ds(base, 16), lanes] = jnp.concatenate(differ, axis=0).astype(low)
            state_out[pl.ds(base, 16), lanes] = jnp.concatenate(held, axis=0).astype(low)
            return state

        lax.fori_loop(0, count // 2, run_states, entered, unroll=True)

    mixed = mm(state_out[:, :channels], read_own[...]) + mm(
        state_out[:, channels:], read_other[...]
    )
    middle = streams[...] + mixed
    middle_out[...] = middle
    scale_two = lax.rsqrt(jnp.mean(middle * middle, axis=-1, keepdims=True) + epsilon)
    normed_out[...] = (middle * scale_two * gain_two[...]).astype(low)


def halves_specs(chunk, width, windows, halves):
    return (
        pl.BlockSpec(
            (1, chunk, width), lambda w, t, core: (windows * core[0] + w, t % halves, 0)
        ),
        pl.BlockSpec((1, chunk, width), lambda w, t, core: (w, t % halves, 0)),
    )


def forward(core, inputs, got, gain, taps, mixers, biases, starts, reads, gain_two):
    windows, half, width = got.shape
    channels = reads[0].shape[0]
    chunk = math.gcd(half, 512)
    halves = half // chunk
    steps = 2 * halves
    rows = 2 * half * windows
    row = lambda lanes: pl.BlockSpec((chunk, lanes), lambda w, t, core: (w * steps + t, 0))
    out = lambda lanes, dtype: jax.ShapeDtypeStruct((rows, lanes), dtype)
    return pl.pallas_call(
        forward_kernel,
        grid_spec=pltpu.PrefetchScalarGridSpec(
            num_scalar_prefetch=1,
            grid=(windows, steps),
            in_specs=[
                *halves_specs(chunk, width, windows, halves),
                whole(gain),
                whole(taps),
                whole(mixers[0]),
                whole(mixers[1]),
                whole(biases[0]),
                whole(biases[1]),
                *[
                    pl.BlockSpec((1, 1, channels), lambda w, t, core: (windows * core[0] + w, 0, 0))
                    for _ in starts
                ],
                whole(reads[0]),
                whole(reads[1]),
                whole(gain_two),
            ],
            out_specs=[
                row(width),
                row(2 * channels),
                row(2 * channels),
                row(2 * channels),
                row(2 * channels),
                row(width),
                row(width),
                pl.BlockSpec((chunk, chunk), lambda w, t, core: (0, 0)),
                pl.BlockSpec((chunk, chunk), lambda w, t, core: (0, 0)),
            ],
            scratch_shapes=[
                pltpu.VMEM((chunk, width), wide),
                pltpu.VMEM((chunk + 8 * (taps.shape[0] - 1), width), wide),
                pltpu.VMEM((8 * (taps.shape[0] - 1), width), wide),
                pltpu.VMEM((chunk, 2 * channels), wide),
                pltpu.VMEM((chunk, 2 * channels), wide),
                pltpu.VMEM((8, 2 * channels), wide),
            ],
        ),
        out_shape=[
            out(width, low),
            out(2 * channels, wide),
            out(2 * channels, low),
            out(2 * channels, low),
            out(2 * channels, low),
            out(width, wide),
            out(width, low),
            jax.ShapeDtypeStruct((chunk, chunk), low),
            jax.ShapeDtypeStruct((chunk, chunk), low),
        ],
        compiler_params=params(60, 2),
        cost_estimate=cost(rows * width * channels * 6, rows * channels * 24, rows * channels * 8),
        name="forward_mixer",
    )(core, inputs, got, gain, taps, *mixers, *biases, *starts, *reads, gain_two)


def feed(core, cotangent, got, order, tangent, normed, up, bias, down, dtype):
    windows, half, width = got.shape
    units = up.shape[1]
    rows = normed.shape[0]
    chunk = order.shape[0]
    block = min(units, 512)
    fresh = tangent is None

    def kernel(core, *refs):
        if fresh:
            own, came, order_in, *refs, tangent_in = refs
        else:
            tangent_in, *refs = refs
        normed_in, up_in, bias_in, down_in, active_out, back_out, bias_out, grad_out = refs

        if fresh:

            @pl.when(pl.program_id(0) == 0)
            def _():
                for window in range(windows):
                    for side in range(2):
                        mine = core[0] == side
                        for at in range(0, half, chunk):
                            rows_at = slice(at, at + chunk)
                            to = (2 * window + side) * half + at
                            tangent_in[to : to + chunk, :] = mm(
                                order_in[...],
                                jnp.where(mine, own[window, rows_at, :], came[window, rows_at, :]),
                            ).astype(low)

        sums = [jnp.zeros((8, block), wide), 0.0, 0.0]
        for at in range(0, rows, chunk):
            rows_at = slice(at, at + chunk)
            v = mm(normed_in[rows_at, :], up_in[...]) + bias_in[...]
            back = mm_nt(tangent_in[rows_at, :], down_in[...])
            square = v * v
            s = jax.nn.sigmoid(v * (2.0 * root + (2.0 * root * cubic) * square))
            active = v * s
            slope = s + (active * (1.0 - s)) * (2.0 * root + (6.0 * root * cubic) * square)
            back = back * slope
            for row in range(0, chunk, 8):
                sums[0] = sums[0] + back[row : row + 8, :]
            active_low, back_low = active.astype(low), back.astype(low)
            active_out[rows_at, :] = active_low
            back_out[rows_at, :] = back_low
            sums[1] = sums[1] + mm_tn(tangent_in[rows_at, :], active_low)
            sums[2] = sums[2] + mm_tn(normed_in[rows_at, :], back_low)
        bias_out[...] = sums[0]
        grad_out[0:width, :] = sums[1].astype(dtype)
        grad_out[width:, :] = sums[2].astype(dtype)

    lanes = lambda count: pl.BlockSpec((count, block), lambda j, core: (0, j))
    in_specs = [whole(normed), lanes(width), lanes(1), pl.BlockSpec((block, width), lambda j, core: (j, 0))]
    arrays = [normed, up, bias, down]
    out_specs = [lanes(rows), lanes(rows), lanes(8), lanes(2 * width)]
    out_shape = [
        jax.ShapeDtypeStruct((rows, units), low),
        jax.ShapeDtypeStruct((rows, units), low),
        jax.ShapeDtypeStruct((8, units), wide),
        jax.ShapeDtypeStruct((2 * width, units), dtype),
    ]
    if fresh:
        in_specs = [
            pl.BlockSpec((windows, half, width), lambda j, core: (core[0], 0, 0)),
            whole(got),
            whole(order),
        ] + in_specs
        arrays = [cotangent, got, order] + arrays
        out_specs.append(pl.BlockSpec((rows, width), lambda j, core: (0, 0)))
        out_shape.append(jax.ShapeDtypeStruct((rows, width), low))
    else:
        in_specs.insert(0, whole(tangent))
        arrays.insert(0, tangent)
    return pl.pallas_call(
        kernel,
        grid_spec=pltpu.PrefetchScalarGridSpec(
            num_scalar_prefetch=1, grid=(units // block,), in_specs=in_specs, out_specs=out_specs
        ),
        out_shape=out_shape,
        compiler_params=params(60, 1),
        cost_estimate=cost(rows * width * units * 4, rows * units * 4, rows * units),
        name="feed_forward",
    )(core, *arrays)


def norm_kernel(
    tangent, back_own, back_other, middle_in, up_own, up_other, gain_two, middle_out, mixed_out, gain_out
):
    @pl.when(pl.program_id(0) == 0)
    def _():
        gain_out[...] = jnp.zeros_like(gain_out)

    rows = tangent.shape[0]
    part = math.gcd(rows, 256)
    for begin in range(0, rows, part):
        at = slice(begin, begin + part)
        back = mm_nt(back_own[at, :], up_own[...]) + mm_nt(back_other[at, :], up_other[...])
        middle = middle_in[at, :]
        scale = lax.rsqrt(jnp.mean(middle * middle, axis=-1, keepdims=True) + epsilon)
        gain_out[...] += jnp.sum(back * (middle * scale), axis=0, keepdims=True)
        weighted = gain_two[...] * back
        inner = jnp.mean(weighted * middle, axis=-1, keepdims=True)
        back_middle = (
            tangent[at, :].astype(wide) + scale * weighted - middle * (scale * scale * scale * inner)
        )
        middle_out[at, :] = back_middle
        mixed_out[at, :] = back_middle.astype(low)


def norm_back(tangent, backs, middle, ups, gain_two):
    rows, width = tangent.shape
    units = ups[0].shape[1]
    chunk = math.gcd(rows, 512)
    row = lambda lanes: pl.BlockSpec((chunk, lanes), lambda t: (t, 0))
    return pl.pallas_call(
        norm_kernel,
        grid=(rows // chunk,),
        in_specs=[
            row(width),
            row(units),
            row(units),
            row(width),
            whole(ups[0]),
            whole(ups[1]),
            whole(gain_two),
        ],
        out_specs=[row(width), row(width), pl.BlockSpec((1, width), lambda t: (0, 0))],
        out_shape=[
            jax.ShapeDtypeStruct((rows, width), wide),
            jax.ShapeDtypeStruct((rows, width), low),
            jax.ShapeDtypeStruct((1, width), wide),
        ],
        compiler_params=params(60, 1),
        cost_estimate=cost(rows * width * 2 * units, rows * (units * 4 + width * 16)),
        name="norm_back",
    )(tangent, *backs, middle, *ups, gain_two)


def scan_kernel(
    windows, chunk, mixed, filtered, read, decay_in, differ_in, cand_in, state_in,
    gate_out, cand_out, state_out, bias_out, grad_out, states,
):
    rows, width = mixed.shape
    group = read.shape[0]
    count = chunk // 16
    chunks = rows // chunk
    each = chunks // windows
    place = lax.broadcasted_iota(jnp.int32, (8, group), 0)
    states[...] = mm_nt(mixed[...], read[...])
    factors = [jnp.ones((8, group), wide)] * chunks
    offsets = [jnp.zeros((8, group), wide)] * chunks
    for index in range(2 * count - 1, -1, -1):
        for at in range(chunks):
            here = slice(at * chunk + 8 * index, at * chunk + 8 * index + 8)
            decay = decay_in[here, :]
            factors[at] = factors[at] * decay
            offsets[at] = decay * (offsets[at] + states[here, :])
    later = [None] * chunks
    for window in range(windows):
        entered = jnp.zeros((8, group), wide)
        for at in range(window * each + each - 1, window * each - 1, -1):
            factor, offset = factors[at], offsets[at]
            for hop in (1, 2, 4):
                inside = place < 8 - hop
                offset = factor * jnp.where(inside, pltpu.roll(offset, 8 - hop, 0), 0.0) + offset
                factor = factor * jnp.where(inside, pltpu.roll(factor, 8 - hop, 0), 1.0)
            leaving = factor * entered + offset
            later[at] = jnp.where(place < 7, pltpu.roll(leaving, 7, 0), entered)
            entered = jnp.broadcast_to(leaving[0:1, :], leaving.shape)
        state_out[window] = entered[0:1, :]
    bias = [jnp.zeros((8, group), wide)] * chunks
    for index in range(count - 1, -1, -1):
        for at in range(chunks):
            base = at * chunk + 16 * index
            both = slice(base, base + 16)
            differ = differ_in[both, :].astype(wide)
            chosen = jax.nn.sigmoid(cand_in[both, :].astype(wide))
            gate, cand = [None] * 2, [None] * 2
            for half in (1, 0):
                near = slice(8 * half, 8 * half + 8)
                here = slice(base + 8 * half, base + 8 * half + 8)
                decay = decay_in[here, :]
                carried = states[here, :] + later[at]
                later[at] = decay * carried
                opened = carried - later[at]
                gate[half] = decay * opened * differ[near]
                cand[half] = opened * chosen[near]
                bias[at] = bias[at] + gate[half]
            gate_out[both, :] = jnp.concatenate(gate, axis=0).astype(low)
            cand_out[both, :] = jnp.concatenate(cand, axis=0).astype(low)
    bias_out[...] = sum(bias[1:], bias[0])
    grad_out[2 * width :, :] = mm_tn(mixed[...], state_in[...]).astype(grad_out.dtype)
    grad_out[0:width, :] = mm_tn(filtered[...], gate_out[...]).astype(grad_out.dtype)
    grad_out[width : 2 * width, :] = mm_tn(filtered[...], cand_out[...]).astype(grad_out.dtype)


def scan_back(windows, chunk, side, mixed, filtered, read, decay, differ, cand, states, dtype):
    rows, width = mixed.shape
    channels = read.shape[0]
    block = min(channels, 256)
    count = channels // block
    lanes = lambda size: pl.BlockSpec((size, block), lambda j: (0, j))
    half = pl.BlockSpec((rows, block), lambda j: (0, side * count + j))
    out = jax.ShapeDtypeStruct((rows, channels), low)
    return pl.pallas_call(
        functools.partial(scan_kernel, windows, chunk),
        grid=(count,),
        in_specs=[
            whole(mixed),
            whole(filtered),
            pl.BlockSpec((block, width), lambda j: (j, 0)),
            half,
            half,
            half,
            half,
        ],
        out_specs=[
            lanes(rows),
            lanes(rows),
            pl.BlockSpec((windows, 1, block), lambda j: (0, 0, j)),
            lanes(8),
            lanes(3 * width),
        ],
        out_shape=[
            out,
            out,
            jax.ShapeDtypeStruct((windows, 1, channels), wide),
            jax.ShapeDtypeStruct((8, channels), wide),
            jax.ShapeDtypeStruct((3 * width, channels), dtype),
        ],
        scratch_shapes=[pltpu.VMEM((rows, block), wide)],
        compiler_params=params(60, 1),
        cost_estimate=cost(rows * width * 4 * channels, rows * channels * 14, rows * channels),
        name="scan_back",
    )(mixed, filtered, read, decay, differ, cand, states)


def entry_kernel(
    core, own, got, order, back_order, gate_own, cand_own, gate_other, cand_other, middle_in, mixer_own,
    mixer_other, gain, taps, mine_out, sent_out, gain_out, taps_out, rim, head,
):
    step = pl.program_id(1)
    steps = pl.num_programs(1)
    half_chunks = steps // 2
    position = steps - 1 - step
    rows, width = own.shape[1:]
    tap_count = taps.shape[0]
    edge = 8 * (tap_count - 1)
    channels = gate_own.shape[1]

    @pl.when((step == 0) & (pl.program_id(0) == 0))
    def _():
        gain_out[...] = jnp.zeros_like(gain_out)
        taps_out[...] = jnp.zeros_like(taps_out)

    @pl.when(step == 0)
    def _():
        head[...] = jnp.zeros_like(head)

    rim[0:rows, :] = (
        mm_nt(gate_own[...], mixer_own[:, :channels])
        + mm_nt(cand_own[...], mixer_own[:, channels:])
        + mm_nt(gate_other[...], mixer_other[:, :channels])
        + mm_nt(cand_other[...], mixer_other[:, channels:])
    )
    last = lax.broadcasted_iota(jnp.int32, (8, width), 0) == 7
    for at in range(0, edge, 8):
        begins = rim[at : at + 8, :]
        rim[rows + at : rows + at + 8, :] = jnp.where(
            last, pltpu.roll(head[at : at + 8, :], 7, 0), pltpu.roll(begins, 7, 0)
        )
        head[at : at + 8, :] = begins
    x = mm(order[...], jnp.where(position // half_chunks == core[0], own[0], got[0]))
    scale = lax.rsqrt(jnp.mean(x * x, axis=-1, keepdims=True) + epsilon)
    unit = x * scale
    normed = unit * gain[...]
    back = jnp.zeros((rows, width), wide)
    for tap in range(tap_count):
        begin = 8 * (tap_count - 1 - tap)
        ahead = rim[begin : begin + rows, :]
        back = back + taps[tap : tap + 1, :] * ahead
        taps_out[tap : tap + 1, :] += jnp.sum(ahead * normed, axis=0, keepdims=True)
    gain_out[...] += jnp.sum(back * unit, axis=0, keepdims=True)
    weighted = gain[...] * back
    inner = jnp.mean(weighted * x, axis=-1, keepdims=True)
    gradient = middle_in[...] + scale * weighted - x * (scale * scale * scale * inner)
    gradient = mm(back_order[...], gradient.astype(low)).astype(low)
    give(gradient, position, half_chunks, core, mine_out, sent_out)


def give(values, position, half_chunks, core, mine_out, sent_out):
    rows = values.shape[0]
    at = pl.ds(pl.multiple_of(position % half_chunks * rows, rows), rows)
    mine = position // half_chunks == core[0]

    @pl.when(mine)
    def _():
        mine_out[0, at, :] = values

    @pl.when(jnp.logical_not(mine))
    def _():
        sent_out[0, at, :] = values


def side_specs(windows, half, width):
    block = (1, half, width)
    return (
        [
            pl.BlockSpec(block, lambda w, t, core: (windows * core[0] + w, 0, 0)),
            pl.BlockSpec(block, lambda w, t, core: (w, 0, 0)),
        ],
        [
            jax.ShapeDtypeStruct((2 * windows, half, width), low),
            jax.ShapeDtypeStruct((windows, half, width), low),
        ],
    )


def entry(core, inputs, got, orders, projects, back_middle, mixers, gain, taps):
    windows, half, width = got.shape
    chunk = math.gcd(half, 512)
    halves = half // chunk
    steps = 2 * halves
    rows = 2 * half * windows
    row = lambda lanes: pl.BlockSpec(
        (chunk, lanes), lambda w, t, core: (w * steps + steps - 1 - t, 0)
    )
    specs, shapes = side_specs(windows, half, width)
    return pl.pallas_call(
        entry_kernel,
        grid_spec=pltpu.PrefetchScalarGridSpec(
            num_scalar_prefetch=1,
            grid=(windows, steps),
            in_specs=[
                pl.BlockSpec(
                    (1, chunk, width),
                    lambda w, t, core: (windows * core[0] + w, (steps - 1 - t) % halves, 0),
                ),
                pl.BlockSpec((1, chunk, width), lambda w, t, core: (w, (steps - 1 - t) % halves, 0)),
                whole(orders[0]),
                whole(orders[1]),
                *[row(array.shape[1]) for array in projects],
                row(width),
                whole(mixers[0]),
                whole(mixers[1]),
                whole(gain),
                whole(taps),
            ],
            out_specs=[
                *specs,
                pl.BlockSpec((1, width), lambda w, t, core: (0, 0)),
                pl.BlockSpec(taps.shape, lambda w, t, core: (0, 0)),
            ],
            scratch_shapes=[
                pltpu.VMEM((chunk + 8 * (taps.shape[0] - 1), width), wide),
                pltpu.VMEM((8 * (taps.shape[0] - 1), width), wide),
            ],
        ),
        out_shape=[
            *shapes,
            jax.ShapeDtypeStruct((1, width), wide),
            jax.ShapeDtypeStruct(taps.shape, wide),
        ],
        compiler_params=params(60, 2),
        cost_estimate=cost(
            rows * width * 2 * mixers[0].shape[1], rows * mixers[0].shape[1] * 6
        ),
        name="input_gradient",
    )(core, inputs, got, *orders, *projects, back_middle, *mixers, gain, taps)


def leave_kernel(
    core, back_order, active_own, active_other, middle, down_own, down_other, mine_out, sent_out
):
    total = middle[...] + mm(active_own[...], down_own[...]) + mm(active_other[...], down_other[...])
    total = mm(back_order[...], total.astype(low)).astype(low)
    give(total, pl.program_id(1), pl.num_programs(1) // 2, core, mine_out, sent_out)


def leave(windows, core, back_order, actives, middle, downs):
    rows, width = middle.shape
    length = rows // windows
    chunk = back_order.shape[0]
    steps = length // chunk
    row = lambda lanes: pl.BlockSpec((chunk, lanes), lambda w, t, core: (w * steps + t, 0))
    specs, shapes = side_specs(windows, length // 2, width)
    return pl.pallas_call(
        leave_kernel,
        grid_spec=pltpu.PrefetchScalarGridSpec(
            num_scalar_prefetch=1,
            grid=(windows, steps),
            in_specs=[
                whole(back_order),
                row(actives[0].shape[1]),
                row(actives[1].shape[1]),
                row(width),
                whole(downs[0]),
                whole(downs[1]),
            ],
            out_specs=specs,
        ),
        out_shape=shapes,
        compiler_params=params(60, 2),
        cost_estimate=cost(rows * width * 2 * downs[0].shape[0], rows * downs[0].shape[0] * 6),
        name="block_output",
    )(core, back_order, *actives, middle, *downs)


def pack_kernel(width, *refs):
    gains, taps, gain_two, gate_own, gate_other, up_own, up_other, mine_out, sent_out = refs
    for out, gate, up in ((mine_out, gate_own, up_own), (sent_out, gate_other, up_other)):
        out[...] = jnp.zeros_like(out)
        row = 0
        for part in (
            gains[...],
            taps[...],
            gain_two[...],
            jnp.sum(gate[...], axis=0, keepdims=True),
            jnp.sum(up[...], axis=0, keepdims=True),
        ):
            for lane in range(0, part.shape[1], width):
                out[row : row + part.shape[0], 0 : min(width, part.shape[1])] = part[:, lane : lane + width]
                row += part.shape[0]


def pack(width, gains, taps, *rest):
    arrays = [gains, taps, *rest]
    count = taps.shape[0] + 3 + -(-rest[-1].shape[1] // width)
    out = jax.ShapeDtypeStruct((-(-count // 8) * 8, width), wide)
    return pl.pallas_call(
        functools.partial(pack_kernel, width),
        out_shape=[out, out],
        compiler_params=params(60, 0),
        name="pack_short",
    )(*arrays)


def finish_feed_kernel(bit, piece, got, down_out, up_out):
    lead = bit[0] == 0
    a, b = piece[...].astype(wide), got[...].astype(wide)
    down_out[...] = jnp.where(lead, a, b).T
    up_out[...] = jnp.where(lead, b, a)


def finish_feed(bit, piece, got):
    width, units = piece.shape
    block = min(units, 512)
    half = pl.BlockSpec((width, block), lambda j, bit: (0, j))
    return pl.pallas_call(
        finish_feed_kernel,
        grid_spec=pltpu.PrefetchScalarGridSpec(
            num_scalar_prefetch=1,
            grid=(units // block,),
            in_specs=[half, half],
            out_specs=[pl.BlockSpec((block, width), lambda j, bit: (j, 0)), half],
        ),
        out_shape=[
            jax.ShapeDtypeStruct((units, width), wide),
            jax.ShapeDtypeStruct((width, units), wide),
        ],
        compiler_params=params(60, 1),
        name="finish_feed",
    )(bit, piece, got)


def finish_mixer_kernel(bit, piece, got, mixer_out, read_out):
    lead = bit[0] == 0
    width = mixer_out.shape[0]
    cut = piece.shape[0]
    a, b = piece[...].astype(wide), got[...].astype(wide)
    a, b = jnp.where(lead, a, b), jnp.where(lead, b, a)
    mixer_out[:, 0, :] = a[:width]
    mixer_out[0 : cut - width, 1, :] = a[width:]
    mixer_out[cut - width :, 1, :] = b[: 2 * width - cut]
    read_out[...] = b[2 * width - cut :].T


def finish_mixer(bit, piece, got):
    cut, channels = piece.shape
    width = 2 * cut // 3
    return pl.pallas_call(
        finish_mixer_kernel,
        grid_spec=pltpu.PrefetchScalarGridSpec(
            num_scalar_prefetch=1,
            grid=(1,),
            in_specs=[whole(piece), whole(got)],
            out_specs=[
                pl.BlockSpec((width, 2, channels), lambda j, bit: (0, 0, 0)),
                pl.BlockSpec((channels, width), lambda j, bit: (0, 0)),
            ],
        ),
        out_shape=[
            jax.ShapeDtypeStruct((width, 2, channels), wide),
            jax.ShapeDtypeStruct((channels, width), wide),
        ],
        compiler_params=params(60, 1),
        name="finish_mixer",
    )(bit, piece, got)


def partner(array):
    return lax.ppermute(array, "tensor", [(0, 1), (1, 0)])


def hold(*values):
    return lax.optimization_barrier(values)


class DpSum:
    def __init__(self, *terms):
        self.terms = terms
        self.piece = None
        count = lax.axis_size("dp").bit_length() - 1
        first = list(range(count))
        if count >= 2:
            groups = [((0,), (1,)), ((1,), (0,))] + [
                (tuple(first[at : at + 2]),) * 2 for at in range(2, count, 2)
            ]
        else:
            groups = [((bit,), (bit,)) for bit in first]
        self.todo = [(False, group) for group in groups] + [(True, group) for group in groups[::-1]]

    def place(self, group):
        index, core = lax.axis_index("dp"), lax.axis_index("tensor")
        return [
            jnp.where(core == 0, (index >> low_bit) & 1, (index >> high_bit) & 1)
            for low_bit, high_bit in zip(*group)
        ]

    def exchange(self, array, group, mask):
        sizes = (lax.axis_size("dp"), lax.axis_size("tensor"))
        flips = [
            sum(1 << bit for at, bit in enumerate(bits) if mask >> at & 1) for bits in group
        ]
        route = [
            (d * sizes[1] + c, (d ^ flips[c]) * sizes[1] + c)
            for d in range(sizes[0])
            for c in range(sizes[1])
        ]
        return lax.ppermute(array, ("dp", "tensor"), route)

    def prepare(self):
        join, group = self.todo[0]
        if join:
            if self.piece is None:
                self.piece = sum(term.astype(wide) for term in self.terms).astype(low)
            self.sends = [self.piece]
            return
        bits = self.place(group)
        self.spot = sum(bit << at for at, bit in enumerate(bits))
        count = 1 << len(bits)
        self.sends = [self.share(self.spot ^ mask, count).astype(low) for mask in range(1, count)]

    def share(self, spot, count):
        size = self.terms[0].shape[0] // count
        cuts = [lax.dynamic_slice_in_dim(term, spot * size, size) for term in self.terms]
        return sum(cut.astype(wide) for cut in cuts)

    def start(self):
        join, group = self.todo[0]
        count = 1 << len(group[0])
        sends = self.sends * (count - 1) if join else self.sends
        self.got = [
            self.exchange(array, group, mask) for array, mask in zip(sends, range(1, count))
        ]

    def finish(self):
        join, group = self.todo.pop(0)
        if not join:
            self.terms = [self.share(self.spot, 1 << len(group[0])), *self.got]
            return
        parts = [self.piece] + self.got
        for bit in self.place(group):
            parts = [
                jnp.where(
                    bit == 0,
                    jnp.concatenate([parts[at], parts[at + 1]]),
                    jnp.concatenate([parts[at + 1], parts[at]]),
                )
                for at in range(0, len(parts), 2)
            ]
        self.piece = parts[0]


    def begin(self, piece):
        self.sends = [piece]
        self.start()
        return self.got[0]

    def last(self):
        _, group = self.todo[0]
        (bit,) = self.place(group)
        return bit.reshape(1).astype(jnp.int32), self.piece, self.got[0]


class DpSmall(DpSum):
    def __init__(self, total):
        super().__init__(total)
        self.todo = [(join, (group[0], group[0])) for join, group in self.todo if not join]

    def prepare(self):
        self.sends = [self.terms[0]] * ((1 << len(self.todo[0][1][0])) - 1)

    def finish(self):
        _, group = self.todo.pop(0)
        parts = [self.terms[0], *self.got]
        while len(parts) > 1:
            parts = [parts[at] + parts[at + 1] for at in range(0, len(parts), 2)]
        self.terms = parts


def beside(chains, work, *leads, loose=()):
    chains = [chain for chain in chains if chain.todo]
    begun = [*chains, *(chain for chain in loose if chain.todo)]
    for chain in begun:
        chain.prepare()
    held = hold(*leads, *(send for chain in begun for send in chain.sends))
    leads, sends = held[: len(leads)], list(held[len(leads) :])
    for chain in begun:
        chain.sends, sends = sends[: len(chain.sends)], sends[len(chain.sends) :]
        chain.start()
    results = work(*leads)
    held = hold(*results, *(got for chain in chains for got in chain.got))
    results, gots = held[: len(results)], list(held[len(results) :])
    for chain in chains:
        chain.got, gots = gots[: len(chain.got)], gots[len(chain.got) :]
        chain.finish()
    return results


def local(
    inputs,
    initial_state,
    first_gain,
    causal_filter,
    mixer_weight,
    gate_bias,
    readout_weight,
    second_gain,
    up_weight,
    up_bias,
    down_weight,
    cotangent,
):
    sides = lax.axis_size("tensor")
    windows = inputs.shape[0] // sides
    half, width = inputs.shape[1:]
    channels = gate_bias.shape[0]
    units = up_bias.shape[0]
    core = lax.axis_index("tensor")
    core_at = core.reshape(1).astype(jnp.int32)

    def other_windows(array):
        return lax.dynamic_slice_in_dim(array, (1 - core) * windows, windows)

    mixer = mixer_weight.reshape(width, 2 * channels)
    mixers = (mixer, partner(mixer))
    got_inputs = partner(other_windows(inputs))
    reads = (readout_weight, partner(readout_weight))
    biases = (gate_bias[None], partner(gate_bias)[None])
    starts = (initial_state[:, None], partner(initial_state)[:, None])
    got_cotangent = partner(other_windows(cotangent))
    ups = (up_weight, partner(up_weight))
    up_biases = (up_bias[None], partner(up_bias)[None])
    downs = (down_weight, partner(down_weight))
    gain, gain_two = first_gain[None], second_gain[None]

    filtered, decay, differ, cand, states, middle, normed, *orders = forward(
        core_at, inputs, got_inputs, gain, causal_filter, mixers, biases, starts, reads, gain_two
    )
    chunk = orders[0].shape[0]
    active_other, back_other, bias_other, feed_other, tangent = feed(
        core_at, cotangent, got_cotangent, orders[0], None, normed, ups[1], up_biases[1], downs[1], low
    )
    tangent, feed_other = hold(tangent, feed_other)
    feed_got = partner(feed_other)
    active_own, back_own, bias_own, feed_own = feed(
        core_at, cotangent, got_cotangent, orders[0], tangent, normed, ups[0], up_biases[0], downs[0], wide
    )
    actives = [active_own, active_other]
    feed_own, feed_got = hold(feed_own, feed_got)
    feed_sum = DpSum(feed_own, feed_got)
    up_bias_own, up_bias_other = bias_own, bias_other

    def scan(side, lead, dtype):
        return scan_back(
            windows, chunk, side, lead, filtered, reads[side], decay, differ, cand, states, dtype
        )

    back_middle, mixed, gain_two_grad = beside(
        [feed_sum],
        lambda lead: norm_back(tangent, [lead, back_other], middle, ups, gain_two),
        back_own,
    )
    gate_other, cand_other, state_other, bias_other, mixer_other = beside(
        [feed_sum], lambda lead: scan(1, lead, low), mixed
    )
    mixed, mixer_other = hold(mixed, mixer_other)
    mixer_got = partner(mixer_other)
    gate_own, cand_own, state_own, bias_own, mixer_own = beside(
        [feed_sum], lambda lead: scan(0, lead, wide), mixed
    )
    mixer_own, mixer_got = hold(mixer_own, mixer_got)
    mixer_sum = DpSum(mixer_own, mixer_got)
    def put_back(whole_rows, got):
        return lax.dynamic_update_slice_in_dim(whole_rows, got, (1 - core) * windows, 0)

    grad_mine, grad_sent, gain_grad, taps_grad = beside(
        [feed_sum, mixer_sum],
        lambda lead: entry(
            core_at, inputs, got_inputs, orders, [lead, cand_own, gate_other, cand_other],
            back_middle, mixers, gain, causal_filter,
        ),
        gate_own,
    )
    def turn(gain_grad, taps_grad, state_other, grad_sent):
        short, sent = pack(
            width, gain_grad, taps_grad, gain_two_grad, bias_own, bias_other, up_bias_own, up_bias_other
        )
        return short + partner(sent), partner(state_other), partner(grad_sent)

    short, state_got, grad_got = beside(
        [mixer_sum], turn, gain_grad, taps_grad, state_other[:, 0], grad_sent
    )
    short_sum = DpSmall(short)
    out_mine, out_sent = beside(
        [feed_sum, mixer_sum, short_sum],
        lambda lead: leave(windows, core_at, orders[1], [lead, active_other], middle, downs),
        active_own,
    )

    def exits(grad_mine, grad_got, state_own, state_got, out_sent):
        state_gradient = jnp.where(
            core == 0,
            jnp.concatenate([state_own, state_got]),
            jnp.concatenate([state_got, state_own]),
        )
        return put_back(grad_mine, grad_got), state_gradient, partner(out_sent)

    input_gradient, state_gradient, out_got = beside(
        [mixer_sum, short_sum], exits, grad_mine, grad_got, state_own[:, 0], state_got, out_sent,
        loose=[feed_sum],
    )
    while len(mixer_sum.todo) > 1 or short_sum.todo:
        beside([mixer_sum, short_sum], lambda: ())

    def feed_results(mine, got, *gots):
        feed_sum.got = list(gots)
        while len(feed_sum.todo) > 1:
            feed_sum.finish()
            feed_sum.prepare()
            feed_sum.start()
        return put_back(mine, got), *finish_feed(*feed_sum.last())

    block_output, down_sum, up_sum, mixer_last = beside(
        [],
        lambda *leads: (*feed_results(*leads[:-1]), mixer_sum.begin(leads[-1])),
        out_mine,
        out_got,
        *feed_sum.got,
        mixer_sum.piece,
    )
    mixer_sum.got = [mixer_last]
    mixer_grad, read_grad = finish_mixer(*mixer_sum.last())
    short_sum = short_sum.terms[0]
    taps = causal_filter.shape[0]
    end = taps + 3 + units // width
    return (
        block_output,
        input_gradient,
        state_gradient,
        short_sum[0],
        short_sum[1 : 1 + taps],
        mixer_grad,
        short_sum[taps + 2, :channels],
        read_grad,
        short_sum[taps + 1],
        up_sum,
        short_sum[taps + 3 : end].reshape(units),
        down_sum,
    )


def solution(mesh):
    return jax.shard_map(
        local,
        mesh=mesh,
        in_specs=(
            P("dp", "tensor", None),
            P("dp", "tensor"),
            P(),
            P(),
            P(None, None, "tensor"),
            P("tensor"),
            P("tensor", None),
            P(),
            P(None, "tensor"),
            P("tensor"),
            P("tensor", None),
            P("dp", "tensor", None),
        ),
        out_specs=(
            P("dp", "tensor", None),
            P("dp", "tensor", None),
            P("dp", "tensor"),
            P(),
            P(),
            P(None, None, "tensor"),
            P("tensor"),
            P("tensor", None),
            P(),
            P(None, "tensor"),
            P("tensor"),
            P("tensor", None),
        ),
        check_vma=False,
    )
```

```python
import functools
import math

import jax
import jax.numpy as jnp
from jax import lax
from jax.experimental import pallas as pl
from jax.experimental.pallas import tpu as pltpu
from jax.sharding import PartitionSpec as P

epsilon = 1e-06
low = jnp.bfloat16
wide = jnp.float32
root = math.sqrt(2.0 / math.pi)
cubic = 0.044715
MIB = 1 << 20


def mm(left, right):
    return lax.dot_general(left, right, (((1,), (0,)), ((), ())), preferred_element_type=wide)


def mm_nt(left, right):
    return lax.dot_general(left, right, (((1,), (1,)), ((), ())), preferred_element_type=wide)


def mm_tn(left, right):
    return lax.dot_general(left, right, (((0,), (0,)), ((), ())), preferred_element_type=wide)


def params(mib, grid):
    return pltpu.CompilerParams(
        vmem_limit_bytes=mib * MIB, dimension_semantics=("arbitrary",) * grid
    )


def cost(macs, moved, curves=0):
    return pl.CostEstimate(flops=2 * macs, bytes_accessed=moved, transcendentals=curves)


def whole(array):
    rank = array.ndim
    return pl.BlockSpec(array.shape, lambda *_: (0,) * rank, pipeline_mode=pl.Buffered(1))


def stream_order(rows, inverse):
    at = lax.broadcasted_iota(jnp.int32, (rows, rows), 1 if inverse else 0)
    source = lax.broadcasted_iota(jnp.int32, (rows, rows), 0 if inverse else 1)
    moved = jnp.bitwise_and(at, 7) * (rows // 8) + lax.shift_right_logical(at, 3)
    return jnp.where(source == moved, 1.0, 0.0).astype(low)


def forward_kernel(
    core, own, got, gain, taps, mixer_own, mixer_other, bias_own, bias_other, start_own, start_other,
    read_own, read_other,
    gain_two, filtered_out, decay_out, differ_out, cand_out, state_out, middle_out, normed_out,
    order, back_order, streams, rim, tail, gates, cands, carry,
):
    half_chunks = pl.num_programs(1) // 2
    step = pl.program_id(1)
    rows = own.shape[1]
    width = own.shape[2]
    count = rows // 8
    tap_count = taps.shape[0]
    edge = 8 * (tap_count - 1)
    channels = read_own.shape[0]
    mine = step // half_chunks == core[0]

    @pl.when((step == 0) & (pl.program_id(0) == 0))
    def _():
        order[...] = stream_order(rows, False)
        back_order[...] = stream_order(rows, True)

    x = mm(order[...], jnp.where(mine, own[0], got[0]))
    streams[...] = x
    scale = lax.rsqrt(jnp.mean(x * x, axis=-1, keepdims=True) + epsilon)
    normed = x * scale * gain[...]

    @pl.when(step == 0)
    def _():
        tail[...] = jnp.zeros_like(tail)
        for at, start in enumerate((start_own, start_other)):
            row = start[pl.ds(core[0] * pl.num_programs(0) + pl.program_id(0), 1), :]
            carry[:, at * channels : (at + 1) * channels] = jnp.broadcast_to(row, (8, channels))

    rim[edge:, :] = normed
    first = lax.broadcasted_iota(jnp.int32, (8, width), 0) == 0
    for at in range(0, edge, 8):
        ends = normed[rows - edge + at : rows - edge + at + 8, :]
        rim[at : at + 8, :] = jnp.where(
            first, pltpu.roll(tail[at : at + 8, :], 1, 0), pltpu.roll(ends, 1, 0)
        )
        tail[at : at + 8, :] = ends
    total = taps[0:1, :] * rim[0:rows, :]
    for tap in range(1, tap_count):
        total = total + taps[tap : tap + 1, :] * rim[8 * tap : 8 * tap + rows, :]
    filtered = total.astype(low)
    filtered_out[...] = filtered
    for at, (weight, bias) in enumerate(((mixer_own, bias_own), (mixer_other, bias_other))):
        lanes = slice(at * channels, (at + 1) * channels)
        gates[:, lanes] = mm(filtered, weight[:, :channels]) + bias[...]
        cands[:, lanes] = mm(filtered, weight[:, channels:])

    group = min(2 * channels, 1024)
    place = lax.broadcasted_iota(jnp.int32, (8, group), 0)
    for lane in range(0, 2 * channels, group):
        lanes = slice(lane, lane + group)

        def open_gates(index, state):
            factor, offset = state
            base = pl.multiple_of(index * 16, 16)
            kept = []
            for sub in (0, 8):
                c = cands[pl.ds(base + sub, 8), lanes]
                decay = jax.nn.sigmoid(-gates[pl.ds(base + sub, 8), lanes])
                soft = jnp.maximum(c, jnp.log(1.0 + jnp.exp(jnp.minimum(c, 60.0))))
                decay_out[pl.ds(base + sub, 8), lanes] = decay
                gates[pl.ds(base + sub, 8), lanes] = soft
                factor = factor * decay
                offset = soft + decay * (offset - soft)
                kept.append(c)
            cand_out[pl.ds(base, 16), lanes] = jnp.concatenate(kept, axis=0).astype(low)
            return factor, offset

        factor, offset = lax.fori_loop(
            0,
            count // 2,
            open_gates,
            (jnp.ones((8, group), wide), jnp.zeros((8, group), wide)),
            unroll=True,
        )
        for hop in (1, 2, 4):
            inside = place >= hop
            offset = factor * jnp.where(inside, pltpu.roll(offset, hop, 0), 0.0) + offset
            factor = factor * jnp.where(inside, pltpu.roll(factor, hop, 0), 1.0)
        entered = carry[:, lanes]
        leaving = factor * entered + offset
        carry[:, lanes] = jnp.broadcast_to(leaving[7:8, :], leaving.shape)
        entered = jnp.where(place >= 1, pltpu.roll(leaving, 1, 0), entered)

        def run_states(index, state):
            base = pl.multiple_of(index * 16, 16)
            held, differ = [], []
            for sub in (0, 8):
                soft = gates[pl.ds(base + sub, 8), lanes]
                differ.append(soft - state)
                state = soft - decay_out[pl.ds(base + sub, 8), lanes] * differ[-1]
                held.append(state)
            differ_out[pl.ds(base, 16), lanes] = jnp.concatenate(differ, axis=0).astype(low)
            state_out[pl.ds(base, 16), lanes] = jnp.concatenate(held, axis=0).astype(low)
            return state

        lax.fori_loop(0, count // 2, run_states, entered, unroll=True)

    mixed = mm(state_out[:, :channels], read_own[...]) + mm(
        state_out[:, channels:], read_other[...]
    )
    middle = streams[...] + mixed
    middle_out[...] = middle
    scale_two = lax.rsqrt(jnp.mean(middle * middle, axis=-1, keepdims=True) + epsilon)
    normed_out[...] = (middle * scale_two * gain_two[...]).astype(low)


def halves_specs(chunk, width, windows, halves):
    return (
        pl.BlockSpec(
            (1, chunk, width), lambda w, t, core: (windows * core[0] + w, t % halves, 0)
        ),
        pl.BlockSpec((1, chunk, width), lambda w, t, core: (w, t % halves, 0)),
    )


def forward(core, inputs, got, gain, taps, mixers, biases, starts, reads, gain_two):
    windows, half, width = got.shape
    channels = reads[0].shape[0]
    chunk = math.gcd(half, 512)
    halves = half // chunk
    steps = 2 * halves
    rows = 2 * half * windows
    row = lambda lanes: pl.BlockSpec((chunk, lanes), lambda w, t, core: (w * steps + t, 0))
    out = lambda lanes, dtype: jax.ShapeDtypeStruct((rows, lanes), dtype)
    return pl.pallas_call(
        forward_kernel,
        grid_spec=pltpu.PrefetchScalarGridSpec(
            num_scalar_prefetch=1,
            grid=(windows, steps),
            in_specs=[
                *halves_specs(chunk, width, windows, halves),
                whole(gain),
                whole(taps),
                whole(mixers[0]),
                whole(mixers[1]),
                whole(biases[0]),
                whole(biases[1]),
                whole(starts[0]),
                whole(starts[1]),
                whole(reads[0]),
                whole(reads[1]),
                whole(gain_two),
            ],
            out_specs=[
                row(width),
                row(2 * channels),
                row(2 * channels),
                row(2 * channels),
                row(2 * channels),
                row(width),
                row(width),
                pl.BlockSpec((chunk, chunk), lambda w, t, core: (0, 0)),
                pl.BlockSpec((chunk, chunk), lambda w, t, core: (0, 0)),
            ],
            scratch_shapes=[
                pltpu.VMEM((chunk, width), wide),
                pltpu.VMEM((chunk + 8 * (taps.shape[0] - 1), width), wide),
                pltpu.VMEM((8 * (taps.shape[0] - 1), width), wide),
                pltpu.VMEM((chunk, 2 * channels), wide),
                pltpu.VMEM((chunk, 2 * channels), wide),
                pltpu.VMEM((8, 2 * channels), wide),
            ],
        ),
        out_shape=[
            out(width, low),
            out(2 * channels, wide),
            out(2 * channels, low),
            out(2 * channels, low),
            out(2 * channels, low),
            out(width, wide),
            out(width, low),
            jax.ShapeDtypeStruct((chunk, chunk), low),
            jax.ShapeDtypeStruct((chunk, chunk), low),
        ],
        compiler_params=params(60, 2),
        cost_estimate=cost(rows * width * channels * 6, rows * channels * 24, rows * channels * 8),
        name="forward_mixer",
    )(core, inputs, got, gain, taps, *mixers, *biases, *starts, *reads, gain_two)


def feed(core, cotangent, got, order, tangent, normed, up, bias, down, dtype):
    windows, half, width = got.shape
    units = up.shape[1]
    rows = normed.shape[0]
    chunk = order.shape[0]
    block = min(units, 512)
    fresh = tangent is None

    def kernel(core, *refs):
        if fresh:
            own, came, order_in, *refs, tangent_in = refs
        else:
            tangent_in, *refs = refs
        normed_in, up_in, bias_in, down_in, active_out, back_out, bias_out, grad_out = refs

        if fresh:

            @pl.when(pl.program_id(0) == 0)
            def _():
                for window in range(windows):
                    for side in range(2):
                        mine = core[0] == side
                        for at in range(0, half, chunk):
                            rows_at = slice(at, at + chunk)
                            to = (2 * window + side) * half + at
                            tangent_in[to : to + chunk, :] = mm(
                                order_in[...],
                                jnp.where(mine, own[window, rows_at, :], came[window, rows_at, :]),
                            ).astype(low)

        total = jnp.zeros((8, block), wide)
        for at in range(0, rows, chunk):
            rows_at = slice(at, at + chunk)
            v = mm(normed_in[rows_at, :], up_in[...]) + bias_in[...]
            back = mm_nt(tangent_in[rows_at, :], down_in[...])
            square = v * v
            s = jax.nn.sigmoid(v * (2.0 * root + (2.0 * root * cubic) * square))
            active = v * s
            slope = s + (active * (1.0 - s)) * (2.0 * root + (6.0 * root * cubic) * square)
            back = back * slope
            for row in range(0, chunk, 8):
                total = total + back[row : row + 8, :]
            active_out[rows_at, :] = active.astype(low)
            back_out[rows_at, :] = back.astype(low)
        bias_out[...] = total
        grad_out[0:width, :] = mm_tn(tangent_in[...], active_out[...]).astype(dtype)
        grad_out[width:, :] = mm_tn(normed_in[...], back_out[...]).astype(dtype)

    lanes = lambda count: pl.BlockSpec((count, block), lambda j, core: (0, j))
    in_specs = [whole(normed), lanes(width), lanes(1), pl.BlockSpec((block, width), lambda j, core: (j, 0))]
    arrays = [normed, up, bias, down]
    out_specs = [lanes(rows), lanes(rows), lanes(8), lanes(2 * width)]
    out_shape = [
        jax.ShapeDtypeStruct((rows, units), low),
        jax.ShapeDtypeStruct((rows, units), low),
        jax.ShapeDtypeStruct((8, units), wide),
        jax.ShapeDtypeStruct((2 * width, units), dtype),
    ]
    if fresh:
        in_specs = [
            pl.BlockSpec((windows, half, width), lambda j, core: (core[0], 0, 0)),
            whole(got),
            whole(order),
        ] + in_specs
        arrays = [cotangent, got, order] + arrays
        out_specs.append(pl.BlockSpec((rows, width), lambda j, core: (0, 0)))
        out_shape.append(jax.ShapeDtypeStruct((rows, width), low))
    else:
        in_specs.insert(0, whole(tangent))
        arrays.insert(0, tangent)
    return pl.pallas_call(
        kernel,
        grid_spec=pltpu.PrefetchScalarGridSpec(
            num_scalar_prefetch=1, grid=(units // block,), in_specs=in_specs, out_specs=out_specs
        ),
        out_shape=out_shape,
        compiler_params=params(60, 1),
        cost_estimate=cost(rows * width * units * 4, rows * units * 4, rows * units),
        name="feed_forward",
    )(core, *arrays)


def norm_kernel(
    tangent, back_own, back_other, middle_in, up_own, up_other, gain_two, middle_out, mixed_out, gain_out
):
    @pl.when(pl.program_id(0) == 0)
    def _():
        gain_out[...] = jnp.zeros_like(gain_out)

    rows = tangent.shape[0]
    part = math.gcd(rows, 256)
    for begin in range(0, rows, part):
        at = slice(begin, begin + part)
        back = mm_nt(back_own[at, :], up_own[...]) + mm_nt(back_other[at, :], up_other[...])
        middle = middle_in[at, :]
        scale = lax.rsqrt(jnp.mean(middle * middle, axis=-1, keepdims=True) + epsilon)
        gain_out[...] += jnp.sum(back * (middle * scale), axis=0, keepdims=True)
        weighted = gain_two[...] * back
        inner = jnp.mean(weighted * middle, axis=-1, keepdims=True)
        back_middle = (
            tangent[at, :].astype(wide) + scale * weighted - middle * (scale * scale * scale * inner)
        )
        middle_out[at, :] = back_middle
        mixed_out[at, :] = back_middle.astype(low)


def norm_back(tangent, backs, middle, ups, gain_two):
    rows, width = tangent.shape
    units = ups[0].shape[1]
    chunk = math.gcd(rows, 512)
    row = lambda lanes: pl.BlockSpec((chunk, lanes), lambda t: (t, 0))
    return pl.pallas_call(
        norm_kernel,
        grid=(rows // chunk,),
        in_specs=[
            row(width),
            row(units),
            row(units),
            row(width),
            whole(ups[0]),
            whole(ups[1]),
            whole(gain_two),
        ],
        out_specs=[row(width), row(width), pl.BlockSpec((1, width), lambda t: (0, 0))],
        out_shape=[
            jax.ShapeDtypeStruct((rows, width), wide),
            jax.ShapeDtypeStruct((rows, width), low),
            jax.ShapeDtypeStruct((1, width), wide),
        ],
        compiler_params=params(60, 1),
        cost_estimate=cost(rows * width * 2 * units, rows * (units * 4 + width * 16)),
        name="norm_back",
    )(tangent, *backs, middle, *ups, gain_two)


def scan_kernel(
    windows, chunk, mixed, filtered, read, decay_in, differ_in, cand_in, state_in,
    gate_out, cand_out, state_out, bias_out, grad_out, states,
):
    rows, width = mixed.shape
    group = read.shape[0]
    count = chunk // 16
    chunks = rows // chunk
    each = chunks // windows
    place = lax.broadcasted_iota(jnp.int32, (8, group), 0)
    states[...] = mm_nt(mixed[...], read[...])
    factors = [jnp.ones((8, group), wide)] * chunks
    offsets = [jnp.zeros((8, group), wide)] * chunks
    for index in range(2 * count - 1, -1, -1):
        for at in range(chunks):
            here = slice(at * chunk + 8 * index, at * chunk + 8 * index + 8)
            decay = decay_in[here, :]
            factors[at] = factors[at] * decay
            offsets[at] = decay * (offsets[at] + states[here, :])
    later = [None] * chunks
    for window in range(windows):
        entered = jnp.zeros((8, group), wide)
        for at in range(window * each + each - 1, window * each - 1, -1):
            factor, offset = factors[at], offsets[at]
            for hop in (1, 2, 4):
                inside = place < 8 - hop
                offset = factor * jnp.where(inside, pltpu.roll(offset, 8 - hop, 0), 0.0) + offset
                factor = factor * jnp.where(inside, pltpu.roll(factor, 8 - hop, 0), 1.0)
            leaving = factor * entered + offset
            later[at] = jnp.where(place < 7, pltpu.roll(leaving, 7, 0), entered)
            entered = jnp.broadcast_to(leaving[0:1, :], leaving.shape)
        state_out[window] = entered[0:1, :]
    bias = [jnp.zeros((8, group), wide)] * chunks
    for index in range(count - 1, -1, -1):
        for at in range(chunks):
            base = at * chunk + 16 * index
            both = slice(base, base + 16)
            differ = differ_in[both, :].astype(wide)
            chosen = jax.nn.sigmoid(cand_in[both, :].astype(wide))
            gate, cand = [None] * 2, [None] * 2
            for half in (1, 0):
                near = slice(8 * half, 8 * half + 8)
                here = slice(base + 8 * half, base + 8 * half + 8)
                decay = decay_in[here, :]
                carried = states[here, :] + later[at]
                later[at] = decay * carried
                opened = carried - later[at]
                gate[half] = decay * opened * differ[near]
                cand[half] = opened * chosen[near]
                bias[at] = bias[at] + gate[half]
            gate_out[both, :] = jnp.concatenate(gate, axis=0).astype(low)
            cand_out[both, :] = jnp.concatenate(cand, axis=0).astype(low)
    bias_out[...] = sum(bias[1:], bias[0])
    grad_out[2 * width :, :] = mm_tn(mixed[...], state_in[...]).astype(grad_out.dtype)
    grad_out[0:width, :] = mm_tn(filtered[...], gate_out[...]).astype(grad_out.dtype)
    grad_out[width : 2 * width, :] = mm_tn(filtered[...], cand_out[...]).astype(grad_out.dtype)


def scan_back(windows, chunk, side, mixed, filtered, read, decay, differ, cand, states, dtype):
    rows, width = mixed.shape
    channels = read.shape[0]
    block = min(channels, 256)
    count = channels // block
    lanes = lambda size: pl.BlockSpec((size, block), lambda j: (0, j))
    half = pl.BlockSpec((rows, block), lambda j: (0, side * count + j))
    out = jax.ShapeDtypeStruct((rows, channels), low)
    return pl.pallas_call(
        functools.partial(scan_kernel, windows, chunk),
        grid=(count,),
        in_specs=[
            whole(mixed),
            whole(filtered),
            pl.BlockSpec((block, width), lambda j: (j, 0)),
            half,
            half,
            half,
            half,
        ],
        out_specs=[
            lanes(rows),
            lanes(rows),
            pl.BlockSpec((windows, 1, block), lambda j: (0, 0, j)),
            lanes(8),
            lanes(3 * width),
        ],
        out_shape=[
            out,
            out,
            jax.ShapeDtypeStruct((windows, 1, channels), wide),
            jax.ShapeDtypeStruct((8, channels), wide),
            jax.ShapeDtypeStruct((3 * width, channels), dtype),
        ],
        scratch_shapes=[pltpu.VMEM((rows, block), wide)],
        compiler_params=params(60, 1),
        cost_estimate=cost(rows * width * 4 * channels, rows * channels * 14, rows * channels),
        name="scan_back",
    )(mixed, filtered, read, decay, differ, cand, states)


def entry_kernel(
    core, own, got, order, back_order, gate_own, cand_own, gate_other, cand_other, middle_in, mixer_own,
    mixer_other, gain, taps, mine_out, sent_out, gain_out, taps_out, rim, head,
):
    step = pl.program_id(1)
    steps = pl.num_programs(1)
    half_chunks = steps // 2
    position = steps - 1 - step
    rows, width = own.shape[1:]
    tap_count = taps.shape[0]
    edge = 8 * (tap_count - 1)
    channels = gate_own.shape[1]

    @pl.when((step == 0) & (pl.program_id(0) == 0))
    def _():
        gain_out[...] = jnp.zeros_like(gain_out)
        taps_out[...] = jnp.zeros_like(taps_out)

    @pl.when(step == 0)
    def _():
        head[...] = jnp.zeros_like(head)

    rim[0:rows, :] = (
        mm_nt(gate_own[...], mixer_own[:, :channels])
        + mm_nt(cand_own[...], mixer_own[:, channels:])
        + mm_nt(gate_other[...], mixer_other[:, :channels])
        + mm_nt(cand_other[...], mixer_other[:, channels:])
    )
    last = lax.broadcasted_iota(jnp.int32, (8, width), 0) == 7
    for at in range(0, edge, 8):
        begins = rim[at : at + 8, :]
        rim[rows + at : rows + at + 8, :] = jnp.where(
            last, pltpu.roll(head[at : at + 8, :], 7, 0), pltpu.roll(begins, 7, 0)
        )
        head[at : at + 8, :] = begins
    x = mm(order[...], jnp.where(position // half_chunks == core[0], own[0], got[0]))
    scale = lax.rsqrt(jnp.mean(x * x, axis=-1, keepdims=True) + epsilon)
    unit = x * scale
    normed = unit * gain[...]
    back = jnp.zeros((rows, width), wide)
    for tap in range(tap_count):
        begin = 8 * (tap_count - 1 - tap)
        ahead = rim[begin : begin + rows, :]
        back = back + taps[tap : tap + 1, :] * ahead
        taps_out[tap : tap + 1, :] += jnp.sum(ahead * normed, axis=0, keepdims=True)
    gain_out[...] += jnp.sum(back * unit, axis=0, keepdims=True)
    weighted = gain[...] * back
    inner = jnp.mean(weighted * x, axis=-1, keepdims=True)
    gradient = middle_in[...] + scale * weighted - x * (scale * scale * scale * inner)
    gradient = mm(back_order[...], gradient.astype(low)).astype(low)
    give(gradient, position, half_chunks, core, mine_out, sent_out)


def give(values, position, half_chunks, core, mine_out, sent_out):
    rows = values.shape[0]
    at = pl.ds(pl.multiple_of(position % half_chunks * rows, rows), rows)
    mine = position // half_chunks == core[0]

    @pl.when(mine)
    def _():
        mine_out[0, at, :] = values

    @pl.when(jnp.logical_not(mine))
    def _():
        sent_out[0, at, :] = values


def side_specs(windows, half, width):
    block = (1, half, width)
    return (
        [
            pl.BlockSpec(block, lambda w, t, core: (windows * core[0] + w, 0, 0)),
            pl.BlockSpec(block, lambda w, t, core: (w, 0, 0)),
        ],
        [
            jax.ShapeDtypeStruct((2 * windows, half, width), low),
            jax.ShapeDtypeStruct((windows, half, width), low),
        ],
    )


def entry(core, inputs, got, orders, projects, back_middle, mixers, gain, taps):
    windows, half, width = got.shape
    chunk = math.gcd(half, 512)
    halves = half // chunk
    steps = 2 * halves
    rows = 2 * half * windows
    row = lambda lanes: pl.BlockSpec(
        (chunk, lanes), lambda w, t, core: (w * steps + steps - 1 - t, 0)
    )
    specs, shapes = side_specs(windows, half, width)
    return pl.pallas_call(
        entry_kernel,
        grid_spec=pltpu.PrefetchScalarGridSpec(
            num_scalar_prefetch=1,
            grid=(windows, steps),
            in_specs=[
                pl.BlockSpec(
                    (1, chunk, width),
                    lambda w, t, core: (windows * core[0] + w, (steps - 1 - t) % halves, 0),
                ),
                pl.BlockSpec((1, chunk, width), lambda w, t, core: (w, (steps - 1 - t) % halves, 0)),
                whole(orders[0]),
                whole(orders[1]),
                *[row(array.shape[1]) for array in projects],
                row(width),
                whole(mixers[0]),
                whole(mixers[1]),
                whole(gain),
                whole(taps),
            ],
            out_specs=[
                *specs,
                pl.BlockSpec((1, width), lambda w, t, core: (0, 0)),
                pl.BlockSpec(taps.shape, lambda w, t, core: (0, 0)),
            ],
            scratch_shapes=[
                pltpu.VMEM((chunk + 8 * (taps.shape[0] - 1), width), wide),
                pltpu.VMEM((8 * (taps.shape[0] - 1), width), wide),
            ],
        ),
        out_shape=[
            *shapes,
            jax.ShapeDtypeStruct((1, width), wide),
            jax.ShapeDtypeStruct(taps.shape, wide),
        ],
        compiler_params=params(60, 2),
        cost_estimate=cost(
            rows * width * 2 * mixers[0].shape[1], rows * mixers[0].shape[1] * 6
        ),
        name="input_gradient",
    )(core, inputs, got, *orders, *projects, back_middle, *mixers, gain, taps)


def leave_kernel(
    core, back_order, active_own, active_other, middle, down_own, down_other, mine_out, sent_out
):
    total = middle[...] + mm(active_own[...], down_own[...]) + mm(active_other[...], down_other[...])
    total = mm(back_order[...], total.astype(low)).astype(low)
    give(total, pl.program_id(1), pl.num_programs(1) // 2, core, mine_out, sent_out)


def leave(windows, core, back_order, actives, middle, downs):
    rows, width = middle.shape
    length = rows // windows
    chunk = back_order.shape[0]
    steps = length // chunk
    row = lambda lanes: pl.BlockSpec((chunk, lanes), lambda w, t, core: (w * steps + t, 0))
    specs, shapes = side_specs(windows, length // 2, width)
    return pl.pallas_call(
        leave_kernel,
        grid_spec=pltpu.PrefetchScalarGridSpec(
            num_scalar_prefetch=1,
            grid=(windows, steps),
            in_specs=[
                whole(back_order),
                row(actives[0].shape[1]),
                row(actives[1].shape[1]),
                row(width),
                whole(downs[0]),
                whole(downs[1]),
            ],
            out_specs=specs,
        ),
        out_shape=shapes,
        compiler_params=params(60, 2),
        cost_estimate=cost(rows * width * 2 * downs[0].shape[0], rows * downs[0].shape[0] * 6),
        name="block_output",
    )(core, back_order, *actives, middle, *downs)


def pack_kernel(width, *refs):
    gains, taps, gain_two, gate_own, gate_other, up_own, up_other, mine_out, sent_out = refs
    for out, gate, up in ((mine_out, gate_own, up_own), (sent_out, gate_other, up_other)):
        out[...] = jnp.zeros_like(out)
        row = 0
        for part in (
            gains[...],
            taps[...],
            gain_two[...],
            jnp.sum(gate[...], axis=0, keepdims=True),
            jnp.sum(up[...], axis=0, keepdims=True),
        ):
            for lane in range(0, part.shape[1], width):
                out[row : row + part.shape[0], 0 : min(width, part.shape[1])] = part[:, lane : lane + width]
                row += part.shape[0]


def pack(width, gains, taps, *rest):
    arrays = [gains, taps, *rest]
    count = taps.shape[0] + 3 + -(-rest[-1].shape[1] // width)
    out = jax.ShapeDtypeStruct((-(-count // 8) * 8, width), wide)
    return pl.pallas_call(
        functools.partial(pack_kernel, width),
        out_shape=[out, out],
        compiler_params=params(60, 0),
        name="pack_short",
    )(*arrays)


def in_order(place, parts):
    for at in range(len(parts).bit_length() - 1):
        lead = place[at] == 0
        parts = [
            jnp.where(lead, parts[one], parts[one ^ (1 << at)]) for one in range(len(parts))
        ]
    return parts


def finish_feed_kernel(place, *refs):
    *shares, down_out, up_out = refs
    total = jnp.concatenate(in_order(place, [share[...].astype(wide) for share in shares]))
    width = up_out.shape[0]
    down_out[...] = total[:width].T
    up_out[...] = total[width:]


def finish_feed(place, shares):
    cut, units = shares[0].shape
    width = cut * len(shares) // 2
    block = min(units, 512)
    return pl.pallas_call(
        finish_feed_kernel,
        grid_spec=pltpu.PrefetchScalarGridSpec(
            num_scalar_prefetch=1,
            grid=(units // block,),
            in_specs=[pl.BlockSpec((cut, block), lambda j, place: (0, j))] * len(shares),
            out_specs=[
                pl.BlockSpec((block, width), lambda j, place: (j, 0)),
                pl.BlockSpec((width, block), lambda j, place: (0, j)),
            ],
        ),
        out_shape=[
            jax.ShapeDtypeStruct((units, width), wide),
            jax.ShapeDtypeStruct((width, units), wide),
        ],
        compiler_params=params(60, 1),
        name="finish_feed",
    )(place, *shares)


def finish_mixer_kernel(place, *refs):
    *shares, mixer_out, read_out, gain_out, taps_out, gain_two_out, gate_out, up_out = refs
    width = mixer_out.shape[0]
    cut = 3 * width // len(shares)
    total = jnp.concatenate(in_order(place, [share[:cut, :].astype(wide) for share in shares]))
    short = sum_alike([share[cut:, :] for share in shares])
    row = 0
    for out in (gain_out, taps_out, gain_two_out, gate_out, up_out):
        for lane in range(0, out.shape[1], width):
            some = min(width, out.shape[1])
            out[:, lane : lane + some] = short[row : row + out.shape[0], :some]
            row += out.shape[0]
    mixer_out[:, 0, :] = total[:width]
    mixer_out[:, 1, :] = total[width : 2 * width]
    read_out[...] = total[2 * width :].T


def finish_mixer(place, shares, width, taps, units):
    channels = shares[0].shape[1]
    short = [(1, width), (taps, width), (1, width), (1, channels), (1, units)]
    return pl.pallas_call(
        finish_mixer_kernel,
        grid_spec=pltpu.PrefetchScalarGridSpec(
            num_scalar_prefetch=1,
            grid=(1,),
            in_specs=[whole(share) for share in shares],
            out_specs=[
                pl.BlockSpec((width, 2, channels), lambda j, place: (0, 0, 0)),
                pl.BlockSpec((channels, width), lambda j, place: (0, 0)),
                *[pl.BlockSpec(shape, lambda j, place: (0, 0)) for shape in short],
            ],
        ),
        out_shape=[
            jax.ShapeDtypeStruct((width, 2, channels), wide),
            jax.ShapeDtypeStruct((channels, width), wide),
            *[jax.ShapeDtypeStruct(shape, wide) for shape in short],
        ],
        compiler_params=params(60, 1),
        name="finish_mixer",
    )(place, *shares)


def partner(array):
    return lax.ppermute(array, "tensor", [(0, 1), (1, 0)])


def hold(*values):
    return lax.optimization_barrier(values)


class DpSum:
    paired = True

    def __init__(self, *terms):
        self.terms = terms
        self.piece = None
        count = lax.axis_size("dp").bit_length() - 1
        first = list(range(count))
        groups = [(tuple(first[at : at + 2]),) * 2 for at in range(0, count, 2)]
        if self.paired and count >= 2:
            groups[:1] = [((0,), (1,)), ((1,), (0,))]
        self.todo = [(False, group) for group in groups] + [(True, group) for group in groups[::-1]]

    def place(self, group):
        index, core = lax.axis_index("dp"), lax.axis_index("tensor")
        return [
            jnp.where(core == 0, (index >> low_bit) & 1, (index >> high_bit) & 1)
            for low_bit, high_bit in zip(*group)
        ]

    def exchange(self, array, group, mask):
        sizes = (lax.axis_size("dp"), lax.axis_size("tensor"))
        flips = [
            sum(1 << bit for at, bit in enumerate(bits) if mask >> at & 1) for bits in group
        ]
        route = [
            (d * sizes[1] + c, (d ^ flips[c]) * sizes[1] + c)
            for d in range(sizes[0])
            for c in range(sizes[1])
        ]
        return lax.ppermute(array, ("dp", "tensor"), route)

    def prepare(self):
        join, group = self.todo[0]
        if join:
            if self.piece is None:
                self.piece = sum(term.astype(wide) for term in self.terms).astype(low)
            self.sends = [self.piece]
            return
        bits = self.place(group)
        self.spot = sum(bit << at for at, bit in enumerate(bits))
        count = 1 << len(bits)
        self.sends = [self.share(self.spot ^ mask, count).astype(low) for mask in range(1, count)]

    def share(self, spot, count):
        size = self.terms[0].shape[0] // count
        cuts = [lax.dynamic_slice_in_dim(term, spot * size, size) for term in self.terms]
        return sum(cut.astype(wide) for cut in cuts)

    def start(self):
        join, group = self.todo[0]
        count = 1 << len(group[0])
        sends = self.sends * (count - 1) if join else self.sends
        self.got = [
            self.exchange(array, group, mask) for array, mask in zip(sends, range(1, count))
        ]

    def finish(self):
        join, group = self.todo.pop(0)
        if not join:
            self.terms = [self.share(self.spot, 1 << len(group[0])), *self.got]
            return
        parts = [self.piece] + self.got
        for bit in self.place(group):
            parts = [
                jnp.where(
                    bit == 0,
                    jnp.concatenate([parts[at], parts[at + 1]]),
                    jnp.concatenate([parts[at + 1], parts[at]]),
                )
                for at in range(0, len(parts), 2)
            ]
        self.piece = parts[0]


    def last(self):
        _, group = self.todo[0]
        return jnp.stack(self.place(group)).astype(jnp.int32), [self.sends[0], *self.got]


class DpDirect(DpSum):
    paired = False
    rider = None

    def prepare(self):
        super().prepare()
        self.rides = self.rider is not None and (not self.todo[0][0] or len(self.todo) == 1)
        if self.rides:
            self.low_rider = self.rider.astype(low)
            self.sends = [jnp.concatenate([send, self.low_rider]) for send in self.sends]

    def finish(self):
        if self.rides:
            size = self.got[0].shape[0] - self.low_rider.shape[0]
            self.rider = sum_alike([self.low_rider, *(got[size:] for got in self.got)])
            self.got = [got[:size] for got in self.got]
        super().finish()


def sum_alike(parts):
    parts = [part.astype(wide) for part in parts]
    while len(parts) > 1:
        parts = [parts[at] + parts[at + 1] for at in range(0, len(parts), 2)]
    return parts[0]


def beside(chains, work, *leads, loose=()):
    chains = [chain for chain in chains if chain.todo]
    begun = [*chains, *(chain for chain in loose if chain.todo)]
    for chain in begun:
        chain.prepare()
    held = hold(*leads, *(send for chain in begun for send in chain.sends))
    leads, sends = held[: len(leads)], list(held[len(leads) :])
    for chain in begun:
        chain.sends, sends = sends[: len(chain.sends)], sends[len(chain.sends) :]
        chain.start()
    results = work(*leads)
    held = hold(*results, *(got for chain in chains for got in chain.got))
    results, gots = held[: len(results)], list(held[len(results) :])
    for chain in chains:
        chain.got, gots = gots[: len(chain.got)], gots[len(chain.got) :]
        chain.finish()
    return results


def local(
    inputs,
    initial_state,
    first_gain,
    causal_filter,
    mixer_weight,
    gate_bias,
    readout_weight,
    second_gain,
    up_weight,
    up_bias,
    down_weight,
    cotangent,
):
    sides = lax.axis_size("tensor")
    windows = inputs.shape[0] // sides
    half, width = inputs.shape[1:]
    channels = gate_bias.shape[0]
    units = up_bias.shape[0]
    core = lax.axis_index("tensor")
    core_at = core.reshape(1).astype(jnp.int32)

    def other_windows(array):
        return lax.dynamic_slice_in_dim(array, (1 - core) * windows, windows)

    mixer = mixer_weight.reshape(width, 2 * channels)
    mixers = (mixer, partner(mixer))
    got_inputs = partner(other_windows(inputs))
    reads = (readout_weight, partner(readout_weight))
    biases = (gate_bias[None], partner(gate_bias)[None])
    starts = (initial_state, partner(initial_state))
    got_cotangent = partner(other_windows(cotangent))
    ups = (up_weight, partner(up_weight))
    up_biases = (up_bias[None], partner(up_bias)[None])
    downs = (down_weight, partner(down_weight))
    gain, gain_two = first_gain[None], second_gain[None]

    filtered, decay, differ, cand, states, middle, normed, *orders = forward(
        core_at, inputs, got_inputs, gain, causal_filter, mixers, biases, starts, reads, gain_two
    )
    chunk = orders[0].shape[0]
    active_other, back_other, bias_other, feed_other, tangent = feed(
        core_at, cotangent, got_cotangent, orders[0], None, normed, ups[1], up_biases[1], downs[1], low
    )
    tangent, feed_other = hold(tangent, feed_other)
    feed_got = partner(feed_other)
    active_own, back_own, bias_own, feed_own = feed(
        core_at, cotangent, got_cotangent, orders[0], tangent, normed, ups[0], up_biases[0], downs[0], wide
    )
    actives = [active_own, active_other]
    feed_own, feed_got = hold(feed_own, feed_got)
    feed_sum = DpSum(feed_own, feed_got)
    up_bias_own, up_bias_other = bias_own, bias_other

    def scan(side, lead, dtype):
        return scan_back(
            windows, chunk, side, lead, filtered, reads[side], decay, differ, cand, states, dtype
        )

    back_middle, mixed, gain_two_grad = beside(
        [feed_sum],
        lambda lead: norm_back(tangent, [lead, back_other], middle, ups, gain_two),
        back_own,
    )
    gate_other, cand_other, state_other, bias_other, mixer_other = beside(
        [feed_sum], lambda lead: scan(1, lead, low), mixed
    )
    mixed, mixer_other = hold(mixed, mixer_other)
    mixer_got = partner(mixer_other)
    gate_own, cand_own, state_own, bias_own, mixer_own = beside(
        [feed_sum], lambda lead: scan(0, lead, wide), mixed
    )
    mixer_own, mixer_got = hold(mixer_own, mixer_got)
    mixer_sum = DpDirect(mixer_own, mixer_got)
    def put_back(whole_rows, got):
        return lax.dynamic_update_slice_in_dim(whole_rows, got, (1 - core) * windows, 0)

    grad_mine, grad_sent, gain_grad, taps_grad = beside(
        [feed_sum, mixer_sum],
        lambda lead: entry(
            core_at, inputs, got_inputs, orders, [lead, cand_own, gate_other, cand_other],
            back_middle, mixers, gain, causal_filter,
        ),
        gate_own,
    )
    short, sent = pack(
        width, gain_grad, taps_grad, gain_two_grad, bias_own, bias_other, up_bias_own, up_bias_other
    )

    mixer_sum.rider = short + partner(sent)

    def leave_all(lead, state_other, grad_sent):
        moved = [partner(array) for array in (state_other, grad_sent)]
        return *leave(windows, core_at, orders[1], [lead, active_other], middle, downs), *moved

    out_mine, out_sent, state_got, grad_got = beside(
        [feed_sum, mixer_sum], leave_all, active_own, state_other[:, 0], grad_sent
    )

    def exits(grad_mine, grad_got, state_own, state_got, out_sent):
        state_gradient = jnp.where(
            core == 0,
            jnp.concatenate([state_own, state_got]),
            jnp.concatenate([state_got, state_own]),
        )
        return put_back(grad_mine, grad_got), state_gradient, partner(out_sent)

    last = len(feed_sum.todo) == 1
    if last:
        feed_sum.prepare()
        feed_sum.start()
    input_gradient, state_gradient, out_got, *feed_got = beside(
        [mixer_sum],
        lambda *leads: (*exits(*leads), *(feed_sum.got if last else ())),
        grad_mine, grad_got, state_own[:, 0], state_got, out_sent,
    )
    while len(mixer_sum.todo) > 1:
        beside([mixer_sum], lambda: ())

    mixer_sum.prepare()
    (mixer_send, *feed_got) = hold(mixer_sum.sends[0], *feed_got)
    mixer_sum.sends = [mixer_send]
    mixer_sum.start()
    if last:
        feed_sum.got = list(feed_got)
    else:
        while len(feed_sum.todo) > 1:
            beside([feed_sum], lambda: ())
        feed_sum.prepare()
        feed_sum.start()
    down_sum, up_sum = finish_feed(*feed_sum.last())
    block_output = put_back(out_mine, out_got)
    mixer_sum.got = list(hold(*mixer_sum.got, down_sum, block_output)[: len(mixer_sum.got)])
    mixer_grad, read_grad, gain_sum, taps_sum, gain_two_sum, gate_bias_sum, up_bias_sum = finish_mixer(
        *mixer_sum.last(), width, causal_filter.shape[0], units
    )
    return (
        block_output,
        input_gradient,
        state_gradient,
        gain_sum[0],
        taps_sum,
        mixer_grad,
        gate_bias_sum[0],
        read_grad,
        gain_two_sum[0],
        up_sum,
        up_bias_sum[0],
        down_sum,
    )


def solution(mesh):
    return jax.shard_map(
        local,
        mesh=mesh,
        in_specs=(
            P("dp", "tensor", None),
            P("dp", "tensor"),
            P(),
            P(),
            P(None, None, "tensor"),
            P("tensor"),
            P("tensor", None),
            P(),
            P(None, "tensor"),
            P("tensor"),
            P("tensor", None),
            P("dp", "tensor", None),
        ),
        out_specs=(
            P("dp", "tensor", None),
            P("dp", "tensor", None),
            P("dp", "tensor"),
            P(),
            P(),
            P(None, None, "tensor"),
            P("tensor"),
            P("tensor", None),
            P(),
            P(None, "tensor"),
            P("tensor"),
            P("tensor", None),
        ),
        check_vma=False,
    )
```

```python
import functools
import math

import jax
import jax.numpy as jnp
from jax import lax
from jax.experimental import pallas as pl
from jax.experimental.pallas import tpu as pltpu
from jax.sharding import PartitionSpec as P

epsilon = 1e-06
low = jnp.bfloat16
wide = jnp.float32
root = math.sqrt(2.0 / math.pi)
cubic = 0.044715
MIB = 1 << 20


def mm(left, right):
    return lax.dot_general(left, right, (((1,), (0,)), ((), ())), preferred_element_type=wide)


def mm_nt(left, right):
    return lax.dot_general(left, right, (((1,), (1,)), ((), ())), preferred_element_type=wide)


def mm_tn(left, right):
    return lax.dot_general(left, right, (((0,), (0,)), ((), ())), preferred_element_type=wide)


def params(mib, grid):
    return pltpu.CompilerParams(
        vmem_limit_bytes=mib * MIB, dimension_semantics=("arbitrary",) * grid
    )


def cost(macs, moved, curves=0):
    return pl.CostEstimate(flops=2 * macs, bytes_accessed=moved, transcendentals=curves)


def whole(array):
    rank = array.ndim
    return pl.BlockSpec(array.shape, lambda *_: (0,) * rank, pipeline_mode=pl.Buffered(1))


def stream_order(rows, inverse):
    at = lax.broadcasted_iota(jnp.int32, (rows, rows), 1 if inverse else 0)
    source = lax.broadcasted_iota(jnp.int32, (rows, rows), 0 if inverse else 1)
    moved = jnp.bitwise_and(at, 7) * (rows // 8) + lax.shift_right_logical(at, 3)
    return jnp.where(source == moved, 1.0, 0.0).astype(low)


def forward_kernel(
    core, own, got, gain, taps, mixer_own, mixer_other, bias_own, bias_other, start_own, start_other,
    read_own, read_other,
    gain_two, filtered_out, decay_out, differ_out, cand_out, state_out, middle_out, normed_out,
    order, back_order, streams, rim, tail, gates, cands, carry,
):
    half_chunks = pl.num_programs(1) // 2
    step = pl.program_id(1)
    rows = own.shape[1]
    width = own.shape[2]
    count = rows // 8
    tap_count = taps.shape[0]
    edge = 8 * (tap_count - 1)
    channels = read_own.shape[0]
    mine = step // half_chunks == core[0]

    @pl.when((step == 0) & (pl.program_id(0) == 0))
    def _():
        order[...] = stream_order(rows, False)
        back_order[...] = stream_order(rows, True)

    x = mm(order[...], jnp.where(mine, own[0], got[0]))
    streams[...] = x
    scale = lax.rsqrt(jnp.mean(x * x, axis=-1, keepdims=True) + epsilon)
    normed = x * scale * gain[...]

    @pl.when(step == 0)
    def _():
        tail[...] = jnp.zeros_like(tail)
        for at, start in enumerate((start_own, start_other)):
            row = start[pl.ds(core[0] * pl.num_programs(0) + pl.program_id(0), 1), :]
            carry[:, at * channels : (at + 1) * channels] = jnp.broadcast_to(row, (8, channels))

    rim[edge:, :] = normed
    first = lax.broadcasted_iota(jnp.int32, (8, width), 0) == 0
    for at in range(0, edge, 8):
        ends = normed[rows - edge + at : rows - edge + at + 8, :]
        rim[at : at + 8, :] = jnp.where(
            first, pltpu.roll(tail[at : at + 8, :], 1, 0), pltpu.roll(ends, 1, 0)
        )
        tail[at : at + 8, :] = ends
    total = taps[0:1, :] * rim[0:rows, :]
    for tap in range(1, tap_count):
        total = total + taps[tap : tap + 1, :] * rim[8 * tap : 8 * tap + rows, :]
    filtered = total.astype(low)
    filtered_out[...] = filtered
    for at, (weight, bias) in enumerate(((mixer_own, bias_own), (mixer_other, bias_other))):
        lanes = slice(at * channels, (at + 1) * channels)
        gates[:, lanes] = mm(filtered, weight[:, :channels]) + bias[...]
        cands[:, lanes] = mm(filtered, weight[:, channels:])

    group = min(2 * channels, 1024)
    place = lax.broadcasted_iota(jnp.int32, (8, group), 0)
    for lane in range(0, 2 * channels, group):
        lanes = slice(lane, lane + group)

        def open_gates(index, state):
            factor, offset = state
            base = pl.multiple_of(index * 16, 16)
            kept = []
            for sub in (0, 8):
                c = cands[pl.ds(base + sub, 8), lanes]
                decay = jax.nn.sigmoid(-gates[pl.ds(base + sub, 8), lanes])
                soft = jnp.maximum(c, jnp.log(1.0 + jnp.exp(jnp.minimum(c, 60.0))))
                decay_out[pl.ds(base + sub, 8), lanes] = decay
                gates[pl.ds(base + sub, 8), lanes] = soft
                factor = factor * decay
                offset = soft + decay * (offset - soft)
                kept.append(c)
            cand_out[pl.ds(base, 16), lanes] = jnp.concatenate(kept, axis=0).astype(low)
            return factor, offset

        factor, offset = lax.fori_loop(
            0,
            count // 2,
            open_gates,
            (jnp.ones((8, group), wide), jnp.zeros((8, group), wide)),
            unroll=True,
        )
        for hop in (1, 2, 4):
            inside = place >= hop
            offset = factor * jnp.where(inside, pltpu.roll(offset, hop, 0), 0.0) + offset
            factor = factor * jnp.where(inside, pltpu.roll(factor, hop, 0), 1.0)
        entered = carry[:, lanes]
        leaving = factor * entered + offset
        carry[:, lanes] = jnp.broadcast_to(leaving[7:8, :], leaving.shape)
        entered = jnp.where(place >= 1, pltpu.roll(leaving, 1, 0), entered)

        def run_states(index, state):
            base = pl.multiple_of(index * 16, 16)
            held, differ = [], []
            for sub in (0, 8):
                soft = gates[pl.ds(base + sub, 8), lanes]
                differ.append(soft - state)
                state = soft - decay_out[pl.ds(base + sub, 8), lanes] * differ[-1]
                held.append(state)
            differ_out[pl.ds(base, 16), lanes] = jnp.concatenate(differ, axis=0).astype(low)
            state_out[pl.ds(base, 16), lanes] = jnp.concatenate(held, axis=0).astype(low)
            return state

        lax.fori_loop(0, count // 2, run_states, entered, unroll=True)

    mixed = mm(state_out[:, :channels], read_own[...]) + mm(
        state_out[:, channels:], read_other[...]
    )
    middle = streams[...] + mixed
    middle_out[...] = middle
    scale_two = lax.rsqrt(jnp.mean(middle * middle, axis=-1, keepdims=True) + epsilon)
    normed_out[...] = (middle * scale_two * gain_two[...]).astype(low)


def halves_specs(chunk, width, windows, halves):
    return (
        pl.BlockSpec(
            (1, chunk, width), lambda w, t, core: (windows * core[0] + w, t % halves, 0)
        ),
        pl.BlockSpec((1, chunk, width), lambda w, t, core: (w, t % halves, 0)),
    )


def forward(core, inputs, got, gain, taps, mixers, biases, starts, reads, gain_two):
    windows, half, width = got.shape
    channels = reads[0].shape[0]
    chunk = math.gcd(half, 512)
    halves = half // chunk
    steps = 2 * halves
    rows = 2 * half * windows
    row = lambda lanes: pl.BlockSpec((chunk, lanes), lambda w, t, core: (w * steps + t, 0))
    out = lambda lanes, dtype: jax.ShapeDtypeStruct((rows, lanes), dtype)
    return pl.pallas_call(
        forward_kernel,
        grid_spec=pltpu.PrefetchScalarGridSpec(
            num_scalar_prefetch=1,
            grid=(windows, steps),
            in_specs=[
                *halves_specs(chunk, width, windows, halves),
                whole(gain),
                whole(taps),
                whole(mixers[0]),
                whole(mixers[1]),
                whole(biases[0]),
                whole(biases[1]),
                whole(starts[0]),
                whole(starts[1]),
                whole(reads[0]),
                whole(reads[1]),
                whole(gain_two),
            ],
            out_specs=[
                row(width),
                row(2 * channels),
                row(2 * channels),
                row(2 * channels),
                row(2 * channels),
                row(width),
                row(width),
                pl.BlockSpec((chunk, chunk), lambda w, t, core: (0, 0)),
                pl.BlockSpec((chunk, chunk), lambda w, t, core: (0, 0)),
            ],
            scratch_shapes=[
                pltpu.VMEM((chunk, width), wide),
                pltpu.VMEM((chunk + 8 * (taps.shape[0] - 1), width), wide),
                pltpu.VMEM((8 * (taps.shape[0] - 1), width), wide),
                pltpu.VMEM((chunk, 2 * channels), wide),
                pltpu.VMEM((chunk, 2 * channels), wide),
                pltpu.VMEM((8, 2 * channels), wide),
            ],
        ),
        out_shape=[
            out(width, low),
            out(2 * channels, wide),
            out(2 * channels, low),
            out(2 * channels, low),
            out(2 * channels, low),
            out(width, wide),
            out(width, low),
            jax.ShapeDtypeStruct((chunk, chunk), low),
            jax.ShapeDtypeStruct((chunk, chunk), low),
        ],
        compiler_params=params(60, 2),
        cost_estimate=cost(rows * width * channels * 6, rows * channels * 24, rows * channels * 8),
        name="forward_mixer",
    )(core, inputs, got, gain, taps, *mixers, *biases, *starts, *reads, gain_two)


def feed(core, cotangent, got, order, tangent, normed, up, bias, down, dtype):
    windows, half, width = got.shape
    units = up.shape[1]
    rows = normed.shape[0]
    chunk = order.shape[0]
    block = min(units, 512)
    fresh = tangent is None

    def kernel(core, *refs):
        if fresh:
            own, came, order_in, *refs, tangent_in = refs
        else:
            tangent_in, *refs = refs
        normed_in, up_in, bias_in, down_in, active_out, back_out, bias_out, grad_out = refs

        if fresh:

            @pl.when(pl.program_id(0) == 0)
            def _():
                for window in range(windows):
                    for side in range(2):
                        mine = core[0] == side
                        for at in range(0, half, chunk):
                            rows_at = slice(at, at + chunk)
                            to = (2 * window + side) * half + at
                            tangent_in[to : to + chunk, :] = mm(
                                order_in[...],
                                jnp.where(mine, own[window, rows_at, :], came[window, rows_at, :]),
                            ).astype(low)

        total = jnp.zeros((8, block), wide)
        for at in range(0, rows, chunk):
            rows_at = slice(at, at + chunk)
            v = mm(normed_in[rows_at, :], up_in[...]) + bias_in[...]
            back = mm_nt(tangent_in[rows_at, :], down_in[...])
            square = v * v
            s = jax.nn.sigmoid(v * (2.0 * root + (2.0 * root * cubic) * square))
            active = v * s
            slope = s + (active * (1.0 - s)) * (2.0 * root + (6.0 * root * cubic) * square)
            back = back * slope
            for row in range(0, chunk, 8):
                total = total + back[row : row + 8, :]
            active_out[rows_at, :] = active.astype(low)
            back_out[rows_at, :] = back.astype(low)
        bias_out[...] = total
        grad_out[0:width, :] = mm_tn(tangent_in[...], active_out[...]).astype(dtype)
        grad_out[width:, :] = mm_tn(normed_in[...], back_out[...]).astype(dtype)

    lanes = lambda count: pl.BlockSpec((count, block), lambda j, core: (0, j))
    in_specs = [whole(normed), lanes(width), lanes(1), pl.BlockSpec((block, width), lambda j, core: (j, 0))]
    arrays = [normed, up, bias, down]
    out_specs = [lanes(rows), lanes(rows), lanes(8), lanes(2 * width)]
    out_shape = [
        jax.ShapeDtypeStruct((rows, units), low),
        jax.ShapeDtypeStruct((rows, units), low),
        jax.ShapeDtypeStruct((8, units), wide),
        jax.ShapeDtypeStruct((2 * width, units), dtype),
    ]
    if fresh:
        in_specs = [
            pl.BlockSpec((windows, half, width), lambda j, core: (core[0], 0, 0)),
            whole(got),
            whole(order),
        ] + in_specs
        arrays = [cotangent, got, order] + arrays
        out_specs.append(pl.BlockSpec((rows, width), lambda j, core: (0, 0)))
        out_shape.append(jax.ShapeDtypeStruct((rows, width), low))
    else:
        in_specs.insert(0, whole(tangent))
        arrays.insert(0, tangent)
    return pl.pallas_call(
        kernel,
        grid_spec=pltpu.PrefetchScalarGridSpec(
            num_scalar_prefetch=1, grid=(units // block,), in_specs=in_specs, out_specs=out_specs
        ),
        out_shape=out_shape,
        compiler_params=params(60, 1),
        cost_estimate=cost(rows * width * units * 4, rows * units * 4, rows * units),
        name="feed_forward",
    )(core, *arrays)


def norm_kernel(
    tangent, back_own, back_other, middle_in, up_own, up_other, gain_two, middle_out, mixed_out, gain_out
):
    @pl.when(pl.program_id(0) == 0)
    def _():
        gain_out[...] = jnp.zeros_like(gain_out)

    rows = tangent.shape[0]
    part = math.gcd(rows, 256)
    for begin in range(0, rows, part):
        at = slice(begin, begin + part)
        back = mm_nt(back_own[at, :], up_own[...]) + mm_nt(back_other[at, :], up_other[...])
        middle = middle_in[at, :]
        scale = lax.rsqrt(jnp.mean(middle * middle, axis=-1, keepdims=True) + epsilon)
        gain_out[...] += jnp.sum(back * (middle * scale), axis=0, keepdims=True)
        weighted = gain_two[...] * back
        inner = jnp.mean(weighted * middle, axis=-1, keepdims=True)
        back_middle = (
            tangent[at, :].astype(wide) + scale * weighted - middle * (scale * scale * scale * inner)
        )
        middle_out[at, :] = back_middle
        mixed_out[at, :] = back_middle.astype(low)


def norm_back(tangent, backs, middle, ups, gain_two):
    rows, width = tangent.shape
    units = ups[0].shape[1]
    chunk = math.gcd(rows, 512)
    row = lambda lanes: pl.BlockSpec((chunk, lanes), lambda t: (t, 0))
    return pl.pallas_call(
        norm_kernel,
        grid=(rows // chunk,),
        in_specs=[
            row(width),
            row(units),
            row(units),
            row(width),
            whole(ups[0]),
            whole(ups[1]),
            whole(gain_two),
        ],
        out_specs=[row(width), row(width), pl.BlockSpec((1, width), lambda t: (0, 0))],
        out_shape=[
            jax.ShapeDtypeStruct((rows, width), wide),
            jax.ShapeDtypeStruct((rows, width), low),
            jax.ShapeDtypeStruct((1, width), wide),
        ],
        compiler_params=params(60, 1),
        cost_estimate=cost(rows * width * 2 * units, rows * (units * 4 + width * 16)),
        name="norm_back",
    )(tangent, *backs, middle, *ups, gain_two)


def scan_kernel(
    windows, chunk, mixed, filtered, read, decay_in, differ_in, cand_in, state_in,
    gate_out, cand_out, state_out, bias_out, grad_out, states,
):
    rows, width = mixed.shape
    group = read.shape[0]
    count = chunk // 16
    chunks = rows // chunk
    each = chunks // windows
    place = lax.broadcasted_iota(jnp.int32, (8, group), 0)
    states[...] = mm_nt(mixed[...], read[...])
    factors = [jnp.ones((8, group), wide)] * chunks
    offsets = [jnp.zeros((8, group), wide)] * chunks
    for index in range(2 * count - 1, -1, -1):
        for at in range(chunks):
            here = slice(at * chunk + 8 * index, at * chunk + 8 * index + 8)
            decay = decay_in[here, :]
            factors[at] = factors[at] * decay
            offsets[at] = decay * (offsets[at] + states[here, :])
    later = [None] * chunks
    for window in range(windows):
        entered = jnp.zeros((8, group), wide)
        for at in range(window * each + each - 1, window * each - 1, -1):
            factor, offset = factors[at], offsets[at]
            for hop in (1, 2, 4):
                inside = place < 8 - hop
                offset = factor * jnp.where(inside, pltpu.roll(offset, 8 - hop, 0), 0.0) + offset
                factor = factor * jnp.where(inside, pltpu.roll(factor, 8 - hop, 0), 1.0)
            leaving = factor * entered + offset
            later[at] = jnp.where(place < 7, pltpu.roll(leaving, 7, 0), entered)
            entered = jnp.broadcast_to(leaving[0:1, :], leaving.shape)
        state_out[window] = entered[0:1, :]
    bias = [jnp.zeros((8, group), wide)] * chunks
    for index in range(count - 1, -1, -1):
        for at in range(chunks):
            base = at * chunk + 16 * index
            both = slice(base, base + 16)
            differ = differ_in[both, :].astype(wide)
            chosen = jax.nn.sigmoid(cand_in[both, :].astype(wide))
            gate, cand = [None] * 2, [None] * 2
            for half in (1, 0):
                near = slice(8 * half, 8 * half + 8)
                here = slice(base + 8 * half, base + 8 * half + 8)
                decay = decay_in[here, :]
                carried = states[here, :] + later[at]
                later[at] = decay * carried
                opened = carried - later[at]
                gate[half] = decay * opened * differ[near]
                cand[half] = opened * chosen[near]
                bias[at] = bias[at] + gate[half]
            gate_out[both, :] = jnp.concatenate(gate, axis=0).astype(low)
            cand_out[both, :] = jnp.concatenate(cand, axis=0).astype(low)
    bias_out[...] = sum(bias[1:], bias[0])
    grad_out[2 * width :, :] = mm_tn(mixed[...], state_in[...]).astype(grad_out.dtype)
    grad_out[0:width, :] = mm_tn(filtered[...], gate_out[...]).astype(grad_out.dtype)
    grad_out[width : 2 * width, :] = mm_tn(filtered[...], cand_out[...]).astype(grad_out.dtype)


def scan_back(windows, chunk, side, mixed, filtered, read, decay, differ, cand, states, dtype):
    rows, width = mixed.shape
    channels = read.shape[0]
    block = min(channels, 256)
    count = channels // block
    lanes = lambda size: pl.BlockSpec((size, block), lambda j: (0, j))
    half = pl.BlockSpec((rows, block), lambda j: (0, side * count + j))
    out = jax.ShapeDtypeStruct((rows, channels), low)
    return pl.pallas_call(
        functools.partial(scan_kernel, windows, chunk),
        grid=(count,),
        in_specs=[
            whole(mixed),
            whole(filtered),
            pl.BlockSpec((block, width), lambda j: (j, 0)),
            half,
            half,
            half,
            half,
        ],
        out_specs=[
            lanes(rows),
            lanes(rows),
            pl.BlockSpec((windows, 1, block), lambda j: (0, 0, j)),
            lanes(8),
            lanes(3 * width),
        ],
        out_shape=[
            out,
            out,
            jax.ShapeDtypeStruct((windows, 1, channels), wide),
            jax.ShapeDtypeStruct((8, channels), wide),
            jax.ShapeDtypeStruct((3 * width, channels), dtype),
        ],
        scratch_shapes=[pltpu.VMEM((rows, block), wide)],
        compiler_params=params(60, 1),
        cost_estimate=cost(rows * width * 4 * channels, rows * channels * 14, rows * channels),
        name="scan_back",
    )(mixed, filtered, read, decay, differ, cand, states)


def entry_kernel(
    core, own, got, order, back_order, gate_own, cand_own, gate_other, cand_other, middle_in, mixer_own,
    mixer_other, gain, taps, gain_two, bias_own, up_own, bias_other, up_other, mine_out, sent_out, short_out,
    rim, head, sums,
):
    step = pl.program_id(1)
    steps = pl.num_programs(1)
    half_chunks = steps // 2
    position = steps - 1 - step
    rows, width = own.shape[1:]
    tap_count = taps.shape[0]
    edge = 8 * (tap_count - 1)
    channels = gate_own.shape[1]

    @pl.when((step == 0) & (pl.program_id(0) == 0))
    def _():
        sums[...] = jnp.zeros_like(sums)

    @pl.when(step == 0)
    def _():
        head[...] = jnp.zeros_like(head)

    rim[0:rows, :] = (
        mm_nt(gate_own[...], mixer_own[:, :channels])
        + mm_nt(cand_own[...], mixer_own[:, channels:])
        + mm_nt(gate_other[...], mixer_other[:, :channels])
        + mm_nt(cand_other[...], mixer_other[:, channels:])
    )
    last = lax.broadcasted_iota(jnp.int32, (8, width), 0) == 7
    for at in range(0, edge, 8):
        begins = rim[at : at + 8, :]
        rim[rows + at : rows + at + 8, :] = jnp.where(
            last, pltpu.roll(head[at : at + 8, :], 7, 0), pltpu.roll(begins, 7, 0)
        )
        head[at : at + 8, :] = begins
    x = mm(order[...], jnp.where(position // half_chunks == core[0], own[0], got[0]))
    scale = lax.rsqrt(jnp.mean(x * x, axis=-1, keepdims=True) + epsilon)
    unit = x * scale
    back = jnp.zeros((rows, width), wide)
    for tap in range(tap_count):
        begin = 8 * (tap_count - 1 - tap)
        ahead = rim[begin : begin + rows, :]
        back = back + taps[tap : tap + 1, :] * ahead
        sums[tap : tap + 1, :] += jnp.sum(ahead * unit, axis=0, keepdims=True)
    weighted = gain[...] * back
    inner = jnp.mean(weighted * x, axis=-1, keepdims=True)
    gradient = middle_in[...] + scale * weighted - x * (scale * scale * scale * inner)
    gradient = mm(back_order[...], gradient.astype(low)).astype(low)
    give(gradient, position, half_chunks, core, mine_out, sent_out)

    @pl.when((step == steps - 1) & (pl.program_id(0) == pl.num_programs(0) - 1))
    def _():
        totals = sums[0:tap_count, :]
        parts = [jnp.sum(totals * taps[...], axis=0, keepdims=True), totals * gain[...], gain_two[...]]
        for bias in (bias_own, up_own, bias_other, up_other):
            parts.append(jnp.sum(bias[...], axis=0, keepdims=True))
        short_out[...] = jnp.zeros_like(short_out)
        row = 0
        for part in parts:
            for lane in range(0, part.shape[1], width):
                some = min(width, part.shape[1])
                short_out[row : row + part.shape[0], 0:some] = part[:, lane : lane + width]
                row += part.shape[0]


def give(values, position, half_chunks, core, mine_out, sent_out):
    rows = values.shape[0]
    at = pl.ds(pl.multiple_of(position % half_chunks * rows, rows), rows)
    mine = position // half_chunks == core[0]

    @pl.when(mine)
    def _():
        mine_out[0, at, :] = values

    @pl.when(jnp.logical_not(mine))
    def _():
        sent_out[0, at, :] = values


def side_specs(windows, half, width):
    block = (1, half, width)
    return (
        [
            pl.BlockSpec(block, lambda w, t, core: (windows * core[0] + w, 0, 0)),
            pl.BlockSpec(block, lambda w, t, core: (w, 0, 0)),
        ],
        [
            jax.ShapeDtypeStruct((2 * windows, half, width), low),
            jax.ShapeDtypeStruct((windows, half, width), low),
        ],
    )


def entry(core, inputs, got, orders, projects, back_middle, mixers, gain, taps, *shorts):
    windows, half, width = got.shape
    chunk = math.gcd(half, 512)
    halves = half // chunk
    steps = 2 * halves
    rows = 2 * half * windows
    row = lambda lanes: pl.BlockSpec(
        (chunk, lanes), lambda w, t, core: (w * steps + steps - 1 - t, 0)
    )
    specs, shapes = side_specs(windows, half, width)
    count = taps.shape[0] + 2 + sum(-(-bias.shape[1] // width) for bias in shorts[1:])
    short = (-(-count // 16) * 16, width)
    return pl.pallas_call(
        entry_kernel,
        grid_spec=pltpu.PrefetchScalarGridSpec(
            num_scalar_prefetch=1,
            grid=(windows, steps),
            in_specs=[
                pl.BlockSpec(
                    (1, chunk, width),
                    lambda w, t, core: (windows * core[0] + w, (steps - 1 - t) % halves, 0),
                ),
                pl.BlockSpec((1, chunk, width), lambda w, t, core: (w, (steps - 1 - t) % halves, 0)),
                whole(orders[0]),
                whole(orders[1]),
                *[row(array.shape[1]) for array in projects],
                row(width),
                whole(mixers[0]),
                whole(mixers[1]),
                whole(gain),
                whole(taps),
                *[whole(short) for short in shorts],
            ],
            out_specs=[*specs, pl.BlockSpec(short, lambda w, t, core: (0, 0))],
            scratch_shapes=[
                pltpu.VMEM((chunk + 8 * (taps.shape[0] - 1), width), wide),
                pltpu.VMEM((8 * (taps.shape[0] - 1), width), wide),
                pltpu.VMEM((-(-taps.shape[0] // 8) * 8, width), wide),
            ],
        ),
        out_shape=[*shapes, jax.ShapeDtypeStruct(short, wide)],
        compiler_params=params(60, 2),
        cost_estimate=cost(
            rows * width * 2 * mixers[0].shape[1], rows * mixers[0].shape[1] * 6
        ),
        name="input_gradient",
    )(core, inputs, got, *orders, *projects, back_middle, *mixers, gain, taps, *shorts)


def leave_kernel(core, back_order, active_own, active_other, middle, down_own, down_other, *refs):
    total = middle[...] + mm(active_own[...], down_own[...]) + mm(active_other[...], down_other[...])
    refs[-1][0] = mm(back_order[...], total.astype(low)).astype(low)


def leave(windows, core, back_order, actives, middle, downs, base=None):
    width = middle.shape[1]
    half = middle.shape[0] // windows // 2
    chunk = back_order.shape[0]
    steps = half // chunk
    side = lambda core: 1 - core[0] if base is None else core[0]
    row = lambda lanes: pl.BlockSpec(
        (chunk, lanes), lambda w, t, core: ((2 * w + side(core)) * steps + t, 0)
    )
    first = lambda core: 0 if base is None else windows * core[0]
    arrays = [core, back_order, *actives, middle, *downs]
    rows = windows * half
    return pl.pallas_call(
        leave_kernel,
        grid_spec=pltpu.PrefetchScalarGridSpec(
            num_scalar_prefetch=1,
            grid=(windows, steps),
            in_specs=[
                whole(back_order),
                row(actives[0].shape[1]),
                row(actives[1].shape[1]),
                row(width),
                whole(downs[0]),
                whole(downs[1]),
                *([] if base is None else [pl.BlockSpec(memory_space=pl.ANY)]),
            ],
            out_specs=pl.BlockSpec(
                (1, chunk, width), lambda w, t, core: (first(core) + w, t, 0)
            ),
        ),
        out_shape=jax.ShapeDtypeStruct((windows if base is None else 2 * windows, half, width), low),
        input_output_aliases={} if base is None else {len(arrays): 0},
        compiler_params=params(60, 2),
        cost_estimate=cost(rows * width * 2 * downs[0].shape[0], rows * downs[0].shape[0] * 6),
        name="block_output",
    )(*arrays, *([] if base is None else [base]))


def in_order(place, parts):
    for at in range(len(parts).bit_length() - 1):
        lead = place[at] == 0
        parts = [
            jnp.where(lead, parts[one], parts[one ^ (1 << at)]) for one in range(len(parts))
        ]
    return parts


def finish_feed_kernel(place, *refs):
    *shares, down_out, up_out = refs
    total = jnp.concatenate(in_order(place, [share[...].astype(wide) for share in shares]))
    width = up_out.shape[0]
    down_out[...] = total[:width].T
    up_out[...] = total[width:]


def finish_feed(place, shares):
    cut, units = shares[0].shape
    width = cut * len(shares) // 2
    block = min(units, 512)
    return pl.pallas_call(
        finish_feed_kernel,
        grid_spec=pltpu.PrefetchScalarGridSpec(
            num_scalar_prefetch=1,
            grid=(units // block,),
            in_specs=[pl.BlockSpec((cut, block), lambda j, place: (0, j))] * len(shares),
            out_specs=[
                pl.BlockSpec((block, width), lambda j, place: (j, 0)),
                pl.BlockSpec((width, block), lambda j, place: (0, j)),
            ],
        ),
        out_shape=[
            jax.ShapeDtypeStruct((units, width), wide),
            jax.ShapeDtypeStruct((width, units), wide),
        ],
        compiler_params=params(60, 1),
        name="finish_feed",
    )(place, *shares)


def finish_mixer_kernel(place, *refs):
    *shares, mixer_out, read_out, gain_out, taps_out, gain_two_out, gate_out, up_out = refs
    width = mixer_out.shape[0]
    cut = 3 * width // len(shares)
    total = jnp.concatenate(in_order(place, [share[:cut, :].astype(wide) for share in shares]))
    short = sum_alike([share[cut:, :] for share in shares])
    row = 0
    for out in (gain_out, taps_out, gain_two_out, gate_out, up_out):
        for lane in range(0, out.shape[1], width):
            some = min(width, out.shape[1])
            out[:, lane : lane + some] = short[row : row + out.shape[0], :some]
            row += out.shape[0]
    mixer_out[:, 0, :] = total[:width]
    mixer_out[:, 1, :] = total[width : 2 * width]
    read_out[...] = total[2 * width :].T


def finish_mixer(place, shares, width, taps, units):
    channels = shares[0].shape[1]
    short = [(1, width), (taps, width), (1, width), (1, channels), (1, units)]
    return pl.pallas_call(
        finish_mixer_kernel,
        grid_spec=pltpu.PrefetchScalarGridSpec(
            num_scalar_prefetch=1,
            grid=(1,),
            in_specs=[whole(share) for share in shares],
            out_specs=[
                pl.BlockSpec((width, 2, channels), lambda j, place: (0, 0, 0)),
                pl.BlockSpec((channels, width), lambda j, place: (0, 0)),
                *[pl.BlockSpec(shape, lambda j, place: (0, 0)) for shape in short],
            ],
        ),
        out_shape=[
            jax.ShapeDtypeStruct((width, 2, channels), wide),
            jax.ShapeDtypeStruct((channels, width), wide),
            *[jax.ShapeDtypeStruct(shape, wide) for shape in short],
        ],
        compiler_params=params(60, 1),
        name="finish_mixer",
    )(place, *shares)


def partner(array):
    return lax.ppermute(array, "tensor", [(0, 1), (1, 0)])


def hold(*values):
    return lax.optimization_barrier(values)


class DpSum:
    paired = True

    def __init__(self, *terms):
        self.terms = terms
        self.piece = None
        count = lax.axis_size("dp").bit_length() - 1
        first = list(range(count))
        groups = [(tuple(first[at : at + 2]),) * 2 for at in range(0, count, 2)]
        if self.paired and count >= 2:
            groups[:1] = [((0,), (1,)), ((1,), (0,))]
        self.todo = [(False, group) for group in groups] + [(True, group) for group in groups[::-1]]

    def place(self, group):
        index, core = lax.axis_index("dp"), lax.axis_index("tensor")
        return [
            jnp.where(core == 0, (index >> low_bit) & 1, (index >> high_bit) & 1)
            for low_bit, high_bit in zip(*group)
        ]

    def exchange(self, array, group, mask):
        sizes = (lax.axis_size("dp"), lax.axis_size("tensor"))
        flips = [
            sum(1 << bit for at, bit in enumerate(bits) if mask >> at & 1) for bits in group
        ]
        route = [
            (d * sizes[1] + c, (d ^ flips[c]) * sizes[1] + c)
            for d in range(sizes[0])
            for c in range(sizes[1])
        ]
        return lax.ppermute(array, ("dp", "tensor"), route)

    def prepare(self):
        join, group = self.todo[0]
        if join:
            if self.piece is None:
                self.piece = sum(term.astype(wide) for term in self.terms).astype(low)
            self.sends = [self.piece]
            return
        bits = self.place(group)
        self.spot = sum(bit << at for at, bit in enumerate(bits))
        count = 1 << len(bits)
        self.sends = [self.share(self.spot ^ mask, count).astype(low) for mask in range(1, count)]

    def share(self, spot, count):
        size = self.terms[0].shape[0] // count
        cuts = [lax.dynamic_slice_in_dim(term, spot * size, size) for term in self.terms]
        return sum(cut.astype(wide) for cut in cuts)

    def start(self):
        join, group = self.todo[0]
        count = 1 << len(group[0])
        sends = self.sends * (count - 1) if join else self.sends
        self.got = [
            self.exchange(array, group, mask) for array, mask in zip(sends, range(1, count))
        ]

    def finish(self):
        join, group = self.todo.pop(0)
        if not join:
            self.terms = [self.share(self.spot, 1 << len(group[0])), *self.got]
            return
        parts = [self.piece] + self.got
        for bit in self.place(group):
            parts = [
                jnp.where(
                    bit == 0,
                    jnp.concatenate([parts[at], parts[at + 1]]),
                    jnp.concatenate([parts[at + 1], parts[at]]),
                )
                for at in range(0, len(parts), 2)
            ]
        self.piece = parts[0]


    def last(self):
        _, group = self.todo[0]
        return jnp.stack(self.place(group)).astype(jnp.int32), [self.sends[0], *self.got]


class DpDirect(DpSum):
    paired = False
    rider = None

    def prepare(self):
        super().prepare()
        self.rides = self.rider is not None and (not self.todo[0][0] or len(self.todo) == 1)
        if self.rides:
            self.low_rider = self.rider.astype(low)
            self.sends = [jnp.concatenate([send, self.low_rider]) for send in self.sends]

    def finish(self):
        if self.rides:
            size = self.got[0].shape[0] - self.low_rider.shape[0]
            self.rider = sum_alike([self.low_rider, *(got[size:] for got in self.got)])
            self.got = [got[:size] for got in self.got]
        super().finish()


def sum_alike(parts):
    parts = [part.astype(wide) for part in parts]
    while len(parts) > 1:
        parts = [parts[at] + parts[at + 1] for at in range(0, len(parts), 2)]
    return parts[0]


def beside(chains, work, *leads, loose=()):
    chains = [chain for chain in chains if chain.todo]
    begun = [*chains, *(chain for chain in loose if chain.todo)]
    for chain in begun:
        chain.prepare()
    held = hold(*leads, *(send for chain in begun for send in chain.sends))
    leads, sends = held[: len(leads)], list(held[len(leads) :])
    for chain in begun:
        chain.sends, sends = sends[: len(chain.sends)], sends[len(chain.sends) :]
        chain.start()
    results = work(*leads)
    held = hold(*results, *(got for chain in chains for got in chain.got))
    results, gots = held[: len(results)], list(held[len(results) :])
    for chain in chains:
        chain.got, gots = gots[: len(chain.got)], gots[len(chain.got) :]
        chain.finish()
    return results


def local(
    inputs,
    initial_state,
    first_gain,
    causal_filter,
    mixer_weight,
    gate_bias,
    readout_weight,
    second_gain,
    up_weight,
    up_bias,
    down_weight,
    cotangent,
):
    sides = lax.axis_size("tensor")
    windows = inputs.shape[0] // sides
    half, width = inputs.shape[1:]
    channels = gate_bias.shape[0]
    units = up_bias.shape[0]
    core = lax.axis_index("tensor")
    core_at = core.reshape(1).astype(jnp.int32)

    def other_windows(array):
        return lax.dynamic_slice_in_dim(array, (1 - core) * windows, windows)

    mixer = mixer_weight.reshape(width, 2 * channels)
    mixers = (mixer, partner(mixer))
    got_inputs = partner(other_windows(inputs))
    reads = (readout_weight, partner(readout_weight))
    biases = (gate_bias[None], partner(gate_bias)[None])
    starts = (initial_state, partner(initial_state))
    got_cotangent = partner(other_windows(cotangent))
    ups = (up_weight, partner(up_weight))
    up_biases = (up_bias[None], partner(up_bias)[None])
    downs = (down_weight, partner(down_weight))
    gain, gain_two = first_gain[None], second_gain[None]

    filtered, decay, differ, cand, states, middle, normed, *orders = forward(
        core_at, inputs, got_inputs, gain, causal_filter, mixers, biases, starts, reads, gain_two
    )
    chunk = orders[0].shape[0]
    active_other, back_other, bias_other, feed_other, tangent = feed(
        core_at, cotangent, got_cotangent, orders[0], None, normed, ups[1], up_biases[1], downs[1], low
    )
    tangent, feed_other = hold(tangent, feed_other)
    feed_got = partner(feed_other)
    active_own, back_own, bias_own, feed_own = feed(
        core_at, cotangent, got_cotangent, orders[0], tangent, normed, ups[0], up_biases[0], downs[0], wide
    )
    actives = [active_own, active_other]
    feed_own, feed_got = hold(feed_own, feed_got)
    feed_sum = DpSum(feed_own, feed_got)
    up_bias_own, up_bias_other = bias_own, bias_other

    def scan(side, lead, dtype):
        return scan_back(
            windows, chunk, side, lead, filtered, reads[side], decay, differ, cand, states, dtype
        )

    back_middle, mixed, gain_two_grad = beside(
        [feed_sum],
        lambda lead: norm_back(tangent, [lead, back_other], middle, ups, gain_two),
        back_own,
    )
    gate_other, cand_other, state_other, bias_other, mixer_other = beside(
        [feed_sum], lambda lead: scan(1, lead, low), mixed
    )
    mixed, mixer_other = hold(mixed, mixer_other)
    mixer_got = partner(mixer_other)
    gate_own, cand_own, state_own, bias_own, mixer_own = beside(
        [feed_sum], lambda lead: scan(0, lead, wide), mixed
    )
    mixer_own, mixer_got = hold(mixer_own, mixer_got)
    mixer_sum = DpDirect(mixer_own, mixer_got)
    def put_back(whole_rows, got):
        return lax.dynamic_update_slice_in_dim(whole_rows, got, (1 - core) * windows, 0)

    grad_mine, grad_sent, short = beside(
        [feed_sum, mixer_sum],
        lambda lead: entry(
            core_at, inputs, got_inputs, orders, [lead, cand_own, gate_other, cand_other],
            back_middle, mixers, gain, causal_filter, gain_two_grad, bias_own, up_bias_own,
            bias_other, up_bias_other,
        ),
        gate_own,
    )
    mixer_sum.rider = short

    def leave_first(lead, state_other, grad_sent):
        moved = [partner(array) for array in (state_other, grad_sent)]
        return leave(windows, core_at, orders[1], [lead, active_other], middle, downs), *moved

    out_sent, state_got, grad_got = beside(
        [feed_sum, mixer_sum], leave_first, active_own, state_other[:, 0], grad_sent
    )
    common = causal_filter.shape[0] + 2
    biases_rows = 1 + units // width

    def swap(short):
        own = short[: common + biases_rows]
        other = jnp.concatenate([short[:common], short[common + biases_rows : common + 2 * biases_rows]])
        filler = jnp.zeros((short.shape[0] - common - biases_rows, width), wide)
        return jnp.concatenate([own + partner(other), filler])

    def exits(grad_mine, grad_got, state_own, state_got, out_sent):
        state_gradient = jnp.where(
            core == 0,
            jnp.concatenate([state_own, state_got]),
            jnp.concatenate([state_got, state_own]),
        )
        out_got = put_back(jnp.zeros_like(grad_mine), partner(out_sent))
        return put_back(grad_mine, grad_got), state_gradient, out_got

    last = len(feed_sum.todo) == 1
    if last:
        feed_sum.prepare()
        feed_sum.start()
    input_gradient, state_gradient, out_base, mixer_sum.rider, *feed_got = beside(
        [mixer_sum],
        lambda *leads: (*exits(*leads[:-1]), swap(leads[-1]), *(feed_sum.got if last else ())),
        grad_mine, grad_got, state_own[:, 0], state_got, out_sent, mixer_sum.rider,
    )
    while len(mixer_sum.todo) > 1:
        beside([mixer_sum], lambda: ())

    mixer_sum.prepare()
    (mixer_send, active_lead, *feed_got) = hold(mixer_sum.sends[0], active_own, *feed_got)
    mixer_sum.sends = [mixer_send]
    mixer_sum.start()
    if last:
        feed_sum.got = list(feed_got)
    else:
        while len(feed_sum.todo) > 1:
            beside([feed_sum], lambda: ())
        feed_sum.prepare()
        feed_sum.start()
    down_sum, up_sum = finish_feed(*feed_sum.last())
    block_output = leave(
        windows, core_at, orders[1], [active_lead, active_other], middle, downs, out_base
    )
    mixer_sum.got = list(hold(*mixer_sum.got, down_sum, block_output)[: len(mixer_sum.got)])
    mixer_grad, read_grad, gain_sum, taps_sum, gain_two_sum, gate_bias_sum, up_bias_sum = finish_mixer(
        *mixer_sum.last(), width, causal_filter.shape[0], units
    )
    return (
        block_output,
        input_gradient,
        state_gradient,
        gain_sum[0],
        taps_sum,
        mixer_grad,
        gate_bias_sum[0],
        read_grad,
        gain_two_sum[0],
        up_sum,
        up_bias_sum[0],
        down_sum,
    )


def solution(mesh):
    return jax.shard_map(
        local,
        mesh=mesh,
        in_specs=(
            P("dp", "tensor", None),
            P("dp", "tensor"),
            P(),
            P(),
            P(None, None, "tensor"),
            P("tensor"),
            P("tensor", None),
            P(),
            P(None, "tensor"),
            P("tensor"),
            P("tensor", None),
            P("dp", "tensor", None),
        ),
        out_specs=(
            P("dp", "tensor", None),
            P("dp", "tensor", None),
            P("dp", "tensor"),
            P(),
            P(),
            P(None, None, "tensor"),
            P("tensor"),
            P("tensor", None),
            P(),
            P(None, "tensor"),
            P("tensor"),
            P("tensor", None),
        ),
        check_vma=False,
    )
```

```python
import functools
import math

import jax
import jax.numpy as jnp
from jax import lax
from jax.experimental import pallas as pl
from jax.experimental.pallas import tpu as pltpu
from jax.sharding import PartitionSpec as P

epsilon = 1e-06
low = jnp.bfloat16
wide = jnp.float32
root = math.sqrt(2.0 / math.pi)
cubic = 0.044715
MIB = 1 << 20


def mm(left, right):
    return lax.dot_general(left, right, (((1,), (0,)), ((), ())), preferred_element_type=wide)


def mm_nt(left, right):
    return lax.dot_general(left, right, (((1,), (1,)), ((), ())), preferred_element_type=wide)


def mm_tn(left, right):
    return lax.dot_general(left, right, (((0,), (0,)), ((), ())), preferred_element_type=wide)


def params(mib, grid):
    return pltpu.CompilerParams(
        vmem_limit_bytes=mib * MIB, dimension_semantics=("arbitrary",) * grid
    )


def cost(macs, moved, curves=0):
    return pl.CostEstimate(flops=2 * macs, bytes_accessed=moved, transcendentals=curves)


def whole(array):
    rank = array.ndim
    return pl.BlockSpec(array.shape, lambda *_: (0,) * rank, pipeline_mode=pl.Buffered(1))


def stream_order(rows, inverse):
    at = lax.broadcasted_iota(jnp.int32, (rows, rows), 1 if inverse else 0)
    source = lax.broadcasted_iota(jnp.int32, (rows, rows), 0 if inverse else 1)
    moved = jnp.bitwise_and(at, 7) * (rows // 8) + lax.shift_right_logical(at, 3)
    return jnp.where(source == moved, 1.0, 0.0).astype(low)


def forward_kernel(
    core, own, got, gain, taps, mixer_own, mixer_other, bias_own, bias_other, start_own, start_other,
    read_own, read_other,
    gain_two, filtered_out, decay_out, differ_out, cand_out, state_out, middle_out, normed_out,
    order, back_order, streams, rim, tail, gates, cands, carry,
):
    half_chunks = pl.num_programs(1) // 2
    step = pl.program_id(1)
    rows = own.shape[1]
    width = own.shape[2]
    count = rows // 8
    tap_count = taps.shape[0]
    edge = 8 * (tap_count - 1)
    channels = read_own.shape[0]
    mine = step // half_chunks == core[0]

    @pl.when((step == 0) & (pl.program_id(0) == 0))
    def _():
        order[...] = stream_order(rows, False)
        back_order[...] = stream_order(rows, True)

    x = mm(order[...], jnp.where(mine, own[0], got[0]))
    streams[...] = x
    scale = lax.rsqrt(jnp.mean(x * x, axis=-1, keepdims=True) + epsilon)
    normed = x * scale * gain[...]

    @pl.when(step == 0)
    def _():
        tail[...] = jnp.zeros_like(tail)
        for at, start in enumerate((start_own, start_other)):
            row = start[pl.ds(core[0] * pl.num_programs(0) + pl.program_id(0), 1), :]
            carry[:, at * channels : (at + 1) * channels] = jnp.broadcast_to(row, (8, channels))

    rim[edge:, :] = normed
    first = lax.broadcasted_iota(jnp.int32, (8, width), 0) == 0
    for at in range(0, edge, 8):
        ends = normed[rows - edge + at : rows - edge + at + 8, :]
        rim[at : at + 8, :] = jnp.where(
            first, pltpu.roll(tail[at : at + 8, :], 1, 0), pltpu.roll(ends, 1, 0)
        )
        tail[at : at + 8, :] = ends
    total = taps[0:1, :] * rim[0:rows, :]
    for tap in range(1, tap_count):
        total = total + taps[tap : tap + 1, :] * rim[8 * tap : 8 * tap + rows, :]
    filtered = total.astype(low)
    filtered_out[...] = filtered
    for at, (weight, bias) in enumerate(((mixer_own, bias_own), (mixer_other, bias_other))):
        lanes = slice(at * channels, (at + 1) * channels)
        gates[:, lanes] = mm(filtered, weight[:, :channels]) + bias[...]
        cands[:, lanes] = mm(filtered, weight[:, channels:])

    group = min(2 * channels, 1024)
    place = lax.broadcasted_iota(jnp.int32, (8, group), 0)
    for lane in range(0, 2 * channels, group):
        lanes = slice(lane, lane + group)

        def open_gates(index, state):
            factor, offset = state
            base = pl.multiple_of(index * 16, 16)
            kept = []
            for sub in (0, 8):
                c = cands[pl.ds(base + sub, 8), lanes]
                decay = jax.nn.sigmoid(-gates[pl.ds(base + sub, 8), lanes])
                soft = jnp.maximum(c, jnp.log(1.0 + jnp.exp(jnp.minimum(c, 60.0))))
                decay_out[pl.ds(base + sub, 8), lanes] = decay
                gates[pl.ds(base + sub, 8), lanes] = soft
                factor = factor * decay
                offset = soft + decay * (offset - soft)
                kept.append(c)
            cand_out[pl.ds(base, 16), lanes] = jnp.concatenate(kept, axis=0).astype(low)
            return factor, offset

        factor, offset = lax.fori_loop(
            0,
            count // 2,
            open_gates,
            (jnp.ones((8, group), wide), jnp.zeros((8, group), wide)),
            unroll=True,
        )
        for hop in (1, 2, 4):
            inside = place >= hop
            offset = factor * jnp.where(inside, pltpu.roll(offset, hop, 0), 0.0) + offset
            factor = factor * jnp.where(inside, pltpu.roll(factor, hop, 0), 1.0)
        entered = carry[:, lanes]
        leaving = factor * entered + offset
        carry[:, lanes] = jnp.broadcast_to(leaving[7:8, :], leaving.shape)
        entered = jnp.where(place >= 1, pltpu.roll(leaving, 1, 0), entered)

        def run_states(index, state):
            base = pl.multiple_of(index * 16, 16)
            held, differ = [], []
            for sub in (0, 8):
                soft = gates[pl.ds(base + sub, 8), lanes]
                differ.append(soft - state)
                state = soft - decay_out[pl.ds(base + sub, 8), lanes] * differ[-1]
                held.append(state)
            differ_out[pl.ds(base, 16), lanes] = jnp.concatenate(differ, axis=0).astype(low)
            state_out[pl.ds(base, 16), lanes] = jnp.concatenate(held, axis=0).astype(low)
            return state

        lax.fori_loop(0, count // 2, run_states, entered, unroll=True)

    mixed = mm(state_out[:, :channels], read_own[...]) + mm(
        state_out[:, channels:], read_other[...]
    )
    middle = streams[...] + mixed
    middle_out[...] = middle
    scale_two = lax.rsqrt(jnp.mean(middle * middle, axis=-1, keepdims=True) + epsilon)
    normed_out[...] = (middle * scale_two * gain_two[...]).astype(low)


def halves_specs(chunk, width, windows, halves):
    return (
        pl.BlockSpec(
            (1, chunk, width), lambda w, t, core: (windows * core[0] + w, t % halves, 0)
        ),
        pl.BlockSpec((1, chunk, width), lambda w, t, core: (w, t % halves, 0)),
    )


def forward(core, inputs, got, gain, taps, mixers, biases, starts, reads, gain_two):
    windows, half, width = got.shape
    channels = reads[0].shape[0]
    chunk = math.gcd(half, 512)
    halves = half // chunk
    steps = 2 * halves
    rows = 2 * half * windows
    row = lambda lanes: pl.BlockSpec((chunk, lanes), lambda w, t, core: (w * steps + t, 0))
    out = lambda lanes, dtype: jax.ShapeDtypeStruct((rows, lanes), dtype)
    return pl.pallas_call(
        forward_kernel,
        grid_spec=pltpu.PrefetchScalarGridSpec(
            num_scalar_prefetch=1,
            grid=(windows, steps),
            in_specs=[
                *halves_specs(chunk, width, windows, halves),
                whole(gain),
                whole(taps),
                whole(mixers[0]),
                whole(mixers[1]),
                whole(biases[0]),
                whole(biases[1]),
                whole(starts[0]),
                whole(starts[1]),
                whole(reads[0]),
                whole(reads[1]),
                whole(gain_two),
            ],
            out_specs=[
                row(width),
                row(2 * channels),
                row(2 * channels),
                row(2 * channels),
                row(2 * channels),
                row(width),
                row(width),
                pl.BlockSpec((chunk, chunk), lambda w, t, core: (0, 0)),
                pl.BlockSpec((chunk, chunk), lambda w, t, core: (0, 0)),
            ],
            scratch_shapes=[
                pltpu.VMEM((chunk, width), wide),
                pltpu.VMEM((chunk + 8 * (taps.shape[0] - 1), width), wide),
                pltpu.VMEM((8 * (taps.shape[0] - 1), width), wide),
                pltpu.VMEM((chunk, 2 * channels), wide),
                pltpu.VMEM((chunk, 2 * channels), wide),
                pltpu.VMEM((8, 2 * channels), wide),
            ],
        ),
        out_shape=[
            out(width, low),
            out(2 * channels, wide),
            out(2 * channels, low),
            out(2 * channels, low),
            out(2 * channels, low),
            out(width, wide),
            out(width, low),
            jax.ShapeDtypeStruct((chunk, chunk), low),
            jax.ShapeDtypeStruct((chunk, chunk), low),
        ],
        compiler_params=params(60, 2),
        cost_estimate=cost(rows * width * channels * 6, rows * channels * 24, rows * channels * 8),
        name="forward_mixer",
    )(core, inputs, got, gain, taps, *mixers, *biases, *starts, *reads, gain_two)


def feed(core, cotangent, got, order, tangent, normed, up, bias, down, dtype):
    windows, half, width = got.shape
    units = up.shape[1]
    rows = normed.shape[0]
    chunk = order.shape[0]
    block = min(units, 512)
    fresh = tangent is None

    def kernel(core, *refs):
        if fresh:
            own, came, order_in, *refs, tangent_in = refs
        else:
            tangent_in, *refs = refs
        normed_in, up_in, bias_in, down_in, active_out, back_out, bias_out, grad_out = refs

        if fresh:

            @pl.when(pl.program_id(0) == 0)
            def _():
                for window in range(windows):
                    for side in range(2):
                        mine = core[0] == side
                        for at in range(0, half, chunk):
                            rows_at = slice(at, at + chunk)
                            to = (2 * window + side) * half + at
                            tangent_in[to : to + chunk, :] = mm(
                                order_in[...],
                                jnp.where(mine, own[window, rows_at, :], came[window, rows_at, :]),
                            ).astype(low)

        total = jnp.zeros((8, block), wide)
        for at in range(0, rows, chunk):
            rows_at = slice(at, at + chunk)
            v = mm(normed_in[rows_at, :], up_in[...]) + bias_in[...]
            back = mm_nt(tangent_in[rows_at, :], down_in[...])
            square = v * v
            s = jax.nn.sigmoid(v * (2.0 * root + (2.0 * root * cubic) * square))
            active = v * s
            slope = s + (active * (1.0 - s)) * (2.0 * root + (6.0 * root * cubic) * square)
            back = back * slope
            for row in range(0, chunk, 8):
                total = total + back[row : row + 8, :]
            active_out[rows_at, :] = active.astype(low)
            back_out[rows_at, :] = back.astype(low)
        bias_out[...] = total
        grad_out[0:width, :] = mm_tn(tangent_in[...], active_out[...]).astype(dtype)
        grad_out[width:, :] = mm_tn(normed_in[...], back_out[...]).astype(dtype)

    lanes = lambda count: pl.BlockSpec((count, block), lambda j, core: (0, j))
    in_specs = [whole(normed), lanes(width), lanes(1), pl.BlockSpec((block, width), lambda j, core: (j, 0))]
    arrays = [normed, up, bias, down]
    out_specs = [lanes(rows), lanes(rows), lanes(8), lanes(2 * width)]
    out_shape = [
        jax.ShapeDtypeStruct((rows, units), low),
        jax.ShapeDtypeStruct((rows, units), low),
        jax.ShapeDtypeStruct((8, units), wide),
        jax.ShapeDtypeStruct((2 * width, units), dtype),
    ]
    if fresh:
        in_specs = [
            pl.BlockSpec((windows, half, width), lambda j, core: (core[0], 0, 0)),
            whole(got),
            whole(order),
        ] + in_specs
        arrays = [cotangent, got, order] + arrays
        out_specs.append(pl.BlockSpec((rows, width), lambda j, core: (0, 0)))
        out_shape.append(jax.ShapeDtypeStruct((rows, width), low))
    else:
        in_specs.insert(0, whole(tangent))
        arrays.insert(0, tangent)
    return pl.pallas_call(
        kernel,
        grid_spec=pltpu.PrefetchScalarGridSpec(
            num_scalar_prefetch=1, grid=(units // block,), in_specs=in_specs, out_specs=out_specs
        ),
        out_shape=out_shape,
        compiler_params=params(60, 1),
        cost_estimate=cost(rows * width * units * 4, rows * units * 4, rows * units),
        name="feed_forward",
    )(core, *arrays)


def norm_kernel(
    tangent, back_own, back_other, middle_in, up_own, up_other, gain_two, middle_out, mixed_out, gain_out
):
    @pl.when(pl.program_id(0) == 0)
    def _():
        gain_out[...] = jnp.zeros_like(gain_out)

    rows = tangent.shape[0]
    part = math.gcd(rows, 256)
    for begin in range(0, rows, part):
        at = slice(begin, begin + part)
        back = mm_nt(back_own[at, :], up_own[...]) + mm_nt(back_other[at, :], up_other[...])
        middle = middle_in[at, :]
        scale = lax.rsqrt(jnp.mean(middle * middle, axis=-1, keepdims=True) + epsilon)
        gain_out[...] += jnp.sum(back * (middle * scale), axis=0, keepdims=True)
        weighted = gain_two[...] * back
        inner = jnp.mean(weighted * middle, axis=-1, keepdims=True)
        back_middle = (
            tangent[at, :].astype(wide) + scale * weighted - middle * (scale * scale * scale * inner)
        )
        middle_out[at, :] = back_middle
        mixed_out[at, :] = back_middle.astype(low)


def norm_back(tangent, backs, middle, ups, gain_two):
    rows, width = tangent.shape
    units = ups[0].shape[1]
    chunk = math.gcd(rows, 512)
    row = lambda lanes: pl.BlockSpec((chunk, lanes), lambda t: (t, 0))
    return pl.pallas_call(
        norm_kernel,
        grid=(rows // chunk,),
        in_specs=[
            row(width),
            row(units),
            row(units),
            row(width),
            whole(ups[0]),
            whole(ups[1]),
            whole(gain_two),
        ],
        out_specs=[row(width), row(width), pl.BlockSpec((1, width), lambda t: (0, 0))],
        out_shape=[
            jax.ShapeDtypeStruct((rows, width), wide),
            jax.ShapeDtypeStruct((rows, width), low),
            jax.ShapeDtypeStruct((1, width), wide),
        ],
        compiler_params=params(60, 1),
        cost_estimate=cost(rows * width * 2 * units, rows * (units * 4 + width * 16)),
        name="norm_back",
    )(tangent, *backs, middle, *ups, gain_two)


def scan_kernel(
    windows, chunk, mixed, filtered, read, decay_in, differ_in, cand_in, state_in,
    gate_out, cand_out, state_out, bias_out, grad_out, states,
):
    rows, width = mixed.shape
    group = read.shape[0]
    count = chunk // 16
    chunks = rows // chunk
    each = chunks // windows
    place = lax.broadcasted_iota(jnp.int32, (8, group), 0)
    states[...] = mm_nt(mixed[...], read[...])
    factors = [jnp.ones((8, group), wide)] * chunks
    offsets = [jnp.zeros((8, group), wide)] * chunks
    for index in range(2 * count - 1, -1, -1):
        for at in range(chunks):
            here = slice(at * chunk + 8 * index, at * chunk + 8 * index + 8)
            decay = decay_in[here, :]
            factors[at] = factors[at] * decay
            offsets[at] = decay * (offsets[at] + states[here, :])
    later = [None] * chunks
    for window in range(windows):
        entered = jnp.zeros((8, group), wide)
        for at in range(window * each + each - 1, window * each - 1, -1):
            factor, offset = factors[at], offsets[at]
            for hop in (1, 2, 4):
                inside = place < 8 - hop
                offset = factor * jnp.where(inside, pltpu.roll(offset, 8 - hop, 0), 0.0) + offset
                factor = factor * jnp.where(inside, pltpu.roll(factor, 8 - hop, 0), 1.0)
            leaving = factor * entered + offset
            later[at] = jnp.where(place < 7, pltpu.roll(leaving, 7, 0), entered)
            entered = jnp.broadcast_to(leaving[0:1, :], leaving.shape)
        state_out[window] = entered[0:1, :]
    bias = [jnp.zeros((8, group), wide)] * chunks
    for index in range(count - 1, -1, -1):
        for at in range(chunks):
            base = at * chunk + 16 * index
            both = slice(base, base + 16)
            differ = differ_in[both, :].astype(wide)
            chosen = jax.nn.sigmoid(cand_in[both, :].astype(wide))
            gate, cand = [None] * 2, [None] * 2
            for half in (1, 0):
                near = slice(8 * half, 8 * half + 8)
                here = slice(base + 8 * half, base + 8 * half + 8)
                decay = decay_in[here, :]
                carried = states[here, :] + later[at]
                later[at] = decay * carried
                opened = carried - later[at]
                gate[half] = decay * opened * differ[near]
                cand[half] = opened * chosen[near]
                bias[at] = bias[at] + gate[half]
            gate_out[both, :] = jnp.concatenate(gate, axis=0).astype(low)
            cand_out[both, :] = jnp.concatenate(cand, axis=0).astype(low)
    bias_out[...] = sum(bias[1:], bias[0])
    grad_out[2 * width :, :] = mm_tn(mixed[...], state_in[...]).astype(grad_out.dtype)
    grad_out[0:width, :] = mm_tn(filtered[...], gate_out[...]).astype(grad_out.dtype)
    grad_out[width : 2 * width, :] = mm_tn(filtered[...], cand_out[...]).astype(grad_out.dtype)


def scan_back(windows, chunk, side, mixed, filtered, read, decay, differ, cand, states, dtype):
    rows, width = mixed.shape
    channels = read.shape[0]
    block = min(channels, 256)
    count = channels // block
    lanes = lambda size: pl.BlockSpec((size, block), lambda j: (0, j))
    half = pl.BlockSpec((rows, block), lambda j: (0, side * count + j))
    out = jax.ShapeDtypeStruct((rows, channels), low)
    return pl.pallas_call(
        functools.partial(scan_kernel, windows, chunk),
        grid=(count,),
        in_specs=[
            whole(mixed),
            whole(filtered),
            pl.BlockSpec((block, width), lambda j: (j, 0)),
            half,
            half,
            half,
            half,
        ],
        out_specs=[
            lanes(rows),
            lanes(rows),
            pl.BlockSpec((windows, 1, block), lambda j: (0, 0, j)),
            lanes(8),
            lanes(3 * width),
        ],
        out_shape=[
            out,
            out,
            jax.ShapeDtypeStruct((windows, 1, channels), wide),
            jax.ShapeDtypeStruct((8, channels), wide),
            jax.ShapeDtypeStruct((3 * width, channels), dtype),
        ],
        scratch_shapes=[pltpu.VMEM((rows, block), wide)],
        compiler_params=params(60, 1),
        cost_estimate=cost(rows * width * 4 * channels, rows * channels * 14, rows * channels),
        name="scan_back",
    )(mixed, filtered, read, decay, differ, cand, states)


def entry_kernel(
    core, own, got, order, back_order, gate_own, cand_own, gate_other, cand_other, middle_in, mixer_own,
    mixer_other, gain, taps, gain_two, bias_own, up_own, bias_other, up_other, mine_out, sent_out, short_out,
    rim, head, sums, packed,
):
    step = pl.program_id(1)
    steps = pl.num_programs(1)
    half_chunks = steps // 2
    position = steps - 1 - step
    rows, width = own.shape[1:]
    tap_count = taps.shape[0]
    edge = 8 * (tap_count - 1)
    channels = gate_own.shape[1]

    @pl.when((step == 0) & (pl.program_id(0) == 0))
    def _():
        sums[...] = jnp.zeros_like(sums)

    @pl.when(step == 0)
    def _():
        head[...] = jnp.zeros_like(head)

    rim[0:rows, :] = (
        mm_nt(gate_own[...], mixer_own[:, :channels])
        + mm_nt(cand_own[...], mixer_own[:, channels:])
        + mm_nt(gate_other[...], mixer_other[:, :channels])
        + mm_nt(cand_other[...], mixer_other[:, channels:])
    )
    last = lax.broadcasted_iota(jnp.int32, (8, width), 0) == 7
    for at in range(0, edge, 8):
        begins = rim[at : at + 8, :]
        rim[rows + at : rows + at + 8, :] = jnp.where(
            last, pltpu.roll(head[at : at + 8, :], 7, 0), pltpu.roll(begins, 7, 0)
        )
        head[at : at + 8, :] = begins
    x = mm(order[...], jnp.where(position // half_chunks == core[0], own[0], got[0]))
    scale = lax.rsqrt(jnp.mean(x * x, axis=-1, keepdims=True) + epsilon)
    unit = x * scale
    back = jnp.zeros((rows, width), wide)
    for tap in range(tap_count):
        begin = 8 * (tap_count - 1 - tap)
        ahead = rim[begin : begin + rows, :]
        back = back + taps[tap : tap + 1, :] * ahead
        sums[tap : tap + 1, :] += jnp.sum(ahead * unit, axis=0, keepdims=True)
    weighted = gain[...] * back
    inner = jnp.mean(weighted * x, axis=-1, keepdims=True)
    gradient = middle_in[...] + scale * weighted - x * (scale * scale * scale * inner)
    gradient = mm(back_order[...], gradient.astype(low)).astype(low)
    give(gradient, position, half_chunks, core, mine_out, sent_out)

    @pl.when((step == steps - 1) & (pl.program_id(0) == pl.num_programs(0) - 1))
    def _():
        totals = sums[0:tap_count, :]
        parts = [jnp.sum(totals * taps[...], axis=0, keepdims=True), totals * gain[...], gain_two[...]]
        for bias in (bias_own, up_own, bias_other, up_other):
            parts.append(jnp.sum(bias[...], axis=0, keepdims=True))
        packed[...] = jnp.zeros_like(packed)
        row = 0
        for part in parts:
            for lane in range(0, part.shape[1], width):
                some = min(width, part.shape[1])
                packed[row : row + part.shape[0], 0:some] = part[:, lane : lane + width]
                row += part.shape[0]
        short_out[...] = packed[...].astype(low)


def give(values, position, half_chunks, core, mine_out, sent_out):
    rows = values.shape[0]
    at = pl.ds(pl.multiple_of(position % half_chunks * rows, rows), rows)
    mine = position // half_chunks == core[0]

    @pl.when(mine)
    def _():
        mine_out[0, at, :] = values

    @pl.when(jnp.logical_not(mine))
    def _():
        sent_out[0, at, :] = values


def side_specs(windows, half, width):
    block = (1, half, width)
    return (
        [
            pl.BlockSpec(block, lambda w, t, core: (windows * core[0] + w, 0, 0)),
            pl.BlockSpec(block, lambda w, t, core: (w, 0, 0)),
        ],
        [
            jax.ShapeDtypeStruct((2 * windows, half, width), low),
            jax.ShapeDtypeStruct((windows, half, width), low),
        ],
    )


def entry(core, inputs, got, orders, projects, back_middle, mixers, gain, taps, *shorts):
    windows, half, width = got.shape
    chunk = math.gcd(half, 512)
    halves = half // chunk
    steps = 2 * halves
    rows = 2 * half * windows
    row = lambda lanes: pl.BlockSpec(
        (chunk, lanes), lambda w, t, core: (w * steps + steps - 1 - t, 0)
    )
    specs, shapes = side_specs(windows, half, width)
    count = taps.shape[0] + 2 + sum(-(-bias.shape[1] // width) for bias in shorts[1:])
    short = (-(-count // 16) * 16, width)
    return pl.pallas_call(
        entry_kernel,
        grid_spec=pltpu.PrefetchScalarGridSpec(
            num_scalar_prefetch=1,
            grid=(windows, steps),
            in_specs=[
                pl.BlockSpec(
                    (1, chunk, width),
                    lambda w, t, core: (windows * core[0] + w, (steps - 1 - t) % halves, 0),
                ),
                pl.BlockSpec((1, chunk, width), lambda w, t, core: (w, (steps - 1 - t) % halves, 0)),
                whole(orders[0]),
                whole(orders[1]),
                *[row(array.shape[1]) for array in projects],
                row(width),
                whole(mixers[0]),
                whole(mixers[1]),
                whole(gain),
                whole(taps),
                *[whole(short) for short in shorts],
            ],
            out_specs=[*specs, pl.BlockSpec(short, lambda w, t, core: (0, 0))],
            scratch_shapes=[
                pltpu.VMEM((chunk + 8 * (taps.shape[0] - 1), width), wide),
                pltpu.VMEM((8 * (taps.shape[0] - 1), width), wide),
                pltpu.VMEM((-(-taps.shape[0] // 8) * 8, width), wide),
                pltpu.VMEM(short, wide),
            ],
        ),
        out_shape=[*shapes, jax.ShapeDtypeStruct(short, low)],
        compiler_params=params(60, 2),
        cost_estimate=cost(
            rows * width * 2 * mixers[0].shape[1], rows * mixers[0].shape[1] * 6
        ),
        name="input_gradient",
    )(core, inputs, got, *orders, *projects, back_middle, *mixers, gain, taps, *shorts)


def leave_kernel(core, back_order, active_own, active_other, middle, down_own, down_other, *refs):
    total = middle[...] + mm(active_own[...], down_own[...]) + mm(active_other[...], down_other[...])
    refs[-1][0] = mm(back_order[...], total.astype(low)).astype(low)


def leave(windows, core, back_order, actives, middle, downs, base=None):
    width = middle.shape[1]
    half = middle.shape[0] // windows // 2
    chunk = back_order.shape[0]
    steps = half // chunk
    side = lambda core: 1 - core[0] if base is None else core[0]
    row = lambda lanes: pl.BlockSpec(
        (chunk, lanes), lambda w, t, core: ((2 * w + side(core)) * steps + t, 0)
    )
    first = lambda core: 0 if base is None else windows * core[0]
    arrays = [core, back_order, *actives, middle, *downs]
    rows = windows * half
    return pl.pallas_call(
        leave_kernel,
        grid_spec=pltpu.PrefetchScalarGridSpec(
            num_scalar_prefetch=1,
            grid=(windows, steps),
            in_specs=[
                whole(back_order),
                row(actives[0].shape[1]),
                row(actives[1].shape[1]),
                row(width),
                whole(downs[0]),
                whole(downs[1]),
                *([] if base is None else [pl.BlockSpec(memory_space=pl.ANY)]),
            ],
            out_specs=pl.BlockSpec(
                (1, chunk, width), lambda w, t, core: (first(core) + w, t, 0)
            ),
        ),
        out_shape=jax.ShapeDtypeStruct((windows if base is None else 2 * windows, half, width), low),
        input_output_aliases={} if base is None else {len(arrays): 0},
        compiler_params=params(60, 2),
        cost_estimate=cost(rows * width * 2 * downs[0].shape[0], rows * downs[0].shape[0] * 6),
        name="block_output",
    )(*arrays, *([] if base is None else [base]))


def in_order(place, parts):
    for at in range(len(parts).bit_length() - 1):
        lead = place[at] == 0
        parts = [
            jnp.where(lead, parts[one], parts[one ^ (1 << at)]) for one in range(len(parts))
        ]
    return parts


def finish_feed_kernel(place, *refs):
    *shares, down_out, up_out = refs
    total = jnp.concatenate(in_order(place, [share[...].astype(wide) for share in shares]))
    width = up_out.shape[0]
    down_out[...] = total[:width].T
    up_out[...] = total[width:]


def finish_feed(place, shares):
    cut, units = shares[0].shape
    width = cut * len(shares) // 2
    block = min(units, 512)
    return pl.pallas_call(
        finish_feed_kernel,
        grid_spec=pltpu.PrefetchScalarGridSpec(
            num_scalar_prefetch=1,
            grid=(units // block,),
            in_specs=[pl.BlockSpec((cut, block), lambda j, place: (0, j))] * len(shares),
            out_specs=[
                pl.BlockSpec((block, width), lambda j, place: (j, 0)),
                pl.BlockSpec((width, block), lambda j, place: (0, j)),
            ],
        ),
        out_shape=[
            jax.ShapeDtypeStruct((units, width), wide),
            jax.ShapeDtypeStruct((width, units), wide),
        ],
        compiler_params=params(60, 1),
        name="finish_feed",
    )(place, *shares)


def finish_mixer_kernel(place, *refs):
    *shares, mixer_out, read_out, gain_out, taps_out, gain_two_out, gate_out, up_out = refs
    width = mixer_out.shape[0]
    cut = 3 * width // len(shares)
    total = jnp.concatenate(in_order(place, [share[:cut, :].astype(wide) for share in shares]))
    short = sum_alike([share[cut:, :] for share in shares])
    row = 0
    for out in (gain_out, taps_out, gain_two_out, gate_out, up_out):
        for lane in range(0, out.shape[1], width):
            some = min(width, out.shape[1])
            out[:, lane : lane + some] = short[row : row + out.shape[0], :some]
            row += out.shape[0]
    mixer_out[:, 0, :] = total[:width]
    mixer_out[:, 1, :] = total[width : 2 * width]
    read_out[...] = total[2 * width :].T


def finish_mixer(place, shares, width, taps, units):
    channels = shares[0].shape[1]
    short = [(1, width), (taps, width), (1, width), (1, channels), (1, units)]
    return pl.pallas_call(
        finish_mixer_kernel,
        grid_spec=pltpu.PrefetchScalarGridSpec(
            num_scalar_prefetch=1,
            grid=(1,),
            in_specs=[whole(share) for share in shares],
            out_specs=[
                pl.BlockSpec((width, 2, channels), lambda j, place: (0, 0, 0)),
                pl.BlockSpec((channels, width), lambda j, place: (0, 0)),
                *[pl.BlockSpec(shape, lambda j, place: (0, 0)) for shape in short],
            ],
        ),
        out_shape=[
            jax.ShapeDtypeStruct((width, 2, channels), wide),
            jax.ShapeDtypeStruct((channels, width), wide),
            *[jax.ShapeDtypeStruct(shape, wide) for shape in short],
        ],
        compiler_params=params(60, 1),
        name="finish_mixer",
    )(place, *shares)


def partner(array):
    return lax.ppermute(array, "tensor", [(0, 1), (1, 0)])


def hold(*values):
    return lax.optimization_barrier(values)


class DpSum:
    paired = True

    def __init__(self, *terms):
        self.terms = terms
        self.piece = None
        count = lax.axis_size("dp").bit_length() - 1
        first = list(range(count))
        groups = [(tuple(first[at : at + 2]),) * 2 for at in range(0, count, 2)]
        if self.paired and count >= 2:
            groups[:1] = [((0,), (1,)), ((1,), (0,))]
        self.todo = [(False, group) for group in groups] + [(True, group) for group in groups[::-1]]

    def place(self, group):
        index, core = lax.axis_index("dp"), lax.axis_index("tensor")
        return [
            jnp.where(core == 0, (index >> low_bit) & 1, (index >> high_bit) & 1)
            for low_bit, high_bit in zip(*group)
        ]

    def exchange(self, array, group, mask):
        sizes = (lax.axis_size("dp"), lax.axis_size("tensor"))
        flips = [
            sum(1 << bit for at, bit in enumerate(bits) if mask >> at & 1) for bits in group
        ]
        route = [
            (d * sizes[1] + c, (d ^ flips[c]) * sizes[1] + c)
            for d in range(sizes[0])
            for c in range(sizes[1])
        ]
        return lax.ppermute(array, ("dp", "tensor"), route)

    def prepare(self):
        join, group = self.todo[0]
        if join:
            if self.piece is None:
                self.piece = sum(term.astype(wide) for term in self.terms).astype(low)
            self.sends = [self.piece]
            return
        bits = self.place(group)
        self.spot = sum(bit << at for at, bit in enumerate(bits))
        count = 1 << len(bits)
        self.sends = [self.share(self.spot ^ mask, count).astype(low) for mask in range(1, count)]

    def cuts(self, spot, count):
        size = self.terms[0].shape[0] // count
        return [lax.dynamic_slice_in_dim(term, spot * size, size) for term in self.terms]

    def share(self, spot, count):
        return sum(cut.astype(wide) for cut in self.cuts(spot, count))

    def start(self):
        join, group = self.todo[0]
        count = 1 << len(group[0])
        sends = self.sends * (count - 1) if join else self.sends
        self.got = [
            self.exchange(array, group, mask) for array, mask in zip(sends, range(1, count))
        ]

    def finish(self):
        join, group = self.todo.pop(0)
        if not join:
            count = 1 << len(group[0])
            if self.paired and len(self.terms) == 2:
                self.terms = [*self.cuts(self.spot, count), *self.got]
            else:
                self.terms = [self.share(self.spot, count), *self.got]
            return
        parts = [self.piece] + self.got
        for bit in self.place(group):
            parts = [
                jnp.where(
                    bit == 0,
                    jnp.concatenate([parts[at], parts[at + 1]]),
                    jnp.concatenate([parts[at + 1], parts[at]]),
                )
                for at in range(0, len(parts), 2)
            ]
        self.piece = parts[0]


    def last(self):
        _, group = self.todo[0]
        return jnp.stack(self.place(group)).astype(jnp.int32), [self.sends[0], *self.got]


class DpDirect(DpSum):
    paired = False
    rider = None

    def prepare(self):
        super().prepare()
        self.rides = self.rider is not None and (not self.todo[0][0] or len(self.todo) == 1)
        if self.rides:
            self.low_rider = self.rider.astype(low)
            self.sends = [jnp.concatenate([send, self.low_rider]) for send in self.sends]

    def finish(self):
        if self.rides:
            size = self.got[0].shape[0] - self.low_rider.shape[0]
            self.rider = sum_alike([self.low_rider, *(got[size:] for got in self.got)])
            self.got = [got[:size] for got in self.got]
        super().finish()


def sum_alike(parts):
    parts = [part.astype(wide) for part in parts]
    while len(parts) > 1:
        parts = [parts[at] + parts[at + 1] for at in range(0, len(parts), 2)]
    return parts[0]


def beside(chains, work, *leads):
    chains = [chain for chain in chains if chain.todo]
    for chain in chains:
        chain.prepare()
    held = hold(*leads, *(send for chain in chains for send in chain.sends))
    leads, sends = held[: len(leads)], list(held[len(leads) :])
    for chain in chains:
        chain.sends, sends = sends[: len(chain.sends)], sends[len(chain.sends) :]
        chain.start()
    results = work(*leads)
    held = hold(*results, *(got for chain in chains for got in chain.got))
    results, gots = held[: len(results)], list(held[len(results) :])
    for chain in chains:
        chain.got, gots = gots[: len(chain.got)], gots[len(chain.got) :]
        chain.finish()
    return results


def local(
    inputs,
    initial_state,
    first_gain,
    causal_filter,
    mixer_weight,
    gate_bias,
    readout_weight,
    second_gain,
    up_weight,
    up_bias,
    down_weight,
    cotangent,
):
    sides = lax.axis_size("tensor")
    windows = inputs.shape[0] // sides
    half, width = inputs.shape[1:]
    channels = gate_bias.shape[0]
    units = up_bias.shape[0]
    core = lax.axis_index("tensor")
    core_at = core.reshape(1).astype(jnp.int32)

    def other_windows(array):
        return lax.dynamic_slice_in_dim(array, (1 - core) * windows, windows)

    mixer = mixer_weight.reshape(width, 2 * channels)
    mixers = (mixer, partner(mixer))
    got_inputs = partner(other_windows(inputs))
    reads = (readout_weight, partner(readout_weight))
    biases = (gate_bias[None], partner(gate_bias)[None])
    starts = (initial_state, partner(initial_state))
    got_cotangent = partner(other_windows(cotangent))
    ups = (up_weight, partner(up_weight))
    up_biases = (up_bias[None], partner(up_bias)[None])
    downs = (down_weight, partner(down_weight))
    gain, gain_two = first_gain[None], second_gain[None]

    filtered, decay, differ, cand, states, middle, normed, *orders = forward(
        core_at, inputs, got_inputs, gain, causal_filter, mixers, biases, starts, reads, gain_two
    )
    chunk = orders[0].shape[0]
    active_other, back_other, bias_other, feed_other, tangent = feed(
        core_at, cotangent, got_cotangent, orders[0], None, normed, ups[1], up_biases[1], downs[1], low
    )
    tangent, feed_other = hold(tangent, feed_other)
    feed_got = partner(feed_other)
    active_own, back_own, bias_own, feed_own = feed(
        core_at, cotangent, got_cotangent, orders[0], tangent, normed, ups[0], up_biases[0], downs[0], wide
    )
    actives = [active_own, active_other]
    feed_own, feed_got = hold(feed_own, feed_got)
    feed_sum = DpSum(feed_own, feed_got)
    up_bias_own, up_bias_other = bias_own, bias_other

    def scan(side, lead, dtype):
        return scan_back(
            windows, chunk, side, lead, filtered, reads[side], decay, differ, cand, states, dtype
        )

    back_middle, mixed, gain_two_grad = beside(
        [feed_sum],
        lambda lead: norm_back(tangent, [lead, back_other], middle, ups, gain_two),
        back_own,
    )
    gate_other, cand_other, state_other, bias_other, mixer_other = beside(
        [feed_sum], lambda lead: scan(1, lead, low), mixed
    )
    mixed, mixer_other = hold(mixed, mixer_other)
    mixer_got = partner(mixer_other)
    gate_own, cand_own, state_own, bias_own, mixer_own = beside(
        [feed_sum], lambda lead: scan(0, lead, wide), mixed
    )
    mixer_own, mixer_got = hold(mixer_own, mixer_got)
    mixer_sum = DpDirect(mixer_own, mixer_got)
    def put_back(whole_rows, got):
        return lax.dynamic_update_slice_in_dim(whole_rows, got, (1 - core) * windows, 0)

    grad_mine, grad_sent, short = beside(
        [feed_sum, mixer_sum],
        lambda lead: entry(
            core_at, inputs, got_inputs, orders, [lead, cand_own, gate_other, cand_other],
            back_middle, mixers, gain, causal_filter, gain_two_grad, bias_own, up_bias_own,
            bias_other, up_bias_other,
        ),
        gate_own,
    )
    mixer_sum.rider = short

    def leave_first(lead, state_other, grad_sent):
        moved = [partner(array) for array in (state_other, grad_sent)]
        return leave(windows, core_at, orders[1], [lead, active_other], middle, downs), *moved

    out_sent, state_got, grad_got = beside(
        [feed_sum, mixer_sum], leave_first, active_own, state_other[:, 0], grad_sent
    )
    common = causal_filter.shape[0] + 2
    biases_rows = 1 + units // width

    def swap(short):
        own = short[: common + biases_rows]
        other = jnp.concatenate([short[:common], short[common + biases_rows : common + 2 * biases_rows]])
        filler = jnp.zeros((short.shape[0] - common - biases_rows, width), wide)
        return jnp.concatenate([own + partner(other), filler])

    def exits(grad_mine, grad_got, state_own, state_got, out_sent):
        state_gradient = jnp.where(
            core == 0,
            jnp.concatenate([state_own, state_got]),
            jnp.concatenate([state_got, state_own]),
        )
        out_got = put_back(jnp.zeros_like(grad_mine), partner(out_sent))
        return put_back(grad_mine, grad_got), state_gradient, out_got

    last = len(feed_sum.todo) == 1
    if last:
        feed_sum.prepare()
        feed_sum.start()
    input_gradient, state_gradient, out_base, mixer_sum.rider, *feed_got = beside(
        [mixer_sum],
        lambda *leads: (*exits(*leads[:-1]), swap(leads[-1]), *(feed_sum.got if last else ())),
        grad_mine, grad_got, state_own[:, 0], state_got, out_sent, mixer_sum.rider,
    )
    while len(mixer_sum.todo) > 1:
        beside([mixer_sum], lambda: ())

    mixer_sum.prepare()
    (mixer_send, active_lead, *feed_got) = hold(mixer_sum.sends[0], active_own, *feed_got)
    mixer_sum.sends = [mixer_send]
    mixer_sum.start()
    if last:
        feed_sum.got = list(feed_got)
    else:
        while len(feed_sum.todo) > 1:
            beside([feed_sum], lambda: ())
        feed_sum.prepare()
        feed_sum.start()
    down_sum, up_sum = finish_feed(*feed_sum.last())
    block_output = leave(
        windows, core_at, orders[1], [active_lead, active_other], middle, downs, out_base
    )
    mixer_sum.got = list(hold(*mixer_sum.got, down_sum, block_output)[: len(mixer_sum.got)])
    mixer_grad, read_grad, gain_sum, taps_sum, gain_two_sum, gate_bias_sum, up_bias_sum = finish_mixer(
        *mixer_sum.last(), width, causal_filter.shape[0], units
    )
    return (
        block_output,
        input_gradient,
        state_gradient,
        gain_sum[0],
        taps_sum,
        mixer_grad,
        gate_bias_sum[0],
        read_grad,
        gain_two_sum[0],
        up_sum,
        up_bias_sum[0],
        down_sum,
    )


def solution(mesh):
    return jax.shard_map(
        local,
        mesh=mesh,
        in_specs=(
            P("dp", "tensor", None),
            P("dp", "tensor"),
            P(),
            P(),
            P(None, None, "tensor"),
            P("tensor"),
            P("tensor", None),
            P(),
            P(None, "tensor"),
            P("tensor"),
            P("tensor", None),
            P("dp", "tensor", None),
        ),
        out_specs=(
            P("dp", "tensor", None),
            P("dp", "tensor", None),
            P("dp", "tensor"),
            P(),
            P(),
            P(None, None, "tensor"),
            P("tensor"),
            P("tensor", None),
            P(),
            P(None, "tensor"),
            P("tensor"),
            P("tensor", None),
        ),
        check_vma=False,
    )
```

```python
import functools
import math

import jax
import jax.numpy as jnp
from jax import lax
from jax.experimental import pallas as pl
from jax.experimental.pallas import tpu as pltpu
from jax.sharding import PartitionSpec as P

epsilon = 1e-06
low = jnp.bfloat16
wide = jnp.float32
root = math.sqrt(2.0 / math.pi)
cubic = 0.044715
MIB = 1 << 20


def mm(left, right):
    return lax.dot_general(left, right, (((1,), (0,)), ((), ())), preferred_element_type=wide)


def mm_nt(left, right):
    return lax.dot_general(left, right, (((1,), (1,)), ((), ())), preferred_element_type=wide)


def mm_tn(left, right):
    return lax.dot_general(left, right, (((0,), (0,)), ((), ())), preferred_element_type=wide)


def params(mib, grid):
    return pltpu.CompilerParams(
        vmem_limit_bytes=mib * MIB, dimension_semantics=("arbitrary",) * grid
    )


def cost(macs, moved, curves=0):
    return pl.CostEstimate(flops=2 * macs, bytes_accessed=moved, transcendentals=curves)


def whole(array):
    rank = array.ndim
    return pl.BlockSpec(array.shape, lambda *_: (0,) * rank, pipeline_mode=pl.Buffered(1))


def stream_order(rows, inverse):
    at = lax.broadcasted_iota(jnp.int32, (rows, rows), 1 if inverse else 0)
    source = lax.broadcasted_iota(jnp.int32, (rows, rows), 0 if inverse else 1)
    moved = jnp.bitwise_and(at, 7) * (rows // 8) + lax.shift_right_logical(at, 3)
    return jnp.where(source == moved, 1.0, 0.0).astype(low)


def forward_kernel(
    core, own, got, gain, taps, mixer_own, mixer_other, bias_own, bias_other, start_own, start_other,
    read_own, read_other,
    gain_two, filtered_out, decay_out, differ_out, cand_out, state_out, middle_out, normed_out,
    order, back_order, streams, rim, tail, gates, cands, carry,
):
    half_chunks = pl.num_programs(1) // 2
    step = pl.program_id(1)
    rows = own.shape[1]
    width = own.shape[2]
    count = rows // 8
    tap_count = taps.shape[0]
    edge = 8 * (tap_count - 1)
    channels = read_own.shape[0]
    mine = step // half_chunks == core[0]

    @pl.when((step == 0) & (pl.program_id(0) == 0))
    def _():
        order[...] = stream_order(rows, False)
        back_order[...] = stream_order(rows, True)

    x = mm(order[...], jnp.where(mine, own[0], got[0]))
    streams[...] = x
    scale = lax.rsqrt(jnp.mean(x * x, axis=-1, keepdims=True) + epsilon)
    normed = x * scale * gain[...]

    @pl.when(step == 0)
    def _():
        tail[...] = jnp.zeros_like(tail)
        for at, start in enumerate((start_own, start_other)):
            row = start[pl.ds(core[0] * pl.num_programs(0) + pl.program_id(0), 1), :]
            carry[:, at * channels : (at + 1) * channels] = jnp.broadcast_to(row, (8, channels))

    rim[edge:, :] = normed
    first = lax.broadcasted_iota(jnp.int32, (8, width), 0) == 0
    for at in range(0, edge, 8):
        ends = normed[rows - edge + at : rows - edge + at + 8, :]
        rim[at : at + 8, :] = jnp.where(
            first, pltpu.roll(tail[at : at + 8, :], 1, 0), pltpu.roll(ends, 1, 0)
        )
        tail[at : at + 8, :] = ends
    total = taps[0:1, :] * rim[0:rows, :]
    for tap in range(1, tap_count):
        total = total + taps[tap : tap + 1, :] * rim[8 * tap : 8 * tap + rows, :]
    filtered = total.astype(low)
    filtered_out[...] = filtered
    for at, (weight, bias) in enumerate(((mixer_own, bias_own), (mixer_other, bias_other))):
        lanes = slice(at * channels, (at + 1) * channels)
        gates[:, lanes] = mm(filtered, weight[:, :channels]) + bias[...]
        cands[:, lanes] = mm(filtered, weight[:, channels:])

    group = min(2 * channels, 1024)
    place = lax.broadcasted_iota(jnp.int32, (8, group), 0)
    for lane in range(0, 2 * channels, group):
        lanes = slice(lane, lane + group)

        def open_gates(index, state):
            factor, offset = state
            base = pl.multiple_of(index * 16, 16)
            kept = []
            for sub in (0, 8):
                c = cands[pl.ds(base + sub, 8), lanes]
                decay = jax.nn.sigmoid(-gates[pl.ds(base + sub, 8), lanes])
                soft = jnp.maximum(c, jnp.log(1.0 + jnp.exp(jnp.minimum(c, 60.0))))
                decay_out[pl.ds(base + sub, 8), lanes] = decay
                gates[pl.ds(base + sub, 8), lanes] = soft
                factor = factor * decay
                offset = soft + decay * (offset - soft)
                kept.append(c)
            cand_out[pl.ds(base, 16), lanes] = jnp.concatenate(kept, axis=0).astype(low)
            return factor, offset

        factor, offset = lax.fori_loop(
            0,
            count // 2,
            open_gates,
            (jnp.ones((8, group), wide), jnp.zeros((8, group), wide)),
            unroll=True,
        )
        for hop in (1, 2, 4):
            inside = place >= hop
            offset = factor * jnp.where(inside, pltpu.roll(offset, hop, 0), 0.0) + offset
            factor = factor * jnp.where(inside, pltpu.roll(factor, hop, 0), 1.0)
        entered = carry[:, lanes]
        leaving = factor * entered + offset
        carry[:, lanes] = jnp.broadcast_to(leaving[7:8, :], leaving.shape)
        entered = jnp.where(place >= 1, pltpu.roll(leaving, 1, 0), entered)

        def run_states(index, state):
            base = pl.multiple_of(index * 16, 16)
            held, differ = [], []
            for sub in (0, 8):
                soft = gates[pl.ds(base + sub, 8), lanes]
                differ.append(soft - state)
                state = soft - decay_out[pl.ds(base + sub, 8), lanes] * differ[-1]
                held.append(state)
            differ_out[pl.ds(base, 16), lanes] = jnp.concatenate(differ, axis=0).astype(low)
            state_out[pl.ds(base, 16), lanes] = jnp.concatenate(held, axis=0).astype(low)
            return state

        lax.fori_loop(0, count // 2, run_states, entered, unroll=True)

    mixed = mm(state_out[:, :channels], read_own[...]) + mm(
        state_out[:, channels:], read_other[...]
    )
    middle = streams[...] + mixed
    middle_out[...] = middle
    scale_two = lax.rsqrt(jnp.mean(middle * middle, axis=-1, keepdims=True) + epsilon)
    normed_out[...] = (middle * scale_two * gain_two[...]).astype(low)


def halves_specs(chunk, width, windows, halves):
    return (
        pl.BlockSpec(
            (1, chunk, width), lambda w, t, core: (windows * core[0] + w, t % halves, 0)
        ),
        pl.BlockSpec((1, chunk, width), lambda w, t, core: (w, t % halves, 0)),
    )


def forward(core, inputs, got, gain, taps, mixers, biases, starts, reads, gain_two):
    windows, half, width = got.shape
    channels = reads[0].shape[0]
    chunk = math.gcd(half, 512)
    halves = half // chunk
    steps = 2 * halves
    rows = 2 * half * windows
    row = lambda lanes: pl.BlockSpec((chunk, lanes), lambda w, t, core: (w * steps + t, 0))
    out = lambda lanes, dtype: jax.ShapeDtypeStruct((rows, lanes), dtype)
    return pl.pallas_call(
        forward_kernel,
        grid_spec=pltpu.PrefetchScalarGridSpec(
            num_scalar_prefetch=1,
            grid=(windows, steps),
            in_specs=[
                *halves_specs(chunk, width, windows, halves),
                whole(gain),
                whole(taps),
                whole(mixers[0]),
                whole(mixers[1]),
                whole(biases[0]),
                whole(biases[1]),
                whole(starts[0]),
                whole(starts[1]),
                whole(reads[0]),
                whole(reads[1]),
                whole(gain_two),
            ],
            out_specs=[
                row(width),
                row(2 * channels),
                row(2 * channels),
                row(2 * channels),
                row(2 * channels),
                row(width),
                row(width),
                pl.BlockSpec((chunk, chunk), lambda w, t, core: (0, 0)),
                pl.BlockSpec((chunk, chunk), lambda w, t, core: (0, 0)),
            ],
            scratch_shapes=[
                pltpu.VMEM((chunk, width), wide),
                pltpu.VMEM((chunk + 8 * (taps.shape[0] - 1), width), wide),
                pltpu.VMEM((8 * (taps.shape[0] - 1), width), wide),
                pltpu.VMEM((chunk, 2 * channels), wide),
                pltpu.VMEM((chunk, 2 * channels), wide),
                pltpu.VMEM((8, 2 * channels), wide),
            ],
        ),
        out_shape=[
            out(width, low),
            out(2 * channels, wide),
            out(2 * channels, low),
            out(2 * channels, low),
            out(2 * channels, low),
            out(width, wide),
            out(width, low),
            jax.ShapeDtypeStruct((chunk, chunk), low),
            jax.ShapeDtypeStruct((chunk, chunk), low),
        ],
        compiler_params=params(60, 2),
        cost_estimate=cost(rows * width * channels * 6, rows * channels * 24, rows * channels * 8),
        name="forward_mixer",
    )(core, inputs, got, gain, taps, *mixers, *biases, *starts, *reads, gain_two)


def feed(core, cotangent, got, order, tangent, normed, up, bias, down, dtype):
    windows, half, width = got.shape
    units = up.shape[1]
    rows = normed.shape[0]
    chunk = order.shape[0]
    block = min(units, 512)
    fresh = tangent is None

    def kernel(core, *refs):
        if fresh:
            own, came, order_in, *refs, tangent_in = refs
        else:
            tangent_in, *refs = refs
        normed_in, up_in, bias_in, down_in, active_out, back_out, bias_out, grad_out = refs

        if fresh:

            @pl.when(pl.program_id(0) == 0)
            def _():
                for window in range(windows):
                    for side in range(2):
                        mine = core[0] == side
                        for at in range(0, half, chunk):
                            rows_at = slice(at, at + chunk)
                            to = (2 * window + side) * half + at
                            tangent_in[to : to + chunk, :] = mm(
                                order_in[...],
                                jnp.where(mine, own[window, rows_at, :], came[window, rows_at, :]),
                            ).astype(low)

        total = jnp.zeros((8, block), wide)
        for at in range(0, rows, chunk):
            rows_at = slice(at, at + chunk)
            v = mm(normed_in[rows_at, :], up_in[...]) + bias_in[...]
            back = mm_nt(tangent_in[rows_at, :], down_in[...])
            square = v * v
            s = jax.nn.sigmoid(v * (2.0 * root + (2.0 * root * cubic) * square))
            active = v * s
            slope = s + (active * (1.0 - s)) * (2.0 * root + (6.0 * root * cubic) * square)
            back = back * slope
            for row in range(0, chunk, 8):
                total = total + back[row : row + 8, :]
            active_out[rows_at, :] = active.astype(low)
            back_out[rows_at, :] = back.astype(low)
        bias_out[...] = total
        grad_out[0:width, :] = mm_tn(tangent_in[...], active_out[...]).astype(dtype)
        grad_out[width:, :] = mm_tn(normed_in[...], back_out[...]).astype(dtype)

    lanes = lambda count: pl.BlockSpec((count, block), lambda j, core: (0, j))
    in_specs = [whole(normed), lanes(width), lanes(1), pl.BlockSpec((block, width), lambda j, core: (j, 0))]
    arrays = [normed, up, bias, down]
    out_specs = [lanes(rows), lanes(rows), lanes(8), lanes(2 * width)]
    out_shape = [
        jax.ShapeDtypeStruct((rows, units), low),
        jax.ShapeDtypeStruct((rows, units), low),
        jax.ShapeDtypeStruct((8, units), wide),
        jax.ShapeDtypeStruct((2 * width, units), dtype),
    ]
    if fresh:
        in_specs = [
            pl.BlockSpec((windows, half, width), lambda j, core: (core[0], 0, 0)),
            whole(got),
            whole(order),
        ] + in_specs
        arrays = [cotangent, got, order] + arrays
        out_specs.append(pl.BlockSpec((rows, width), lambda j, core: (0, 0)))
        out_shape.append(jax.ShapeDtypeStruct((rows, width), low))
    else:
        in_specs.insert(0, whole(tangent))
        arrays.insert(0, tangent)
    return pl.pallas_call(
        kernel,
        grid_spec=pltpu.PrefetchScalarGridSpec(
            num_scalar_prefetch=1, grid=(units // block,), in_specs=in_specs, out_specs=out_specs
        ),
        out_shape=out_shape,
        compiler_params=params(60, 1),
        cost_estimate=cost(rows * width * units * 4, rows * units * 4, rows * units),
        name="feed_forward",
    )(core, *arrays)


def norm_kernel(
    tangent, back_own, back_other, middle_in, up_own, up_other, gain_two, middle_out, mixed_out, gain_out
):
    @pl.when(pl.program_id(0) == 0)
    def _():
        gain_out[...] = jnp.zeros_like(gain_out)

    rows = tangent.shape[0]
    part = math.gcd(rows, 256)

    def lead(begin):
        at = slice(begin, begin + part)
        return mm_nt(back_own[at, :], up_own[...]) + mm_nt(back_other[at, :], up_other[...])

    ahead = lead(0)
    for begin in range(0, rows, part):
        at = slice(begin, begin + part)
        back = ahead
        if begin + part < rows:
            ahead = lead(begin + part)
        middle = middle_in[at, :]
        scale = lax.rsqrt(jnp.mean(middle * middle, axis=-1, keepdims=True) + epsilon)
        gain_out[...] += jnp.sum(back * (middle * scale), axis=0, keepdims=True)
        weighted = gain_two[...] * back
        inner = jnp.mean(weighted * middle, axis=-1, keepdims=True)
        back_middle = (
            tangent[at, :].astype(wide) + scale * weighted - middle * (scale * scale * scale * inner)
        )
        middle_out[at, :] = back_middle
        mixed_out[at, :] = back_middle.astype(low)


def norm_back(tangent, backs, middle, ups, gain_two):
    rows, width = tangent.shape
    units = ups[0].shape[1]
    chunk = math.gcd(rows, 512)
    row = lambda lanes: pl.BlockSpec((chunk, lanes), lambda t: (t, 0))
    return pl.pallas_call(
        norm_kernel,
        grid=(rows // chunk,),
        in_specs=[
            row(width),
            row(units),
            row(units),
            row(width),
            whole(ups[0]),
            whole(ups[1]),
            whole(gain_two),
        ],
        out_specs=[row(width), row(width), pl.BlockSpec((1, width), lambda t: (0, 0))],
        out_shape=[
            jax.ShapeDtypeStruct((rows, width), wide),
            jax.ShapeDtypeStruct((rows, width), low),
            jax.ShapeDtypeStruct((1, width), wide),
        ],
        compiler_params=params(60, 1),
        cost_estimate=cost(rows * width * 2 * units, rows * (units * 4 + width * 16)),
        name="norm_back",
    )(tangent, *backs, middle, *ups, gain_two)


def scan_kernel(
    windows, chunk, mixed, filtered, read, decay_in, differ_in, cand_in, state_in,
    gate_out, cand_out, state_out, bias_out, grad_out, states,
):
    rows, width = mixed.shape
    group = read.shape[0]
    count = chunk // 16
    chunks = rows // chunk
    each = chunks // windows
    place = lax.broadcasted_iota(jnp.int32, (8, group), 0)
    states[...] = mm_nt(mixed[...], read[...])
    factors = [jnp.ones((8, group), wide)] * chunks
    offsets = [jnp.zeros((8, group), wide)] * chunks
    for index in range(2 * count - 1, -1, -1):
        for at in range(chunks):
            here = slice(at * chunk + 8 * index, at * chunk + 8 * index + 8)
            decay = decay_in[here, :]
            factors[at] = factors[at] * decay
            offsets[at] = decay * (offsets[at] + states[here, :])
    later = [None] * chunks
    for window in range(windows):
        entered = jnp.zeros((8, group), wide)
        for at in range(window * each + each - 1, window * each - 1, -1):
            factor, offset = factors[at], offsets[at]
            for hop in (1, 2, 4):
                inside = place < 8 - hop
                offset = factor * jnp.where(inside, pltpu.roll(offset, 8 - hop, 0), 0.0) + offset
                factor = factor * jnp.where(inside, pltpu.roll(factor, 8 - hop, 0), 1.0)
            leaving = factor * entered + offset
            later[at] = jnp.where(place < 7, pltpu.roll(leaving, 7, 0), entered)
            entered = jnp.broadcast_to(leaving[0:1, :], leaving.shape)
        state_out[window] = entered[0:1, :]
    bias = [jnp.zeros((8, group), wide)] * chunks
    for index in range(count - 1, -1, -1):
        for at in range(chunks):
            base = at * chunk + 16 * index
            both = slice(base, base + 16)
            differ = differ_in[both, :].astype(wide)
            chosen = jax.nn.sigmoid(cand_in[both, :].astype(wide))
            gate, cand = [None] * 2, [None] * 2
            for half in (1, 0):
                near = slice(8 * half, 8 * half + 8)
                here = slice(base + 8 * half, base + 8 * half + 8)
                decay = decay_in[here, :]
                carried = states[here, :] + later[at]
                later[at] = decay * carried
                opened = carried - later[at]
                gate[half] = decay * opened * differ[near]
                cand[half] = opened * chosen[near]
                bias[at] = bias[at] + gate[half]
            gate_out[both, :] = jnp.concatenate(gate, axis=0).astype(low)
            cand_out[both, :] = jnp.concatenate(cand, axis=0).astype(low)
    bias_out[...] = sum(bias[1:], bias[0])
    grad_out[2 * width :, :] = mm_tn(mixed[...], state_in[...]).astype(grad_out.dtype)
    grad_out[0:width, :] = mm_tn(filtered[...], gate_out[...]).astype(grad_out.dtype)
    grad_out[width : 2 * width, :] = mm_tn(filtered[...], cand_out[...]).astype(grad_out.dtype)


def scan_back(windows, chunk, side, mixed, filtered, read, decay, differ, cand, states, dtype):
    rows, width = mixed.shape
    channels = read.shape[0]
    block = min(channels, 256)
    count = channels // block
    lanes = lambda size: pl.BlockSpec((size, block), lambda j: (0, j))
    half = pl.BlockSpec((rows, block), lambda j: (0, side * count + j))
    out = jax.ShapeDtypeStruct((rows, channels), low)
    return pl.pallas_call(
        functools.partial(scan_kernel, windows, chunk),
        grid=(count,),
        in_specs=[
            whole(mixed),
            whole(filtered),
            pl.BlockSpec((block, width), lambda j: (j, 0)),
            half,
            half,
            half,
            half,
        ],
        out_specs=[
            lanes(rows),
            lanes(rows),
            pl.BlockSpec((windows, 1, block), lambda j: (0, 0, j)),
            lanes(8),
            lanes(3 * width),
        ],
        out_shape=[
            out,
            out,
            jax.ShapeDtypeStruct((windows, 1, channels), wide),
            jax.ShapeDtypeStruct((8, channels), wide),
            jax.ShapeDtypeStruct((3 * width, channels), dtype),
        ],
        scratch_shapes=[pltpu.VMEM((rows, block), wide)],
        compiler_params=params(60, 1),
        cost_estimate=cost(rows * width * 4 * channels, rows * channels * 14, rows * channels),
        name="scan_back",
    )(mixed, filtered, read, decay, differ, cand, states)


def entry_kernel(
    core, own, got, order, back_order, gate_own, cand_own, gate_other, cand_other, middle_in, mixer_own,
    mixer_other, gain, taps, gain_two, bias_own, up_own, bias_other, up_other, mine_out, sent_out, short_out,
    rim, head, sums, packed,
):
    step = pl.program_id(1)
    steps = pl.num_programs(1)
    half_chunks = steps // 2
    position = steps - 1 - step
    rows, width = own.shape[1:]
    tap_count = taps.shape[0]
    edge = 8 * (tap_count - 1)
    channels = gate_own.shape[1]

    @pl.when((step == 0) & (pl.program_id(0) == 0))
    def _():
        sums[...] = jnp.zeros_like(sums)

    @pl.when(step == 0)
    def _():
        head[...] = jnp.zeros_like(head)

    rim[0:rows, :] = (
        mm_nt(gate_own[...], mixer_own[:, :channels])
        + mm_nt(cand_own[...], mixer_own[:, channels:])
        + mm_nt(gate_other[...], mixer_other[:, :channels])
        + mm_nt(cand_other[...], mixer_other[:, channels:])
    )
    last = lax.broadcasted_iota(jnp.int32, (8, width), 0) == 7
    for at in range(0, edge, 8):
        begins = rim[at : at + 8, :]
        rim[rows + at : rows + at + 8, :] = jnp.where(
            last, pltpu.roll(head[at : at + 8, :], 7, 0), pltpu.roll(begins, 7, 0)
        )
        head[at : at + 8, :] = begins
    x = mm(order[...], jnp.where(position // half_chunks == core[0], own[0], got[0]))
    scale = lax.rsqrt(jnp.mean(x * x, axis=-1, keepdims=True) + epsilon)
    unit = x * scale
    back = jnp.zeros((rows, width), wide)
    for tap in range(tap_count):
        begin = 8 * (tap_count - 1 - tap)
        ahead = rim[begin : begin + rows, :]
        back = back + taps[tap : tap + 1, :] * ahead
        sums[tap : tap + 1, :] += jnp.sum(ahead * unit, axis=0, keepdims=True)
    weighted = gain[...] * back
    inner = jnp.mean(weighted * x, axis=-1, keepdims=True)
    gradient = middle_in[...] + scale * weighted - x * (scale * scale * scale * inner)
    gradient = mm(back_order[...], gradient.astype(low)).astype(low)
    give(gradient, position, half_chunks, core, mine_out, sent_out)

    @pl.when((step == steps - 1) & (pl.program_id(0) == pl.num_programs(0) - 1))
    def _():
        totals = sums[0:tap_count, :]
        parts = [jnp.sum(totals * taps[...], axis=0, keepdims=True), totals * gain[...], gain_two[...]]
        for bias in (bias_own, up_own, bias_other, up_other):
            parts.append(jnp.sum(bias[...], axis=0, keepdims=True))
        packed[...] = jnp.zeros_like(packed)
        row = 0
        for part in parts:
            for lane in range(0, part.shape[1], width):
                some = min(width, part.shape[1])
                packed[row : row + part.shape[0], 0:some] = part[:, lane : lane + width]
                row += part.shape[0]
        short_out[...] = packed[...].astype(low)


def give(values, position, half_chunks, core, mine_out, sent_out):
    rows = values.shape[0]
    at = pl.ds(pl.multiple_of(position % half_chunks * rows, rows), rows)
    mine = position // half_chunks == core[0]

    @pl.when(mine)
    def _():
        mine_out[0, at, :] = values

    @pl.when(jnp.logical_not(mine))
    def _():
        sent_out[0, at, :] = values


def side_specs(windows, half, width):
    block = (1, half, width)
    return (
        [
            pl.BlockSpec(block, lambda w, t, core: (windows * core[0] + w, 0, 0)),
            pl.BlockSpec(block, lambda w, t, core: (w, 0, 0)),
        ],
        [
            jax.ShapeDtypeStruct((2 * windows, half, width), low),
            jax.ShapeDtypeStruct((windows, half, width), low),
        ],
    )


def entry(core, inputs, got, orders, projects, back_middle, mixers, gain, taps, *shorts):
    windows, half, width = got.shape
    chunk = math.gcd(half, 512)
    halves = half // chunk
    steps = 2 * halves
    rows = 2 * half * windows
    row = lambda lanes: pl.BlockSpec(
        (chunk, lanes), lambda w, t, core: (w * steps + steps - 1 - t, 0)
    )
    specs, shapes = side_specs(windows, half, width)
    count = taps.shape[0] + 2 + sum(-(-bias.shape[1] // width) for bias in shorts[1:])
    short = (-(-count // 16) * 16, width)
    return pl.pallas_call(
        entry_kernel,
        grid_spec=pltpu.PrefetchScalarGridSpec(
            num_scalar_prefetch=1,
            grid=(windows, steps),
            in_specs=[
                pl.BlockSpec(
                    (1, chunk, width),
                    lambda w, t, core: (windows * core[0] + w, (steps - 1 - t) % halves, 0),
                ),
                pl.BlockSpec((1, chunk, width), lambda w, t, core: (w, (steps - 1 - t) % halves, 0)),
                whole(orders[0]),
                whole(orders[1]),
                *[row(array.shape[1]) for array in projects],
                row(width),
                whole(mixers[0]),
                whole(mixers[1]),
                whole(gain),
                whole(taps),
                *[whole(short) for short in shorts],
            ],
            out_specs=[*specs, pl.BlockSpec(short, lambda w, t, core: (0, 0))],
            scratch_shapes=[
                pltpu.VMEM((chunk + 8 * (taps.shape[0] - 1), width), wide),
                pltpu.VMEM((8 * (taps.shape[0] - 1), width), wide),
                pltpu.VMEM((-(-taps.shape[0] // 8) * 8, width), wide),
                pltpu.VMEM(short, wide),
            ],
        ),
        out_shape=[*shapes, jax.ShapeDtypeStruct(short, low)],
        compiler_params=params(60, 2),
        cost_estimate=cost(
            rows * width * 2 * mixers[0].shape[1], rows * mixers[0].shape[1] * 6
        ),
        name="input_gradient",
    )(core, inputs, got, *orders, *projects, back_middle, *mixers, gain, taps, *shorts)


def leave_kernel(core, back_order, active_own, active_other, middle, down_own, down_other, *refs):
    total = middle[...] + mm(active_own[...], down_own[...]) + mm(active_other[...], down_other[...])
    refs[-1][0] = mm(back_order[...], total.astype(low)).astype(low)


def leave(windows, core, back_order, actives, middle, downs, base=None):
    width = middle.shape[1]
    half = middle.shape[0] // windows // 2
    chunk = back_order.shape[0]
    steps = half // chunk
    side = lambda core: 1 - core[0] if base is None else core[0]
    row = lambda lanes: pl.BlockSpec(
        (chunk, lanes), lambda w, t, core: ((2 * w + side(core)) * steps + t, 0)
    )
    first = lambda core: 0 if base is None else windows * core[0]
    arrays = [core, back_order, *actives, middle, *downs]
    rows = windows * half
    return pl.pallas_call(
        leave_kernel,
        grid_spec=pltpu.PrefetchScalarGridSpec(
            num_scalar_prefetch=1,
            grid=(windows, steps),
            in_specs=[
                whole(back_order),
                row(actives[0].shape[1]),
                row(actives[1].shape[1]),
                row(width),
                whole(downs[0]),
                whole(downs[1]),
                *([] if base is None else [pl.BlockSpec(memory_space=pl.ANY)]),
            ],
            out_specs=pl.BlockSpec(
                (1, chunk, width), lambda w, t, core: (first(core) + w, t, 0)
            ),
        ),
        out_shape=jax.ShapeDtypeStruct((windows if base is None else 2 * windows, half, width), low),
        input_output_aliases={} if base is None else {len(arrays): 0},
        compiler_params=params(60, 2),
        cost_estimate=cost(rows * width * 2 * downs[0].shape[0], rows * downs[0].shape[0] * 6),
        name="block_output",
    )(*arrays, *([] if base is None else [base]))


def in_order(place, parts):
    for at in range(len(parts).bit_length() - 1):
        lead = place[at] == 0
        parts = [
            jnp.where(lead, parts[one], parts[one ^ (1 << at)]) for one in range(len(parts))
        ]
    return parts


def finish_feed_kernel(place, *refs):
    *shares, down_out, up_out = refs
    total = jnp.concatenate(in_order(place, [share[...].astype(wide) for share in shares]))
    width = up_out.shape[0]
    down_out[...] = total[:width].T
    up_out[...] = total[width:]


def finish_feed(place, shares):
    cut, units = shares[0].shape
    width = cut * len(shares) // 2
    block = min(units, 512)
    return pl.pallas_call(
        finish_feed_kernel,
        grid_spec=pltpu.PrefetchScalarGridSpec(
            num_scalar_prefetch=1,
            grid=(units // block,),
            in_specs=[pl.BlockSpec((cut, block), lambda j, place: (0, j))] * len(shares),
            out_specs=[
                pl.BlockSpec((block, width), lambda j, place: (j, 0)),
                pl.BlockSpec((width, block), lambda j, place: (0, j)),
            ],
        ),
        out_shape=[
            jax.ShapeDtypeStruct((units, width), wide),
            jax.ShapeDtypeStruct((width, units), wide),
        ],
        compiler_params=params(60, 1),
        name="finish_feed",
    )(place, *shares)


def finish_mixer_kernel(place, *refs):
    *shares, mixer_out, read_out, gain_out, taps_out, gain_two_out, gate_out, up_out = refs
    width = mixer_out.shape[0]
    cut = 3 * width // len(shares)
    total = jnp.concatenate(in_order(place, [share[:cut, :].astype(wide) for share in shares]))
    short = sum_alike([share[cut:, :] for share in shares])
    lanes = short.shape[1]
    row = 0
    for out in (gain_out, taps_out, gain_two_out, gate_out):
        out[...] = short[row : row + out.shape[0], :]
        row += out.shape[0]
    for lane in range(0, up_out.shape[1], width):
        at = pl.multiple_of(lane + pl.program_id(0) * lanes, lanes)
        up_out[:, pl.ds(at, lanes)] = short[row : row + 1, :]
        row += 1
    mixer_out[:, 0, :] = total[:width]
    mixer_out[:, 1, :] = total[width : 2 * width]
    read_out[...] = total[2 * width :].T


def finish_mixer(place, shares, width, taps, units):
    rows, channels = shares[0].shape
    block = min(channels, 256)
    lanes = lambda count: pl.BlockSpec((count, block), lambda j, place: (0, j))
    return pl.pallas_call(
        finish_mixer_kernel,
        grid_spec=pltpu.PrefetchScalarGridSpec(
            num_scalar_prefetch=1,
            grid=(channels // block,),
            in_specs=[lanes(rows) for _ in shares],
            out_specs=[
                pl.BlockSpec((width, 2, block), lambda j, place: (0, 0, j)),
                pl.BlockSpec((block, width), lambda j, place: (j, 0)),
                lanes(1),
                lanes(taps),
                lanes(1),
                lanes(1),
                pl.BlockSpec((1, units), lambda j, place: (0, 0)),
            ],
        ),
        out_shape=[
            jax.ShapeDtypeStruct((width, 2, channels), wide),
            jax.ShapeDtypeStruct((channels, width), wide),
            *[
                jax.ShapeDtypeStruct(shape, wide)
                for shape in ((1, width), (taps, width), (1, width), (1, channels), (1, units))
            ],
        ],
        compiler_params=params(60, 1),
        name="finish_mixer",
    )(place, *shares)


def partner(array):
    return lax.ppermute(array, "tensor", [(0, 1), (1, 0)])


def hold(*values):
    return lax.optimization_barrier(values)


class DpSum:
    paired = True

    def __init__(self, *terms):
        self.terms = terms
        self.piece = None
        count = lax.axis_size("dp").bit_length() - 1
        first = list(range(count))
        groups = [(tuple(first[at : at + 2]),) * 2 for at in range(0, count, 2)]
        if self.paired and count >= 2:
            groups[:1] = [((0,), (1,)), ((1,), (0,))]
        self.todo = [(False, group) for group in groups] + [(True, group) for group in groups[::-1]]

    def place(self, group):
        index, core = lax.axis_index("dp"), lax.axis_index("tensor")
        return [
            jnp.where(core == 0, (index >> low_bit) & 1, (index >> high_bit) & 1)
            for low_bit, high_bit in zip(*group)
        ]

    def exchange(self, array, group, mask):
        sizes = (lax.axis_size("dp"), lax.axis_size("tensor"))
        flips = [
            sum(1 << bit for at, bit in enumerate(bits) if mask >> at & 1) for bits in group
        ]
        route = [
            (d * sizes[1] + c, (d ^ flips[c]) * sizes[1] + c)
            for d in range(sizes[0])
            for c in range(sizes[1])
        ]
        return lax.ppermute(array, ("dp", "tensor"), route)

    def prepare(self):
        join, group = self.todo[0]
        if join:
            if self.piece is None:
                self.piece = sum(term.astype(wide) for term in self.terms).astype(low)
            self.sends = [self.piece]
            return
        bits = self.place(group)
        self.spot = sum(bit << at for at, bit in enumerate(bits))
        count = 1 << len(bits)
        self.sends = [self.share(self.spot ^ mask, count).astype(low) for mask in range(1, count)]

    def cuts(self, spot, count):
        size = self.terms[0].shape[0] // count
        return [lax.dynamic_slice_in_dim(term, spot * size, size) for term in self.terms]

    def share(self, spot, count):
        return sum(cut.astype(wide) for cut in self.cuts(spot, count))

    def start(self):
        join, group = self.todo[0]
        count = 1 << len(group[0])
        sends = self.sends * (count - 1) if join else self.sends
        self.got = [
            self.exchange(array, group, mask) for array, mask in zip(sends, range(1, count))
        ]

    def finish(self):
        join, group = self.todo.pop(0)
        if not join:
            count = 1 << len(group[0])
            if self.paired and len(self.terms) == 2:
                self.terms = [*self.cuts(self.spot, count), *self.got]
            else:
                self.terms = [self.share(self.spot, count), *self.got]
            return
        parts = [self.piece] + self.got
        for bit in self.place(group):
            parts = [
                jnp.where(
                    bit == 0,
                    jnp.concatenate([parts[at], parts[at + 1]]),
                    jnp.concatenate([parts[at + 1], parts[at]]),
                )
                for at in range(0, len(parts), 2)
            ]
        self.piece = parts[0]


    def last(self):
        _, group = self.todo[0]
        return jnp.stack(self.place(group)).astype(jnp.int32), [self.sends[0], *self.got]


class DpDirect(DpSum):
    paired = False
    rider = None

    def prepare(self):
        super().prepare()
        self.rides = self.rider is not None and (not self.todo[0][0] or len(self.todo) == 1)
        if self.rides:
            self.low_rider = self.rider.astype(low)
            self.sends = [jnp.concatenate([send, self.low_rider]) for send in self.sends]

    def finish(self):
        if self.rides:
            size = self.got[0].shape[0] - self.low_rider.shape[0]
            self.rider = sum_alike([self.low_rider, *(got[size:] for got in self.got)])
            self.got = [got[:size] for got in self.got]
        super().finish()


def sum_alike(parts):
    parts = [part.astype(wide) for part in parts]
    while len(parts) > 1:
        parts = [parts[at] + parts[at + 1] for at in range(0, len(parts), 2)]
    return parts[0]


def beside(chains, work, *leads):
    chains = [chain for chain in chains if chain.todo]
    for chain in chains:
        chain.prepare()
    held = hold(*leads, *(send for chain in chains for send in chain.sends))
    leads, sends = held[: len(leads)], list(held[len(leads) :])
    for chain in chains:
        chain.sends, sends = sends[: len(chain.sends)], sends[len(chain.sends) :]
        chain.start()
    results = work(*leads)
    held = hold(*results, *(got for chain in chains for got in chain.got))
    results, gots = held[: len(results)], list(held[len(results) :])
    for chain in chains:
        chain.got, gots = gots[: len(chain.got)], gots[len(chain.got) :]
        chain.finish()
    return results


def local(
    inputs,
    initial_state,
    first_gain,
    causal_filter,
    mixer_weight,
    gate_bias,
    readout_weight,
    second_gain,
    up_weight,
    up_bias,
    down_weight,
    cotangent,
):
    sides = lax.axis_size("tensor")
    windows = inputs.shape[0] // sides
    half, width = inputs.shape[1:]
    channels = gate_bias.shape[0]
    units = up_bias.shape[0]
    core = lax.axis_index("tensor")
    core_at = core.reshape(1).astype(jnp.int32)

    def other_windows(array):
        return lax.dynamic_slice_in_dim(array, (1 - core) * windows, windows)

    mixer = mixer_weight.reshape(width, 2 * channels)
    mixers = (mixer, partner(mixer))
    got_inputs = partner(other_windows(inputs))
    reads = (readout_weight, partner(readout_weight))
    biases = (gate_bias[None], partner(gate_bias)[None])
    starts = (initial_state, partner(initial_state))
    got_cotangent = partner(other_windows(cotangent))
    ups = (up_weight, partner(up_weight))
    up_biases = (up_bias[None], partner(up_bias)[None])
    downs = (down_weight, partner(down_weight))
    gain, gain_two = first_gain[None], second_gain[None]

    filtered, decay, differ, cand, states, middle, normed, *orders = forward(
        core_at, inputs, got_inputs, gain, causal_filter, mixers, biases, starts, reads, gain_two
    )
    chunk = orders[0].shape[0]
    active_other, back_other, bias_other, feed_other, tangent = feed(
        core_at, cotangent, got_cotangent, orders[0], None, normed, ups[1], up_biases[1], downs[1], low
    )
    tangent, feed_other = hold(tangent, feed_other)
    feed_got = partner(feed_other)
    active_own, back_own, bias_own, feed_own = feed(
        core_at, cotangent, got_cotangent, orders[0], tangent, normed, ups[0], up_biases[0], downs[0], wide
    )
    actives = [active_own, active_other]
    feed_own, feed_got = hold(feed_own, feed_got)
    feed_sum = DpSum(feed_own, feed_got)
    up_bias_own, up_bias_other = bias_own, bias_other

    def scan(side, lead, dtype):
        return scan_back(
            windows, chunk, side, lead, filtered, reads[side], decay, differ, cand, states, dtype
        )

    back_middle, mixed, gain_two_grad = beside(
        [feed_sum],
        lambda lead: norm_back(tangent, [lead, back_other], middle, ups, gain_two),
        back_own,
    )
    gate_other, cand_other, state_other, bias_other, mixer_other = beside(
        [feed_sum], lambda lead: scan(1, lead, low), mixed
    )
    mixed, mixer_other = hold(mixed, mixer_other)
    mixer_got = partner(mixer_other)
    gate_own, cand_own, state_own, bias_own, mixer_own = beside(
        [feed_sum], lambda lead: scan(0, lead, wide), mixed
    )
    mixer_own, mixer_got = hold(mixer_own, mixer_got)
    mixer_sum = DpDirect(mixer_own, mixer_got)
    def put_back(whole_rows, got):
        return lax.dynamic_update_slice_in_dim(whole_rows, got, (1 - core) * windows, 0)

    grad_mine, grad_sent, short = beside(
        [feed_sum, mixer_sum],
        lambda lead: entry(
            core_at, inputs, got_inputs, orders, [lead, cand_own, gate_other, cand_other],
            back_middle, mixers, gain, causal_filter, gain_two_grad, bias_own, up_bias_own,
            bias_other, up_bias_other,
        ),
        gate_own,
    )
    mixer_sum.rider = short

    def leave_first(lead, state_other, grad_sent):
        moved = [partner(array) for array in (state_other, grad_sent)]
        return leave(windows, core_at, orders[1], [lead, active_other], middle, downs), *moved

    out_sent, state_got, grad_got = beside(
        [feed_sum, mixer_sum], leave_first, active_own, state_other[:, 0], grad_sent
    )
    common = causal_filter.shape[0] + 2
    biases_rows = 1 + units // width

    def swap(short):
        own = short[: common + biases_rows]
        other = jnp.concatenate([short[:common], short[common + biases_rows : common + 2 * biases_rows]])
        filler = jnp.zeros((short.shape[0] - common - biases_rows, width), wide)
        return jnp.concatenate([own + partner(other), filler])

    def exits(grad_mine, grad_got, state_own, state_got, out_sent):
        state_gradient = jnp.where(
            core == 0,
            jnp.concatenate([state_own, state_got]),
            jnp.concatenate([state_got, state_own]),
        )
        out_got = put_back(jnp.zeros_like(grad_mine), partner(out_sent))
        return put_back(grad_mine, grad_got), state_gradient, out_got

    last = len(feed_sum.todo) == 1
    if last:
        feed_sum.prepare()
        feed_sum.start()
    input_gradient, state_gradient, out_base, mixer_sum.rider, *feed_got = beside(
        [mixer_sum],
        lambda *leads: (*exits(*leads[:-1]), swap(leads[-1]), *(feed_sum.got if last else ())),
        grad_mine, grad_got, state_own[:, 0], state_got, out_sent, mixer_sum.rider,
    )
    while len(mixer_sum.todo) > 1:
        beside([mixer_sum], lambda: ())

    mixer_sum.prepare()
    (mixer_send, active_lead, *feed_got) = hold(mixer_sum.sends[0], active_own, *feed_got)
    mixer_sum.sends = [mixer_send]
    mixer_sum.start()
    if last:
        feed_sum.got = list(feed_got)
    else:
        while len(feed_sum.todo) > 1:
            beside([feed_sum], lambda: ())
        feed_sum.prepare()
        feed_sum.start()
    down_sum, up_sum = finish_feed(*feed_sum.last())
    block_output = leave(
        windows, core_at, orders[1], [active_lead, active_other], middle, downs, out_base
    )
    mixer_sum.got = list(hold(*mixer_sum.got, down_sum, block_output)[: len(mixer_sum.got)])
    mixer_grad, read_grad, gain_sum, taps_sum, gain_two_sum, gate_bias_sum, up_bias_sum = finish_mixer(
        *mixer_sum.last(), width, causal_filter.shape[0], units
    )
    return (
        block_output,
        input_gradient,
        state_gradient,
        gain_sum[0],
        taps_sum,
        mixer_grad,
        gate_bias_sum[0],
        read_grad,
        gain_two_sum[0],
        up_sum,
        up_bias_sum[0],
        down_sum,
    )


def solution(mesh):
    return jax.shard_map(
        local,
        mesh=mesh,
        in_specs=(
            P("dp", "tensor", None),
            P("dp", "tensor"),
            P(),
            P(),
            P(None, None, "tensor"),
            P("tensor"),
            P("tensor", None),
            P(),
            P(None, "tensor"),
            P("tensor"),
            P("tensor", None),
            P("dp", "tensor", None),
        ),
        out_specs=(
            P("dp", "tensor", None),
            P("dp", "tensor", None),
            P("dp", "tensor"),
            P(),
            P(),
            P(None, None, "tensor"),
            P("tensor"),
            P("tensor", None),
            P(),
            P(None, "tensor"),
            P("tensor"),
            P("tensor", None),
        ),
        check_vma=False,
    )
```
